32 devices in a mesh: gx: 8 (over z, y), gy: 4 (over x, core).
Axes of the slice: x: 2, y: 2, z: 4, core: 2. Of those that a mesh axis runs over, the one named last changes fastest.
Arguments:
- layer_input: bfloat16 [8192, 768], P('gx'), may hold values from -6 to 6
- w_query: bfloat16 [768, 768], P('gx', 'gy'), may hold values from -0.21875 to 0.21875
- w_key: bfloat16 [768, 768], P('gx', 'gy'), may hold values from -0.21875 to 0.21875
- w_value: bfloat16 [768, 768], P('gx', 'gy'), may hold values from -0.21875 to 0.21875
- w_output: bfloat16 [768, 768], P('gx', 'gy'), may hold values from -1.25 to 1.25
- attn_gain: bfloat16 [768], P('gx'), may hold values from 0.5 to 1.5
- moe_gain: bfloat16 [768], P('gx'), may hold values from 0.5 to 1.5
- router: bfloat16 [768, 4], P('gx'), may hold values from -0.15625 to 0.15625
- rel_table: float32 [12, 32], P('gy'), may hold values from -4 to 4
- w_in: bfloat16 [8, 768, 1536], P('gx', None, 'gy'), may hold values from -0.21875 to 0.21875
- w_out: bfloat16 [8, 1536, 768], P('gx', 'gy'), may hold values from -0.4375 to 0.4375
- expert_ids: int32 [8192, 1], P('gx'), may hold values from 0 to 3
- buckets: int32 [1024], replicated, may hold values from 0 to 31
- block_mask: int32 [4, 4], replicated, may hold values from 0 to 1, as said below
- grad_out: bfloat16 [8192, 768], P('gx'), may hold values from -6 to 6
Outputs:
- layer_output: float32 [8192, 768], P('gx')
- grad_input: float32 [8192, 768], P('gx')
- grad_query: float32 [768, 768], P('gx', 'gy')
- grad_key: float32 [768, 768], P('gx', 'gy')
- grad_value: float32 [768, 768], P('gx', 'gy')
- grad_out_proj: float32 [768, 768], P('gx', 'gy')
- grad_attn_gain: float32 [768], P('gx')
- grad_moe_gain: float32 [768], P('gx')
- grad_router: float32 [768, 4], P('gx')
- grad_table: float32 [12, 32], P('gy')
- grad_w_in: float32 [8, 768, 1536], P('gx', None, 'gy')
- grad_w_out: float32 [8, 1536, 768], P('gx', 'gy')
The draws below stay inside these ranges and needn't reach their ends.
Inputs may be any that keep to these rules, and one draw needn't show every extreme that they name: block_mask is 1 on its diagonal and 0 above it. `expert_ids`: every expert is named by some token.
All inputs are finite; a program needn't handle non-finite values.
Results may differ from the reference program's by a relative error of at most 0.02.
Values may be sent and summed in bfloat16 or wider, within the bound.
No kernel may reach another device: no remote copies, remote signals or barrier semaphores. Data moves between devices by JAX's collectives and lax.ppermute only.
A program may use at most 256 MiB of HBM per device.

```python
import jax
import jax.numpy as jnp
from jax import lax

D = 768
HEADS = 12
HEAD_DIM = 64
FF = 3072
NBUCK = 32
BLOCK = 256
SEQ = 1024
EXPERTS = 4
NBLK = 4
CAP = 320
TOKENS = 8192
N_GX = 8


def draw_block_mask(key, part):
    key = jax.random.fold_in(key, 7)
    coins = jax.random.randint(key, (NBLK, NBLK), 0, 2)
    row_ids = jnp.arange(NBLK)[:, None]
    col_ids = jnp.arange(NBLK)[None, :]
    return jnp.where(col_ids == row_ids, 1, jnp.where(col_ids < row_ids, coins, 0)).astype(jnp.int32)


def plant(drawn, key, low, largest):
    extent = drawn.shape
    place = [jax.random.randint(jax.random.fold_in(key, axis), (), 0, extent[axis]) for axis in range(len(extent))]
    drawn = drawn.at[tuple(place)].set(low)
    longest = extent.index(max(extent))
    place[longest] = (place[longest] + 1) % extent[longest]
    return drawn.at[tuple(place)].set(largest)


def block_levels(rng, shape, cuts, low, largest):
    def one(position, shards_of):
        draws = jax.random.uniform(jax.random.fold_in(jax.random.fold_in(rng, 6), position), (shards_of,), jnp.float32, low / len(cuts), largest / len(cuts))
        return jnp.repeat(jnp.exp(draws), shape[position] // shards_of).reshape((-1,) + (1,) * (len(shape) - position - 1))

    level = one(*cuts[0])
    for cut in cuts[1:]:
        level = level * one(*cut)
    return level


def distinct(key, rows, amount, top, lift):
    order = jax.random.permutation(jax.random.fold_in(key, 1), amount)
    pull = order
    for power in range(3):
        pull = pull * pull // amount
    pull = pull * lift // amount
    tickets = jax.random.randint(jax.random.fold_in(key, 2), (rows, amount), 0, 4096) + pull
    fixed_rows = jax.random.permutation(jax.random.fold_in(key, 3), rows)[jnp.arange(amount) % rows]
    tickets = jnp.where(jnp.arange(rows)[:, None] == fixed_rows[None, :], 1 << 14, tickets)
    priority = tickets * amount + jnp.arange(amount)
    return lax.top_k(priority.astype(jnp.int32), top)[1].astype(jnp.int32)


def bell_draw(key, dims, deviation, bound, split=(), kind=jnp.bfloat16):
    level = block_levels(key, dims, split, -0.22, 0.18) if split else 1.0
    values = jax.random.normal(key, dims, jnp.float32) * deviation * level
    return jnp.minimum(jnp.maximum(values, -bound), bound).astype(kind)


def setup_inputs(seed: int = 0) -> dict:
    seeds = jax.random.split(jax.random.key(seed), 16)
    return {
        "layer_input": bell_draw(seeds[0], (TOKENS, D), 1.0, 6.0, ((0, 8),)),
        "w_query": bell_draw(seeds[1], (D, D), D ** -0.5, 0.21875, ((0, 8), (1, 4))),
        "w_key": bell_draw(seeds[2], (D, D), D ** -0.5, 0.21875, ((0, 8), (1, 4))),
        "w_value": bell_draw(seeds[3], (D, D), D ** -0.5, 0.21875, ((0, 8), (1, 4))),
        "w_output": bell_draw(seeds[4], (D, D), (D // 32) ** -0.5, 1.25, ((0, 8), (1, 4))),
        "attn_gain": jnp.clip(1.0 + 0.1 * jax.random.normal(seeds[5], (D,), jnp.float32), 0.5, 1.5).astype(jnp.bfloat16),
        "moe_gain": jnp.clip(1.0 + 0.1 * jax.random.normal(seeds[6], (D,), jnp.float32), 0.5, 1.5).astype(jnp.bfloat16),
        "router": bell_draw(seeds[7], (D, EXPERTS), (2 * D) ** -0.5, 0.15625, ((0, 8),)),
        "rel_table": bell_draw(seeds[8], (HEADS, NBUCK), 1.0, 4.0, ((0, 4),), jnp.float32),
        "w_in": bell_draw(seeds[9], (2 * EXPERTS, D, FF // 2), D ** -0.5, 0.21875, ((0, 8), (2, 4))),
        "w_out": bell_draw(seeds[10], (2 * EXPERTS, FF // 2, D), (max(FF // (EXPERTS * EXPERTS), 1)) ** -0.5, 0.4375, ((0, 8), (1, 4))),
        "expert_ids": distinct(seeds[11], TOKENS, EXPERTS, 1, 2048),
        "buckets": plant(jax.random.randint(seeds[12], (SEQ,), 0, NBUCK), jax.random.fold_in(seeds[12], 1), 0, NBUCK - 1).astype(jnp.int32),
        "block_mask": draw_block_mask(jax.random.fold_in(seeds[15], 71), 0),
        "grad_out": bell_draw(seeds[14], (TOKENS, D), 1.0, 6.0, ((0, 8),)),
    }


@jax.custom_vjp
def low(v):
    return lax.optimization_barrier(v.astype(jnp.bfloat16)).astype(jnp.float32)

@jax.custom_vjp
def low_back(v):
    return v

def low_keep(v):
    return (low(v), None)

def low_pass(kept, grad):
    return (grad,)

def back_keep(v):
    return (v, None)

def back_low(kept, grad):
    return (low(grad),)
low.defvjp(low_keep, low_pass)
low_back.defvjp(back_keep, back_low)
EPS = 1e-06
HIGHEST = lax.Precision.HIGHEST

def product(left, right):
    return jnp.dot(left, right, precision=HIGHEST, preferred_element_type=jnp.float32)

def norm_rows(values, gain):
    return values * lax.rsqrt(lax.optimization_barrier(jnp.mean(values * values, axis=-1, keepdims=True)) + EPS) * gain

def forward(layer_input, w_query, w_key, w_value, w_output, attn_gain, moe_gain, router, rel_table, w_in, w_out, expert_ids, buckets, block_mask):
    positions = jnp.arange(SEQ, dtype=jnp.int32)
    distance = positions[:, None] - positions[None, :]
    block_ids = positions // BLOCK
    pattern = block_mask[block_ids][:, block_ids]
    allowed = (distance >= 0) & (pattern == 1)
    bias_all = rel_table[:, buckets[jnp.clip(distance, 0, SEQ - 1)]]

    def attend(seq_rows):
        hidden_one = low(norm_rows(seq_rows, attn_gain))
        query_heads = low_back(low(product(hidden_one, w_query))).reshape(SEQ, HEADS, HEAD_DIM)
        key_heads = low_back(low(product(hidden_one, w_key))).reshape(SEQ, HEADS, HEAD_DIM)
        value_heads = low_back(low(product(hidden_one, w_value))).reshape(SEQ, HEADS, HEAD_DIM)
        scores = low_back(jnp.einsum('qhd,khd->hqk', query_heads, key_heads, precision=HIGHEST) * 0.125)
        logits = jnp.where(allowed[None], scores + bias_all, -1e+30)
        weights = low(jax.nn.softmax(logits, axis=-1))
        mixed = jnp.einsum('hqk,khd->qhd', weights, value_heads, precision=HIGHEST)
        mixed = low_back(low(mixed)).reshape(SEQ, D)
        return low_back(product(mixed, w_output.T))
    seq_inputs = layer_input.reshape(N_GX, SEQ, D)
    residual = seq_inputs + lax.map(jax.checkpoint(attend), seq_inputs)
    hidden_two = low(norm_rows(residual, moe_gain))
    router_logits = low_back(product(hidden_two.reshape(N_GX * SEQ, D), router)).reshape(N_GX, SEQ, EXPERTS)
    router_prob = jax.nn.softmax(router_logits, axis=-1)
    chosen_ids = expert_ids.reshape(N_GX, SEQ)
    expert_hot = (chosen_ids[:, :, None] == jnp.arange(EXPERTS, dtype=jnp.int32)[None, None, :]).astype(jnp.int32)
    slot_rank = lax.optimization_barrier(jnp.sum((jnp.cumsum(expert_hot, axis=1) - expert_hot) * expert_hot, axis=-1))
    is_kept = slot_rank < CAP
    slot_index = jnp.where(is_kept, chosen_ids * CAP + slot_rank, EXPERTS * CAP).astype(jnp.int32)
    gate_value = lax.optimization_barrier(jnp.sum(router_prob * expert_hot.astype(jnp.float32), axis=-1))
    seq_ids = jnp.arange(N_GX, dtype=jnp.int32)[:, None]
    token_ids = jnp.broadcast_to(positions[None, :], (N_GX, SEQ))
    slot_owner = jnp.full((N_GX, EXPERTS * CAP + 1), SEQ, jnp.int32).at[seq_ids, slot_index].set(token_ids)[:, :EXPERTS * CAP]
    slot_filled = (slot_owner < SEQ).astype(jnp.float32)
    gathered = jnp.take_along_axis(hidden_two, jnp.minimum(slot_owner, SEQ - 1)[:, :, None], axis=1) * slot_filled[:, :, None]
    expert_rows = gathered.reshape(N_GX, EXPERTS, CAP, D).transpose(1, 0, 2, 3).reshape(EXPERTS, N_GX * CAP, D)
    expert_rows = low_back(expert_rows)
    full_in = w_in.reshape(EXPERTS, 2, D, FF // 2).transpose(0, 2, 1, 3).reshape(EXPERTS, D, FF)
    full_out = w_out.reshape(EXPERTS, FF, D)

    def run_expert(pieces):
        rows_here, weight_in, weight_out = pieces
        pre_act = low_back(product(rows_here, weight_in))
        activation = low(jax.nn.gelu(pre_act, approximate=False))
        return low_back(low(product(activation, weight_out)))
    results = lax.map(jax.checkpoint(run_expert), (expert_rows, full_in, full_out))
    results = results.reshape(EXPERTS, N_GX, CAP, D).transpose(1, 0, 2, 3).reshape(N_GX, EXPERTS * CAP, D)
    results = jnp.concatenate([results, jnp.zeros((N_GX, 1, D), jnp.float32)], axis=1)
    combined = jnp.take_along_axis(results, slot_index[:, :, None], axis=1)
    layer_output = residual + gate_value[:, :, None] * combined
    return layer_output.reshape(TOKENS, D)

def reference(layer_input, w_query, w_key, w_value, w_output, attn_gain, moe_gain, router, rel_table, w_in, w_out, expert_ids, buckets, block_mask, grad_out):

    def wrapped(a_input, a_query, a_key, a_value, a_output, a_gain, b_gain, a_router, a_table, a_in, a_out):
        return forward(a_input, a_query, a_key, a_value, a_output, a_gain, b_gain, a_router, a_table, a_in, a_out, expert_ids, buckets, block_mask)
    layer_output, pullback = jax.vjp(wrapped, layer_input.astype(jnp.float32), w_query.astype(jnp.float32), w_key.astype(jnp.float32), w_value.astype(jnp.float32), w_output.astype(jnp.float32), attn_gain.astype(jnp.float32), moe_gain.astype(jnp.float32), router.astype(jnp.float32), rel_table.astype(jnp.float32), w_in.astype(jnp.float32), w_out.astype(jnp.float32))
    grads = pullback(grad_out.astype(jnp.float32))
    return (layer_output, grads[0], grads[1], grads[2], grads[3], grads[4], grads[5], grads[6], grads[7], grads[8], grads[9], grads[10])
```

```python
from functools import partial

import jax
import jax.numpy as jnp
from jax import lax
from jax.experimental import pallas as pl
from jax.experimental.pallas import tpu as pltpu
from jax.sharding import PartitionSpec as P

BLOCK = 256
EPS = 1e-06
LANES = 128
BF = jnp.bfloat16
F32 = jnp.float32
HIGH = lax.Precision.HIGHEST
VMEM_BYTES = 56 * 1024 * 1024


def mm(left, right, precision=None):
    return lax.dot_general(
        left, right, (((1,), (0,)), ((), ())), precision=precision, preferred_element_type=F32
    )


def mm_nt(left, right, precision=None):
    return lax.dot_general(
        left, right, (((1,), (1,)), ((), ())), precision=precision, preferred_element_type=F32
    )


def mm_tn(left, right, precision=None):
    return lax.dot_general(
        left, right, (((0,), (0,)), ((), ())), precision=precision, preferred_element_type=F32
    )


VM = pl.BlockSpec(memory_space=pltpu.VMEM)
SM = pl.BlockSpec(memory_space=pltpu.SMEM)
ANY = pl.BlockSpec(memory_space=pl.ANY)


def call(kernel, name, outs, in_specs, args, scratch=(), flops=0, out_specs=None):
    moved = sum(a.size * a.dtype.itemsize for a in args)
    moved += sum(o.size * o.dtype.itemsize for o in outs)
    return pl.pallas_call(
        kernel,
        name=name,
        out_shape=list(outs),
        in_specs=in_specs,
        out_specs=[VM] * len(outs) if out_specs is None else out_specs,
        scratch_shapes=list(scratch),
        compiler_params=pltpu.CompilerParams(vmem_limit_bytes=VMEM_BYTES),
        cost_estimate=pl.CostEstimate(flops=flops, bytes_accessed=moved, transcendentals=0),
    )(*args)


def struct(shape, dtype):
    return jax.ShapeDtypeStruct(shape, dtype)


def one_hot_rows(pos_row, start, count):
    slots = lax.broadcasted_iota(jnp.int32, (count, pos_row.shape[1]), 0) + start
    return jnp.where(slots == pos_row, 1.0, 0.0).astype(BF)


def one_hot_cols(pos_col, start, count):
    slots = lax.broadcasted_iota(jnp.int32, (pos_col.shape[0], count), 1) + start
    return jnp.where(slots == pos_col, 1.0, 0.0).astype(BF)


def presort_kernel(gy_ref, pos_ref, x_ref, g_ref, info_ref, xs_ref, gs_ref, infos_ref):
    own = xs_ref.shape[0]
    pick = one_hot_rows(pos_ref[...], gy_ref[0] * own, own)
    xs_ref[...] = mm(pick, x_ref[...]).astype(BF)
    gs_ref[...] = mm(pick, g_ref[...]).astype(BF)
    infos_ref[...] = mm(pick, info_ref[...])


def attend_kernel(
    gy_ref,
    mask_ref,
    x_ref,
    w_ref,
    table_ref,
    brev_ref,
    pos_ref,
    h1_ref,
    qkv_ref,
    prob_ref,
    mixed_ref,
    s0_ref,
    s1_ref,
    s2_ref,
    s3_ref,
    toep_ref,
):
    seq = x_ref.shape[0]
    width = mixed_ref.shape[1]
    blocks = seq // BLOCK
    head = 64
    heads = width // head
    gain = jnp.transpose(w_ref[:, :LANES].astype(F32))[0:1]
    for i in range(blocks):
        rows = pl.ds(i * BLOCK, BLOCK)
        x = x_ref[rows, :].astype(F32)
        scale = lax.rsqrt(jnp.mean(x * x, axis=-1, keepdims=True) + EPS)
        h1 = (x * scale * gain).astype(BF)
        h1_ref[rows, :] = h1
        out = mm(h1, w_ref[:, LANES:])
        qkv_ref[rows, :] = jnp.concatenate(
            [out[:, :width].astype(BF) * jnp.asarray(0.125, BF), out[:, width:].astype(BF)], axis=1
        )
    bucket_count = table_ref.shape[1]
    biases = []
    for k in range(blocks):
        labels = lax.broadcasted_iota(jnp.int32, (bucket_count, 2 * BLOCK), 0)
        hot = jnp.where(labels == brev_ref[k : k + 1, :], 1.0, 0.0)
        biases.append(mm(table_ref[...], hot, HIGH))
    for h in range(heads):
        for k in range(blocks):
            line = jnp.broadcast_to(biases[k][h : h + 1, :], (BLOCK, 2 * BLOCK))
            skew = pltpu.roll(line, BLOCK + 1, 1, stride=1, stride_axis=0)[:, :BLOCK]
            if k == 0:
                r = lax.broadcasted_iota(jnp.int32, (BLOCK, BLOCK), 0)
                c = lax.broadcasted_iota(jnp.int32, (BLOCK, BLOCK), 1)
                skew = jnp.where(r >= c, skew, -1e30)
            toep_ref[k] = skew
        at = h * head
        for i in range(blocks):
            q = qkv_ref[pl.ds(i * BLOCK, BLOCK), :][:, at : at + head]
            scores = []
            peak = None
            for j in range(i + 1):
                key = qkv_ref[pl.ds(j * BLOCK, BLOCK), :][:, width + at : width + at + head]
                s = mm_nt(q, key) + toep_ref[i - j]
                if j < i:
                    s = s + jnp.where(mask_ref[i, j] == 1, 0.0, -1e30)
                scores.append(s)
                peak = s if peak is None else jnp.maximum(peak, s)
            peak = jnp.max(peak, axis=-1, keepdims=True)
            total = None
            terms = []
            for s in scores:
                e = jnp.exp(s - peak)
                terms.append(e)
                total = e if total is None else total + e
            inverse = 1.0 / jnp.sum(total, axis=-1, keepdims=True)
            acc = None
            for j in range(i + 1):
                prob = (terms[j] * inverse).astype(BF)
                prob_ref[h * (blocks * (blocks + 1) // 2) + i * (i + 1) // 2 + j] = prob
                value = qkv_ref[pl.ds(j * BLOCK, BLOCK), :][
                    :, 2 * width + at : 2 * width + at + head
                ]
                part = mm(prob, value)
                acc = part if acc is None else acc + part
            mixed_ref[pl.ds(i * BLOCK, BLOCK), at : at + head] = acc.astype(BF)
    own = s0_ref.shape[0]
    mixed = mixed_ref[...]
    for j, ref in enumerate((s0_ref, s1_ref, s2_ref, s3_ref)):
        start = jnp.bitwise_xor(gy_ref[0], j) * own
        ref[...] = mm(one_hot_rows(pos_ref[...], start, own), mixed).astype(BF)


def route_kernel(
    experts,
    m0_ref,
    m1_ref,
    m2_ref,
    m3_ref,
    w0_ref,
    w1_ref,
    w2_ref,
    w3_ref,
    xs_ref,
    gs_ref,
    infos_ref,
    w_ref,
    h2_ref,
    sg_ref,
    res_ref,
    prob_ref,
):
    attn = mm_nt(m0_ref[...], w0_ref[...])
    attn = attn + mm_nt(m1_ref[...], w1_ref[...])
    attn = attn + mm_nt(m2_ref[...], w2_ref[...])
    attn = attn + mm_nt(m3_ref[...], w3_ref[...])
    extras = w_ref[:, :LANES]
    gain = jnp.transpose(extras.astype(F32))[1:2]
    residual = xs_ref[...].astype(F32) + attn
    res_ref[...] = residual
    scale = lax.rsqrt(jnp.mean(residual * residual, axis=-1, keepdims=True) + EPS)
    h2 = (residual * scale * gain).astype(BF)
    logits = mm(h2, extras)
    lane = lax.broadcasted_iota(jnp.int32, logits.shape, 1)
    real = (lane >= 2) & (lane < 2 + experts)
    logits = jnp.where(real, logits, -1e30)
    e = jnp.exp(logits - jnp.max(logits, axis=-1, keepdims=True))
    prob = e / jnp.sum(e, axis=-1, keepdims=True)
    prob_ref[...] = prob
    info = infos_ref[...]
    keep = info[:, 0:1]
    gate = jnp.sum(jnp.where(real, prob * info, 0.0), axis=-1, keepdims=True)
    h2_ref[...] = jnp.where(keep > 0.0, h2.astype(F32), 0.0).astype(BF)
    sg_ref[...] = jnp.where(keep > 0.0, gate * gs_ref[...].astype(F32), 0.0).astype(BF)


def expert_kernel(rows_ref, *refs):
    wins, wouts = refs[:8], refs[8:16]
    er_ref, act_ref, slope_ref = refs[16:19]
    win_buf, wout_buf, sems = refs[19:]
    copies = []
    for j in range(8):
        a = pltpu.make_async_copy(wins[j], win_buf.at[j], sems.at[j])
        b = pltpu.make_async_copy(wouts[j], wout_buf.at[j], sems.at[8 + j])
        a.start()
        b.start()
        copies.append((a, b))
    rows = rows_ref[...]
    acc = None
    for j in range(8):
        copies[j][0].wait()
        pre = mm(rows, win_buf[j])
        cdf = 0.5 * (1.0 + lax.erf(pre * 0.7071067811865476))
        slope = cdf + pre * (0.3989422804014327 * jnp.exp(-0.5 * pre * pre))
        act = (pre * cdf).astype(BF)
        act_ref[j] = act
        slope_ref[j] = slope.astype(BF)
        copies[j][1].wait()
        part = mm(act, wout_buf[j])
        acc = part if acc is None else acc + part
    er_ref[...] = acc.astype(BF)


def expert_back_kernel(sg_ref, slope_ref, *refs):
    wins, wouts = refs[:8], refs[8:16]
    gr_ref, gp_ref = refs[16:18]
    win_buf, wout_buf, sems = refs[18:]
    copies = []
    for j in range(8):
        a = pltpu.make_async_copy(wins[j], win_buf.at[j], sems.at[j])
        b = pltpu.make_async_copy(wouts[j], wout_buf.at[j], sems.at[8 + j])
        b.start()
        a.start()
        copies.append((a, b))
    sg = sg_ref[...]
    acc = None
    for j in range(8):
        copies[j][1].wait()
        grad = mm_nt(sg, wout_buf[j])
        grad = (grad * slope_ref[j].astype(F32)).astype(BF)
        gp_ref[j] = grad
        copies[j][0].wait()
        part = mm_nt(grad, win_buf[j])
        acc = part if acc is None else acc + part
    gr_ref[...] = acc.astype(BF)


def expert_weight_kernel(order, rows_ref, sg_ref, act_ref, gp_ref, *outs):
    rows = rows_ref[...]
    sg = sg_ref[...]
    half = len(order)
    for n, j in enumerate(order):
        outs[n][...] = mm_tn(rows, gp_ref[j]).astype(BF)
        outs[half + n][...] = mm_tn(act_ref[j], sg).astype(BF)


def combine_kernel(
    experts,
    er_ref,
    gr_ref,
    res_ref,
    xs_ref,
    gs_ref,
    infos_ref,
    prob_ref,
    h2_ref,
    w_ref,
    w0_ref,
    w1_ref,
    w2_ref,
    w3_ref,
    g0_ref,
    g1_ref,
    g2_ref,
    g3_ref,
    d1_ref,
    d2_ref,
    small_ref,
):
    extras = w_ref[:, :LANES]
    gain = jnp.transpose(extras.astype(F32))[1:2]
    residual = res_ref[...]
    g = gs_ref[...].astype(F32)
    prob = prob_ref[...]
    lane = lax.broadcasted_iota(jnp.int32, prob.shape, 1)
    real = (lane >= 2) & (lane < 2 + experts)
    hot = jnp.where(real, infos_ref[...], 0.0)
    gate = jnp.sum(prob * hot, axis=-1, keepdims=True)
    result = er_ref[...].astype(F32)
    d1_ref[...] = (residual - xs_ref[...].astype(F32) + gate * result).astype(BF)
    grad_gate = jnp.sum(g * result, axis=-1, keepdims=True)
    grad_logits = (prob * (hot - gate) * grad_gate).astype(BF)
    grad_h2 = mm_nt(grad_logits, extras) + gr_ref[...].astype(F32)
    scale = lax.rsqrt(jnp.mean(residual * residual, axis=-1, keepdims=True) + EPS)
    unit = residual * scale
    scaled = grad_h2 * gain
    centre = jnp.mean(scaled * unit, axis=-1, keepdims=True)
    grad_res = scale * (scaled - unit * centre)
    d2 = grad_res.astype(BF)
    d2_ref[...] = d2
    small = mm_tn(grad_logits, h2_ref[...])
    grad_gain = jnp.sum(grad_h2 * unit, axis=0, keepdims=True)
    row = lax.broadcasted_iota(jnp.int32, small.shape, 0)
    small = jnp.where(row == 1, grad_gain, small)
    small_ref[...] = small[: small_ref.shape[0]]
    grad_attn = (g + d2.astype(F32)).astype(BF)
    for out, w in zip((g0_ref, g1_ref, g2_ref, g3_ref), (w0_ref, w1_ref, w2_ref, w3_ref)):
        out[...] = mm(grad_attn, w[...]).astype(BF)


def unskew_sum(block):
    zeros = jnp.zeros((8, BLOCK), F32)
    acc = None
    for i in range(BLOCK // 8):
        piece = jnp.concatenate([block[8 * i : 8 * i + 8, :], zeros], axis=1)
        shift = BLOCK - 8 - 8 * i
        if shift:
            piece = pltpu.roll(piece, shift, 1)
        acc = piece if acc is None else acc + piece
    left = 7 - lax.broadcasted_iota(jnp.int32, acc.shape, 0)
    for bit in range(3):
        moved = pltpu.roll(acc, 1 << bit, 1)
        acc = jnp.where((left >> bit) & 1 == 1, moved, acc)
    return jnp.sum(acc, axis=0, keepdims=True)


def attend_back_kernel(
    gy_ref,
    g0_ref,
    g1_ref,
    g2_ref,
    g3_ref,
    pos_ref,
    prob_ref,
    qkv_ref,
    h1_ref,
    x_ref,
    w_ref,
    brev_ref,
    dw_ref,
    keep_ref,
    send_ref,
    gain_ref,
    table_ref,
    gm_ref,
    grads_ref,
):
    seq, width = gm_ref.shape
    blocks = seq // BLOCK
    head = 64
    heads = width // head
    own = g0_ref.shape[0]
    gy = gy_ref[0]
    for i in range(blocks):
        rows = pl.ds(i * BLOCK, BLOCK)
        pos = pos_ref[rows, :]
        acc = None
        for j, ref in enumerate((g0_ref, g1_ref, g2_ref, g3_ref)):
            part = mm(one_hot_cols(pos, jnp.bitwise_xor(gy, j) * own, own), ref[...])
            acc = part if acc is None else acc + part
        gm_ref[rows, :] = acc.astype(BF)
    sums = [[None] * heads for _ in range(blocks)]
    for h in range(heads):
        at = h * head
        diagonals = [None] * blocks
        grad_keys = [None] * blocks
        grad_values = [None] * blocks
        for i in range(blocks):
            rows = pl.ds(i * BLOCK, BLOCK)
            q = qkv_ref[rows, :][:, at : at + head]
            gm = gm_ref[rows, :][:, at : at + head]
            centre = None
            kept = []
            for j in range(i + 1):
                value = qkv_ref[pl.ds(j * BLOCK, BLOCK), :][
                    :, 2 * width + at : 2 * width + at + head
                ]
                low = prob_ref[h * (blocks * (blocks + 1) // 2) + i * (i + 1) // 2 + j]
                prob = low.astype(F32)
                grad_prob = mm_nt(gm, value)
                both = prob * grad_prob
                centre = both if centre is None else centre + both
                kept.append((prob, grad_prob))
                part = mm_tn(low, gm)
                grad_values[j] = part if grad_values[j] is None else grad_values[j] + part
            centre = jnp.sum(centre, axis=-1, keepdims=True)
            acc = None
            for j in range(i + 1):
                prob, grad_prob = kept[j]
                score = prob * (grad_prob - centre)
                diagonals[i - j] = score if diagonals[i - j] is None else diagonals[i - j] + score
                score = score.astype(BF)
                key = qkv_ref[pl.ds(j * BLOCK, BLOCK), :][:, width + at : width + at + head]
                part = mm(score, key)
                acc = part if acc is None else acc + part
                part = mm_tn(score, q)
                grad_keys[j] = part if grad_keys[j] is None else grad_keys[j] + part
            grads_ref[rows, at : at + head] = (acc * 0.125).astype(BF)
        for j in range(blocks):
            rows = pl.ds(j * BLOCK, BLOCK)
            grads_ref[rows, width + at : width + at + head] = grad_keys[j].astype(BF)
            grads_ref[rows, 2 * width + at : 2 * width + at + head] = grad_values[j].astype(BF)
        for k in range(blocks):
            sums[k][h] = unskew_sum(diagonals[k])
    bucket_count = table_ref.shape[1]
    table = None
    for k in range(blocks):
        labels = lax.broadcasted_iota(jnp.int32, (bucket_count, 2 * BLOCK), 0)
        hot = jnp.where(labels == brev_ref[k : k + 1, :], 1.0, 0.0)
        lines = jnp.concatenate(sums[k] + [jnp.zeros((8 - heads, 2 * BLOCK), F32)], axis=0)
        part = mm_nt(lines, hot, HIGH)
        table = part if table is None else table + part
    table_ref[...] = table
    gain_total = None
    weights = w_ref[:, LANES:]
    for j in range(4):
        rows = pl.ds(pl.multiple_of(jnp.bitwise_xor(gy, j) * BLOCK, BLOCK), BLOCK)
        part = mm_nt(grads_ref[rows, :], weights)
        x = x_ref[rows, :].astype(F32)
        unit = x * lax.rsqrt(jnp.mean(x * x, axis=-1, keepdims=True) + EPS)
        line = jnp.sum(part * unit, axis=0, keepdims=True)
        gain_total = line if gain_total is None else gain_total + line
        target = send_ref if j % 2 else keep_ref
        target[j // 2] = part.astype(BF)
    gain_ref[...] = jnp.broadcast_to(gain_total, gain_ref.shape)
    dw_ref[...] = mm_tn(h1_ref[...], grads_ref[...]).astype(BF)


def unsort_kernel(gy_ref, pos_ref, x_ref, g_ref, mixed_ref, *refs):
    d1, d2 = refs[:4], refs[4:8]
    out_ref, back_ref, dwo_ref, ga_ref = refs[8:]
    own = d1[0].shape[0]
    gy = gy_ref[0]
    blocks = x_ref.shape[0] // BLOCK
    for i in range(blocks):
        rows = pl.ds(i * BLOCK, BLOCK)
        pos = pos_ref[rows, :]
        first, second = None, None
        for j in range(4):
            hot = one_hot_cols(pos, jnp.bitwise_xor(gy, j) * own, own)
            a = mm(hot, d1[j][...])
            b = mm(hot, d2[j][...])
            first = a if first is None else first + a
            second = b if second is None else second + b
        out_ref[rows, :] = x_ref[rows, :].astype(F32) + first
        grad = g_ref[rows, :].astype(F32) + second
        back_ref[rows, :] = grad
        ga_ref[rows, :] = grad.astype(BF)
    dwo_ref[...] = mm_tn(ga_ref[...], mixed_ref[...]).astype(BF)


def finish_kernel(gy_ref, own_ref, other_ref, x_ref, w_ref, back_ref, out_ref):
    gain = jnp.transpose(w_ref[:, :LANES].astype(F32))[0:1]
    gy = gy_ref[0]
    for j in range(4):
        rows = pl.ds(pl.multiple_of(jnp.bitwise_xor(gy, j) * BLOCK, BLOCK), BLOCK)
        source = other_ref if j % 2 else own_ref
        x = x_ref[rows, :].astype(F32)
        scale = lax.rsqrt(jnp.mean(x * x, axis=-1, keepdims=True) + EPS)
        unit = x * scale
        scaled = source[j // 2].astype(F32) * gain
        centre = jnp.mean(scaled * unit, axis=-1, keepdims=True)
        out_ref[rows, :] = back_ref[rows, :] + scale * (scaled - unit * centre)


def swap(x, axis, bit):
    size = lax.axis_size(axis)
    return lax.ppermute(x, axis, [(i, i ^ bit) for i in range(size)])


def gather_rows(x):
    size = lax.axis_size("gx")
    copies = jnp.broadcast_to(x[None], (size,) + x.shape).reshape(size * x.shape[0], x.shape[1])
    return lax.all_to_all(copies, "gx", split_axis=0, concat_axis=0, tiled=True)


def spread(x):
    return lax.all_to_all(x, "gx", split_axis=0, concat_axis=0, tiled=True)


def sum_rows(x):
    size = lax.axis_size("gx")
    arrived = spread(x).reshape(size, x.shape[0] // size, x.shape[1])
    return arrived.astype(F32).sum(axis=0)


def add(a, b):
    return a.astype(F32) + b.astype(F32)


def place_tokens(expert_ids, experts, capacity, piece):
    ids = expert_ids[:, 0]
    hot = (ids[:, None] == jnp.arange(experts, dtype=jnp.int32)[None, :]).astype(jnp.int32)
    rank = jnp.sum((jnp.cumsum(hot, axis=0) - hot) * hot, axis=1)
    kept = rank < capacity
    filled = jnp.minimum(jnp.sum(hot, axis=0), capacity)
    empty = capacity - filled
    ends = jnp.cumsum(empty)
    begins = ends - empty
    lost = jnp.where(kept, 0, 1)
    order = jnp.cumsum(lost) - lost
    inside = (order[:, None] >= begins[None, :]) & (order[:, None] < ends[None, :])
    spare_expert = jnp.sum(jnp.where(inside, jnp.arange(experts)[None, :], 0), axis=1)
    spare_rank = jnp.sum(jnp.where(inside, order[:, None] - begins + filled, 0), axis=1)
    expert = jnp.where(kept, ids, spare_expert)
    rank = jnp.where(kept, rank, spare_rank)
    group = 2 * piece
    position = (rank // group) * (experts * group) + expert * group + rank % group
    info = jnp.concatenate(
        [
            jnp.where(kept, 1.0, 0.0)[:, None],
            jnp.zeros((ids.shape[0], 1)),
            hot.astype(F32),
            jnp.zeros((ids.shape[0], LANES - 2 - experts)),
        ],
        axis=1,
    )
    return position.astype(jnp.int32), info.astype(BF)


def on_device(
    layer_input,
    w_query,
    w_key,
    w_value,
    w_output,
    attn_gain,
    moe_gain,
    router,
    rel_table,
    w_in,
    w_out,
    expert_ids,
    buckets,
    block_mask,
    grad_out,
):
    n_gx = lax.axis_size("gx")
    n_gy = lax.axis_size("gy")
    seq, model = layer_input.shape
    heads, bucket_count = rel_table.shape
    width = w_query.shape[1]
    shard = w_query.shape[0]
    experts = router.shape[1]
    hidden = w_in.shape[2]
    capacity = 5 * seq // (4 * experts)
    piece = capacity // (2 * n_gy)
    own = experts * 2 * piece
    blocks = seq // BLOCK
    pairs = blocks * (blocks + 1) // 2
    gy = lax.axis_index("gy").astype(jnp.int32).reshape(1)

    extras = jnp.concatenate(
        [
            attn_gain[:, None],
            moe_gain[:, None],
            router,
            jnp.zeros((shard, LANES - 2 - experts), BF),
        ],
        axis=1,
    )
    packet = jnp.concatenate([extras, w_query, w_key, w_value], axis=1)
    weights = gather_rows(packet)
    out_own = gather_rows(w_output)
    out_core = swap(out_own, "gy", 1)
    out_x = swap(out_own, "gy", 2)
    out_far = swap(out_x, "gy", 1)
    out_pieces = [out_own, out_core, out_x, out_far]

    win, wout = w_in[0], w_out[0]
    win_x, wout_x = swap(win, "gy", 2), swap(wout, "gy", 2)
    win_y, wout_y = swap(win, "gx", 1), swap(wout, "gx", 1)
    win_d, wout_d = swap(win_y, "gy", 2), swap(wout_x, "gx", 1)
    wins = [win, win_x, win_y, win_d]
    wouts = [wout, wout_x, wout_y, wout_d]
    wins = wins + [swap(a, "gy", 1) for a in wins]
    wouts = wouts + [swap(a, "gy", 1) for a in wouts]

    position, info = place_tokens(expert_ids, experts, capacity, piece)
    pos_row = position[None, :]
    pos_col = position[:, None]
    xs, gs, infos = call(
        presort_kernel,
        "presort",
        [struct((own, model), BF), struct((own, model), BF), struct((own, LANES), F32)],
        [SM, VM, VM, VM, VM],
        (gy, pos_row, layer_input, grad_out, info),
        flops=2 * own * seq * (2 * model + LANES),
    )

    backwards = jnp.concatenate([buckets[::-1], jnp.full((BLOCK,), -1, jnp.int32)])
    brev = jnp.stack(
        [
            backwards[seq - BLOCK * (k + 1) : seq - BLOCK * (k + 1) + 2 * BLOCK]
            for k in range(blocks)
        ]
    )
    table_pad = jnp.concatenate([rel_table, jnp.zeros((8 - heads, bucket_count), F32)], axis=0)
    h1, qkv, prob, mixed, *sorted_parts = call(
        attend_kernel,
        "attend",
        [
            struct((seq, model), BF),
            struct((seq, 3 * width), BF),
            struct((heads * pairs, BLOCK, BLOCK), BF),
            struct((seq, width), BF),
        ]
        + [struct((own, width), BF)] * 4,
        [SM, SM, VM, VM, VM, VM, VM],
        (gy, block_mask, layer_input, weights, table_pad, brev, pos_row),
        scratch=[pltpu.VMEM((blocks, BLOCK, BLOCK), F32)],
        flops=10 * 10**9,
    )
    mixed_pieces = [sorted_parts[0]] + [swap(sorted_parts[j], "gy", j) for j in (1, 2, 3)]
    h2, sg, residual, router_prob = call(
        partial(route_kernel, experts),
        "route",
        [
            struct((own, model), BF),
            struct((own, model), BF),
            struct((own, model), F32),
            struct((own, LANES), F32),
        ],
        [VM] * 12,
        (*mixed_pieces, *out_pieces, xs, gs, infos, weights),
        flops=2 * 10**9,
    )
    rows_in = spread(h2)
    grads_in = spread(sg)
    expert_scratch = [
        pltpu.VMEM((8, model, hidden), BF),
        pltpu.VMEM((8, hidden, model), BF),
        pltpu.SemaphoreType.DMA((16,)),
    ]
    result, act, slope = call(
        expert_kernel,
        "expert",
        [
            struct((own, model), BF),
            struct((8, own, hidden), BF),
            struct((8, own, hidden), BF),
        ],
        [VM] + [ANY] * 16,
        (rows_in, *wins, *wouts),
        scratch=expert_scratch,
        flops=6 * 10**9,
    )
    result_back = spread(result)
    grad_rows, grad_pre = call(
        expert_back_kernel,
        "expert_back",
        [struct((own, model), BF), struct((8, own, hidden), BF)],
        [VM, VM] + [ANY] * 16,
        (grads_in, slope, *wins, *wouts),
        scratch=expert_scratch,
        flops=4 * 10**9,
    )
    rows_back = spread(grad_rows)
    weight_shapes = [struct((model, hidden), BF)] * 4 + [struct((hidden, model), BF)] * 4
    sent = call(
        partial(expert_weight_kernel, (4, 5, 6, 7)),
        "expert_weight_a",
        weight_shapes,
        [VM] * 4,
        (rows_in, grads_in, act, grad_pre),
        flops=3 * 10**9,
    )
    held = call(
        partial(expert_weight_kernel, (0, 1, 2, 3)),
        "expert_weight_b",
        weight_shapes,
        [VM] * 4,
        (rows_in, grads_in, act, grad_pre),
        flops=3 * 10**9,
    )
    arrived = [swap(a, "gy", 1) for a in sent]
    chip = [add(a, b) for a, b in zip(held, arrived)]
    win_far = swap(chip[3].astype(BF), "gy", 2)
    wout_far = swap(chip[7].astype(BF), "gx", 1)
    win_by_x = swap(chip[1].astype(BF), "gy", 2)
    wout_by_y = swap(chip[6].astype(BF), "gx", 1)
    win_by_y = swap(add(chip[2], win_far).astype(BF), "gx", 1)
    wout_by_x = swap(add(chip[5], wout_far).astype(BF), "gy", 2)
    grad_w_in = add(add(chip[0], win_by_x), win_by_y)
    grad_w_out = add(add(chip[4], wout_by_y), wout_by_x)

    small_rows = -(-(2 + experts) // 8) * 8
    *mixed_grads, d1, d2, small = call(
        partial(combine_kernel, experts),
        "combine",
        [struct((own, width), BF)] * 4
        + [struct((own, model), BF)] * 2
        + [struct((small_rows, model), F32)],
        [VM] * 13,
        (result_back, rows_back, residual, xs, gs, infos, router_prob, h2, weights, *out_pieces),
        flops=2 * 10**9,
    )
    grads_mixed = [mixed_grads[0]] + [swap(mixed_grads[j], "gy", j) for j in (1, 2, 3)]
    dw, keep, send, gain_one, table = call(
        attend_back_kernel,
        "attend_back",
        [
            struct((model, 3 * width), BF),
            struct((2, BLOCK, model), BF),
            struct((2, BLOCK, model), BF),
            struct((8, model), F32),
            struct((8, bucket_count), F32),
        ],
        [SM] + [VM] * 11,
        (gy, *grads_mixed, pos_col, prob, qkv, h1, layer_input, weights, brev),
        scratch=[pltpu.VMEM((seq, width), BF), pltpu.VMEM((seq, 3 * width), BF)],
        flops=16 * 10**9,
    )
    half = add(keep, swap(send, "gy", 1)).astype(BF)
    total = add(half, swap(half, "gy", 2)[::-1]).astype(BF)
    other = swap(total, "gy", 1)

    d1_x, d2_x = swap(d1, "gy", 2), swap(d2, "gy", 2)
    d1s = [d1, swap(d1, "gy", 1), d1_x, swap(d1_x, "gy", 1)]
    d2s = [d2, swap(d2, "gy", 1), d2_x, swap(d2_x, "gy", 1)]
    layer_output, back, dwo = call(
        unsort_kernel,
        "unsort",
        [struct((seq, model), F32), struct((seq, model), F32), struct((model, width), BF)],
        [SM] + [VM] * 12,
        (gy, pos_col, layer_input, grad_out, mixed, *d1s, *d2s),
        scratch=[pltpu.VMEM((seq, model), BF)],
        flops=5 * 10**9,
    )
    (grad_input,) = call(
        finish_kernel,
        "finish",
        [struct((seq, model), F32)],
        [SM] + [VM] * 5,
        (gy, total, other, layer_input, weights, back),
        flops=10**7,
    )
    grad_qkv = sum_rows(dw)
    grad_out_proj = sum_rows(dwo)

    row = lax.broadcasted_iota(jnp.int32, small.shape, 0)
    small = jnp.where(row == 0, gain_one[0:1], small)
    small = small + swap(small, "gy", 1)
    small = small + swap(small, "gy", 2)
    tiles = small.reshape(small_rows, n_gx, shard).transpose(1, 0, 2)
    small = lax.all_to_all(tiles, "gx", split_axis=0, concat_axis=0, tiled=True).sum(axis=0)
    tables = jnp.broadcast_to(table[None], (n_gx,) + table.shape)
    tables = lax.all_to_all(tables, "gx", split_axis=0, concat_axis=0, tiled=True)
    grad_table = tables.sum(axis=0)[:heads]
    return (
        layer_output,
        grad_input,
        grad_qkv[:, :width],
        grad_qkv[:, width : 2 * width],
        grad_qkv[:, 2 * width :],
        grad_out_proj,
        small[0],
        small[1],
        small[2 : 2 + experts].T,
        grad_table,
        grad_w_in[None],
        grad_w_out[None],
    )


def solution(mesh):
    return jax.shard_map(
        on_device,
        mesh=mesh,
        in_specs=(
            P("gx", None),
            P("gx", "gy"),
            P("gx", "gy"),
            P("gx", "gy"),
            P("gx", "gy"),
            P("gx"),
            P("gx"),
            P("gx", None),
            P("gy", None),
            P("gx", None, "gy"),
            P("gx", "gy", None),
            P("gx", None),
            P(),
            P(),
            P("gx", None),
        ),
        out_specs=(
            P("gx", None),
            P("gx", None),
            P("gx", "gy"),
            P("gx", "gy"),
            P("gx", "gy"),
            P("gx", "gy"),
            P("gx"),
            P("gx"),
            P("gx", None),
            P("gy", None),
            P("gx", None, "gy"),
            P("gx", "gy", None),
        ),
        check_vma=False,
    )
```

```python
from functools import partial

import jax
import jax.numpy as jnp
from jax import lax
from jax.experimental import pallas as pl
from jax.experimental.pallas import tpu as pltpu
from jax.sharding import PartitionSpec as P

BLOCK = 256
EPS = 1e-06
LANES = 128
BF = jnp.bfloat16
F32 = jnp.float32
HIGH = lax.Precision.HIGHEST
VMEM_BYTES = 56 * 1024 * 1024
PEAK = 1.15e9
RING = (0, 2, 4, 6, 7, 5, 3, 1)
RING_STEPS = (0, -1, 1, -2, 2, -3, 3, -4)


def mm(left, right, precision=None):
    return lax.dot_general(
        left, right, (((1,), (0,)), ((), ())), precision=precision, preferred_element_type=F32
    )


def mm_nt(left, right, precision=None):
    return lax.dot_general(
        left, right, (((1,), (1,)), ((), ())), precision=precision, preferred_element_type=F32
    )


def mm_tn(left, right, precision=None):
    return lax.dot_general(
        left, right, (((0,), (0,)), ((), ())), precision=precision, preferred_element_type=F32
    )


VM = pl.BlockSpec(memory_space=pltpu.VMEM)
SM = pl.BlockSpec(memory_space=pltpu.SMEM)
ANY = pl.BlockSpec(memory_space=pl.ANY)


def call(kernel, name, outs, in_specs, args, scratch=(), cost=1):
    return pl.pallas_call(
        kernel,
        name=name,
        out_shape=list(outs),
        in_specs=in_specs,
        out_specs=[VM] * len(outs),
        scratch_shapes=list(scratch),
        compiler_params=pltpu.CompilerParams(vmem_limit_bytes=VMEM_BYTES),
        cost_estimate=pl.CostEstimate(
            flops=int(cost * PEAK), bytes_accessed=1, transcendentals=0
        ),
    )(*args)


def struct(shape, dtype):
    return jax.ShapeDtypeStruct(shape, dtype)


def one_hot_rows(pos_row, start, count):
    slots = lax.broadcasted_iota(jnp.int32, (count, pos_row.shape[1]), 0) + start
    return jnp.where(slots == pos_row, 1.0, 0.0).astype(BF)


def one_hot_cols(pos_col, start, count):
    slots = lax.broadcasted_iota(jnp.int32, (pos_col.shape[0], count), 1) + start
    return jnp.where(slots == pos_col, 1.0, 0.0).astype(BF)


def pack_kernel(q_ref, k_ref, v_ref, o_ref, attn_ref, moe_ref, router_ref, qkv_ref, extras_ref):
    qkv_ref[...] = jnp.concatenate([q_ref[...], k_ref[...], v_ref[...]], axis=1)
    rows, experts = router_ref.shape
    blank = jnp.zeros((1, LANES - rows), F32)
    row = lax.broadcasted_iota(jnp.int32, (LANES, LANES), 0)
    first = jnp.concatenate([attn_ref[...].astype(F32), blank], axis=1)
    second = jnp.concatenate([moe_ref[...].astype(F32), blank], axis=1)
    gains = jnp.where(row == 0, first, jnp.where(row == 1, second, 0.0))
    gains = jnp.transpose(gains)[:rows]
    route = jnp.concatenate(
        [
            jnp.zeros((rows, 2), F32),
            router_ref[...].astype(F32),
            jnp.zeros((rows, LANES - 2 - experts), F32),
        ],
        axis=1,
    )
    extras_ref[...] = jnp.concatenate([(gains + route).astype(BF), o_ref[...]], axis=1)


def lane_prefix(values):
    row = lax.broadcasted_iota(jnp.int32, (LANES, LANES), 0)
    column = lax.broadcasted_iota(jnp.int32, (LANES, LANES), 1)
    sooner = jnp.where(row < column, 1.0, 0.0).astype(BF)
    carry = jnp.zeros((values.shape[0], 1), F32)
    out = []
    for start in range(0, values.shape[1], LANES):
        part = values[:, start : start + LANES]
        out.append(mm(part.astype(BF), sooner) + carry)
        carry = carry + jnp.sum(part, axis=1, keepdims=True)
    return jnp.concatenate(out, axis=1), carry


def place_kernel(experts, capacity, group, gx_ref, ids_ref, row_ref, col_ref, info_ref):
    seq = ids_ref.shape[1]
    ids = ids_ref[...]
    deep = -(-experts // 8) * 8
    label = lax.broadcasted_iota(jnp.int32, (deep, seq), 0)
    hot = jnp.where(label == ids, 1.0, 0.0)
    before, total = lane_prefix(hot)
    rank = jnp.sum(before * hot, axis=0, keepdims=True)
    kept = rank < capacity
    filled = jnp.minimum(total, 1.0 * capacity)
    empty = jnp.where(label[:, 0:1] < experts, capacity - filled, 0.0)
    row = lax.broadcasted_iota(jnp.int32, (deep, deep), 0)
    column = lax.broadcasted_iota(jnp.int32, (deep, deep), 1)
    sooner = jnp.where(column < row, 1.0, 0.0)
    begins = mm(sooner, jnp.broadcast_to(empty, (deep, LANES)), HIGH)[:, 0:1]
    lost = jnp.broadcast_to(jnp.where(kept, 0.0, 1.0), (8, seq))
    order = lane_prefix(lost)[0][0:1]
    inside = (order >= begins) & (order < begins + empty)
    spare_expert = jnp.sum(jnp.where(inside, label.astype(F32), 0.0), axis=0, keepdims=True)
    spare_rank = jnp.sum(jnp.where(inside, order - begins + filled, 0.0), axis=0, keepdims=True)
    expert = jnp.where(kept, ids.astype(F32), spare_expert).astype(jnp.int32)
    rank = jnp.where(kept, rank, spare_rank)
    block = jnp.floor((rank + 0.5) * (1.0 / group))
    near = jnp.bitwise_xor(expert, gx_ref[0] // 2).astype(F32)
    position = block * (experts * group) + near * group + rank - block * group
    row_ref[...] = position.astype(jnp.int32)
    tall = jnp.transpose(jnp.broadcast_to(position, (LANES, seq)))
    col_ref[...] = tall[:, 0:1].astype(jnp.int32)
    line = lax.broadcasted_iota(jnp.int32, (LANES, seq), 0)
    info = jnp.where(line == 0, jnp.where(kept, 1.0, 0.0), jnp.where(line - 2 == ids, 1.0, 0.0))
    info_ref[...] = info.astype(BF)


def presort_kernel(gy_ref, pos_ref, x_ref, g_ref, info_ref, xs_ref, gs_ref, infos_ref):
    own = xs_ref.shape[0]
    pick = one_hot_rows(pos_ref[...], gy_ref[0] * own, own)
    xs_ref[...] = mm(pick, x_ref[...]).astype(BF)
    gs_ref[...] = mm(pick, g_ref[...]).astype(BF)
    infos_ref[...] = mm_nt(pick, info_ref[...])


def ring_source(gx, step):
    spot = jnp.where(gx % 2 == 0, gx // 2, 7 - gx // 2)
    spot = jnp.bitwise_and(spot + step, 7)
    return jnp.where(spot < 4, 2 * spot, 2 * (7 - spot) + 1)


def assemble(pieces, gx_ref, target, sems):
    copies = []
    rows = pieces[0].shape[0]
    for n, piece in enumerate(pieces):
        place = target
        if len(pieces) > 1:
            at = pl.multiple_of(ring_source(gx_ref[0], RING_STEPS[n]) * rows, 32)
            place = target.at[pl.ds(at, rows), :]
        copy = pltpu.make_async_copy(piece, place, sems.at[n])
        copy.start()
        copies.append(copy)
    return copies


def unpack_kernel(count, *refs):
    gx_ref, pieces = refs[0], refs[1 : 1 + count]
    extras_ref, out_ref, buf, sems = refs[1 + count :]
    for copy in assemble(pieces, gx_ref, buf, sems):
        copy.wait()
    extras_ref[...] = buf[:, :LANES]
    out_ref[...] = buf[:, LANES:]


def attend_kernel(count, *refs):
    gy_ref, gx_ref, mask_ref, x_ref, extras_ref, table_ref, brev_ref, pos_ref = refs[:8]
    pieces = refs[8 : 8 + count]
    h1_ref, qkv_ref, prob_ref, mixed_ref, s0_ref, s1_ref, s2_ref, s3_ref = refs[
        8 + count : 16 + count
    ]
    w_ref, toep_ref, sems = refs[16 + count :]
    copies = assemble(pieces, gx_ref, w_ref, sems)
    seq = x_ref.shape[0]
    width = mixed_ref.shape[1]
    blocks = seq // BLOCK
    head = 64
    heads = width // head
    gain = jnp.transpose(extras_ref[...].astype(F32))[0:1]
    for copy in copies:
        copy.wait()
    for i in range(blocks):
        rows = pl.ds(i * BLOCK, BLOCK)
        x = x_ref[rows, :].astype(F32)
        scale = lax.rsqrt(jnp.mean(x * x, axis=-1, keepdims=True) + EPS)
        h1 = (x * scale * gain).astype(BF)
        h1_ref[rows, :] = h1
        out = mm(h1, w_ref[...])
        qkv_ref[rows, :] = jnp.concatenate(
            [out[:, :width].astype(BF) * jnp.asarray(0.125, BF), out[:, width:].astype(BF)], axis=1
        )
    bucket_count = table_ref.shape[1]
    biases = []
    for k in range(blocks):
        labels = lax.broadcasted_iota(jnp.int32, (bucket_count, 2 * BLOCK), 0)
        hot = jnp.where(labels == brev_ref[k : k + 1, :], 1.0, 0.0)
        biases.append(mm(table_ref[...], hot, HIGH))
    for h in range(heads):
        for k in range(blocks):
            line = jnp.broadcast_to(biases[k][h : h + 1, :], (BLOCK, 2 * BLOCK))
            skew = pltpu.roll(line, BLOCK + 1, 1, stride=1, stride_axis=0)[:, :BLOCK]
            if k == 0:
                r = lax.broadcasted_iota(jnp.int32, (BLOCK, BLOCK), 0)
                c = lax.broadcasted_iota(jnp.int32, (BLOCK, BLOCK), 1)
                skew = jnp.where(r >= c, skew, -1e30)
            toep_ref[k] = skew
        at = h * head
        for i in range(blocks):
            q = qkv_ref[pl.ds(i * BLOCK, BLOCK), :][:, at : at + head]
            scores = []
            peak = None
            for j in range(i + 1):
                key = qkv_ref[pl.ds(j * BLOCK, BLOCK), :][:, width + at : width + at + head]
                s = mm_nt(q, key) + toep_ref[i - j]
                if j < i:
                    s = s + jnp.where(mask_ref[i, j] == 1, 0.0, -1e30)
                scores.append(s)
                peak = s if peak is None else jnp.maximum(peak, s)
            peak = jnp.max(peak, axis=-1, keepdims=True)
            total = None
            terms = []
            for s in scores:
                e = jnp.exp(s - peak)
                terms.append(e)
                total = e if total is None else total + e
            inverse = 1.0 / jnp.sum(total, axis=-1, keepdims=True)
            acc = None
            for j in range(i + 1):
                prob = (terms[j] * inverse).astype(BF)
                prob_ref[h * (blocks * (blocks + 1) // 2) + i * (i + 1) // 2 + j] = prob
                value = qkv_ref[pl.ds(j * BLOCK, BLOCK), :][
                    :, 2 * width + at : 2 * width + at + head
                ]
                part = mm(prob, value)
                acc = part if acc is None else acc + part
            mixed_ref[pl.ds(i * BLOCK, BLOCK), at : at + head] = acc.astype(BF)
    own = s0_ref.shape[0]
    mixed = mixed_ref[...]
    for j, ref in enumerate((s0_ref, s1_ref, s2_ref, s3_ref)):
        start = jnp.bitwise_xor(gy_ref[0], j) * own
        ref[...] = mm(one_hot_rows(pos_ref[...], start, own), mixed).astype(BF)


def route_kernel(experts, pieces, *refs):
    mixed_refs, out_refs = refs[:4], refs[4:8]
    xs_ref, gs_ref, infos_ref, extras_ref = refs[8:12]
    h2_refs, sg_refs = refs[12 : 12 + pieces], refs[12 + pieces : 12 + 2 * pieces]
    res_ref, prob_ref, gate_ref = refs[12 + 2 * pieces :]
    attn = None
    for j in range(4):
        part = mm_nt(mixed_refs[j][...], out_refs[j][...])
        attn = part if attn is None else attn + part
    extras = extras_ref[...]
    gain = jnp.transpose(extras.astype(F32))[1:2]
    residual = xs_ref[...].astype(F32) + attn
    res_ref[...] = residual
    scale = lax.rsqrt(jnp.mean(residual * residual, axis=-1, keepdims=True) + EPS)
    h2 = (residual * scale * gain).astype(BF)
    logits = mm(h2, extras)
    lane = lax.broadcasted_iota(jnp.int32, logits.shape, 1)
    real = (lane >= 2) & (lane < 2 + experts)
    logits = jnp.where(real, logits, -1e30)
    e = jnp.exp(logits - jnp.max(logits, axis=-1, keepdims=True))
    prob = e / jnp.sum(e, axis=-1, keepdims=True)
    prob_ref[...] = prob
    info = infos_ref[...]
    keep = info[:, 0:1]
    gate = jnp.sum(jnp.where(real, prob * info, 0.0), axis=-1, keepdims=True)
    gate_ref[...] = jnp.broadcast_to(gate, gate_ref.shape)
    h2 = jnp.where(keep > 0.0, h2.astype(F32), 0.0).astype(BF)
    sg = jnp.where(keep > 0.0, gate * gs_ref[...].astype(F32), 0.0).astype(BF)
    split(h2, h2_refs)
    split(sg, sg_refs)


def split(value, refs):
    rows = refs[0].shape[0]
    for n, ref in enumerate(refs):
        ref[...] = value[n * rows : (n + 1) * rows, :]


def joined(refs):
    if len(refs) == 1:
        return refs[0][...]
    return jnp.concatenate([ref[...] for ref in refs], axis=0)


def fetch(packs, buf, sems, first):
    copies = []
    at = 0
    for n, pack in enumerate(packs):
        rows = pack.shape[0]
        copy = pltpu.make_async_copy(pack, buf.at[pl.ds(at, rows), :], sems.at[first + n])
        copy.start()
        copies.append(copy)
        at += rows
    return copies


def out_half(buf, j, n, hidden):
    model = buf.shape[1] // 2
    return buf[j, model + n * hidden : model + (n + 1) * hidden, :]


def expert_kernel(pieces, groups, last, *refs):
    row_refs = refs[:pieces]
    refs = refs[pieces:]
    if last:
        before_ref, refs = refs[0], refs[1:]
    total = sum(groups)
    packs, refs = refs[:total], refs[total:]
    outs = refs[: pieces if last else 1]
    act_ref, slope_ref, buf, sems = refs[len(outs) :]
    hidden = act_ref.shape[2]
    copies = []
    first = 0
    for j, size in enumerate(groups):
        copies.append(fetch(packs[first : first + size], buf.at[j], sems, first))
        first += size
    rows = joined(row_refs)
    left = before_ref[:, : rows.shape[1] // 2] if last else None
    right = before_ref[:, rows.shape[1] // 2 :] if last else None
    for j in range(len(groups)):
        for copy in copies[j]:
            copy.wait()
        pre = mm(rows, buf[j, : rows.shape[1], :])
        cdf = 0.5 * (1.0 + lax.erf(pre * 0.7071067811865476))
        slope = cdf + pre * (0.3989422804014327 * jnp.exp(-0.5 * pre * pre))
        act = (pre * cdf).astype(BF)
        act_ref[j] = act
        slope_ref[j] = slope.astype(BF)
        a = mm(act, out_half(buf, j, 0, hidden))
        b = mm(act, out_half(buf, j, 1, hidden))
        left = a if left is None else left + a
        right = b if right is None else right + b
    whole = jnp.concatenate([left, right], axis=1)
    if last:
        split(whole.astype(BF), outs)
    else:
        outs[0][...] = whole


def expert_back_kernel(pieces, groups, *refs):
    sg_refs = refs[:pieces]
    slopes = refs[pieces : pieces + 2]
    total = sum(groups)
    refs = refs[pieces + 2 :]
    packs, gr_refs = refs[:total], refs[total : total + pieces]
    gp_ref, buf, sems = refs[total + pieces :]
    hidden = gp_ref.shape[2]
    copies = []
    first = 0
    for j, size in enumerate(groups):
        copies.append(fetch(packs[first : first + size], buf.at[j], sems, first))
        first += size
    sg = joined(sg_refs)
    model = sg.shape[1]
    acc = None
    for j in range(len(groups)):
        for copy in copies[j]:
            copy.wait()
        grad = mm_nt(sg[:, : model // 2], out_half(buf, j, 0, hidden))
        grad = grad + mm_nt(sg[:, model // 2 :], out_half(buf, j, 1, hidden))
        grad = (grad * slopes[j // 4][j % 4].astype(F32)).astype(BF)
        gp_ref[j] = grad
        part = mm_nt(grad, buf[j, :model, :])
        acc = part if acc is None else acc + part
    split(acc.astype(BF), gr_refs)


def outer_sent_kernel(pieces, picks, flip, *refs):
    wide = joined(refs[:pieces])
    sources, out_ref = refs[pieces:-1], refs[-1]
    for n, (a, b) in enumerate(picks):
        thin = sources[a][b]
        out_ref[n] = (mm_tn(thin, wide) if flip else mm_tn(wide, thin)).astype(BF)


def outer_held_kernel(pieces, picks, flip, *refs):
    wide = joined(refs[:pieces])
    sources, arrived_ref = refs[pieces:-5], refs[-5]
    out_refs = refs[-4:]
    for n, (a, b) in enumerate(picks):
        thin = sources[a][b]
        value = mm_tn(thin, wide) if flip else mm_tn(wide, thin)
        value = value + arrived_ref[n].astype(F32)
        out_refs[n][...] = value.astype(out_refs[n].dtype)


def joined_kernel(counts, kernels, *refs):
    sources = refs[: sum(c[0] for c in counts)]
    results = refs[len(sources) :]
    for (taken, given), kernel in zip(counts, kernels):
        kernel(*sources[:taken], *results[:given])
        sources, results = sources[taken:], results[given:]


def deliver_kernel(experts, pieces, *refs):
    er_refs = refs[:pieces]
    res_ref, xs_ref, gs_ref, infos_ref, prob_ref, gate_ref, extras_ref = refs[
        pieces : pieces + 7
    ]
    h2_refs = refs[pieces + 7 : 2 * pieces + 7]
    d1_ref, gh_ref, router_ref = refs[2 * pieces + 7 :]
    prob = prob_ref[...]
    gate = gate_ref[...][:, 0:1]
    lane = lax.broadcasted_iota(jnp.int32, prob.shape, 1)
    real = (lane >= 2) & (lane < 2 + experts)
    hot = jnp.where(real, infos_ref[...], 0.0)
    result = joined(er_refs).astype(F32)
    d1_ref[...] = (res_ref[...] - xs_ref[...].astype(F32) + gate * result).astype(BF)
    grad_gate = jnp.sum(gs_ref[...].astype(F32) * result, axis=-1, keepdims=True)
    grad_logits = (prob * (hot - gate) * grad_gate).astype(BF)
    gh_ref[...] = mm_nt(grad_logits, extras_ref[...])
    router_ref[...] = mm_tn(grad_logits, joined(h2_refs))[: router_ref.shape[0]]


def combine_kernel(pieces, *refs):
    gr_refs = refs[:pieces]
    gh_ref, res_ref, gs_ref, router_ref, extras_ref = refs[pieces : pieces + 5]
    out_refs, mixed_refs = refs[pieces + 5 : pieces + 9], refs[pieces + 9 : pieces + 13]
    gm_refs = refs[pieces + 13 : pieces + 17]
    d2_ref, small_ref, keep_ref, send_ref = refs[pieces + 17 :]
    gain = jnp.transpose(extras_ref[...].astype(F32))[1:2]
    residual = res_ref[...]
    g = gs_ref[...].astype(F32)
    grad_h2 = gh_ref[...] + joined(gr_refs).astype(F32)
    scale = lax.rsqrt(jnp.mean(residual * residual, axis=-1, keepdims=True) + EPS)
    unit = residual * scale
    scaled = grad_h2 * gain
    centre = jnp.mean(scaled * unit, axis=-1, keepdims=True)
    d2 = (scale * (scaled - unit * centre)).astype(BF)
    d2_ref[...] = d2
    grad_attn = (g + d2.astype(F32)).astype(BF)
    for j in range(4):
        gm_refs[j][...] = mm(grad_attn, out_refs[j][...]).astype(BF)
    for target, j in ((keep_ref, 0), (send_ref, 1)):
        mixed = jnp.concatenate([mixed_refs[j][...], mixed_refs[j + 2][...]], axis=1)
        target[...] = mm_tn(grad_attn, mixed).astype(BF)
    grad_gain = jnp.sum(grad_h2 * unit, axis=0, keepdims=True)
    small = router_ref[...]
    row = lax.broadcasted_iota(jnp.int32, small.shape, 0)
    small_ref[...] = jnp.where(row == 1, grad_gain, small)


def unskew_sum(block):
    zeros = jnp.zeros((8, BLOCK), F32)
    acc = None
    for i in range(BLOCK // 8):
        piece = jnp.concatenate([block[8 * i : 8 * i + 8, :], zeros], axis=1)
        shift = BLOCK - 8 - 8 * i
        if shift:
            piece = pltpu.roll(piece, shift, 1)
        acc = piece if acc is None else acc + piece
    left = 7 - lax.broadcasted_iota(jnp.int32, acc.shape, 0)
    for bit in range(3):
        moved = pltpu.roll(acc, 1 << bit, 1)
        acc = jnp.where((left >> bit) & 1 == 1, moved, acc)
    return jnp.sum(acc, axis=0, keepdims=True)


def attend_back_kernel(count, *refs):
    gy_ref, gx_ref, g0_ref, g1_ref, g2_ref, g3_ref = refs[:6]
    pos_ref, prob_ref, qkv_ref, h1_ref, x_ref, w_ref, extras_ref, brev_ref = refs[6:14]
    d2_ref, small_ref = refs[14:16]
    dw_refs = refs[16 : 16 + count]
    keep_ref, send_ref, table_ref, gm_ref, grads_ref, dw_buf = refs[16 + count :]
    seq, width = gm_ref.shape
    blocks = seq // BLOCK
    head = 64
    heads = width // head
    own = g0_ref.shape[0]
    gy = gy_ref[0]
    for i in range(blocks):
        rows = pl.ds(i * BLOCK, BLOCK)
        pos = pos_ref[rows, :]
        acc = None
        for j, ref in enumerate((g0_ref, g1_ref, g2_ref, g3_ref)):
            part = mm(one_hot_cols(pos, jnp.bitwise_xor(gy, j) * own, own), ref[...])
            acc = part if acc is None else acc + part
        gm_ref[rows, :] = acc.astype(BF)
    sums = [[None] * heads for _ in range(blocks)]
    for h in range(heads):
        at = h * head
        diagonals = [None] * blocks
        grad_keys = [None] * blocks
        grad_values = [None] * blocks
        for i in range(blocks):
            rows = pl.ds(i * BLOCK, BLOCK)
            q = qkv_ref[rows, :][:, at : at + head]
            gm = gm_ref[rows, :][:, at : at + head]
            centre = None
            kept = []
            for j in range(i + 1):
                value = qkv_ref[pl.ds(j * BLOCK, BLOCK), :][
                    :, 2 * width + at : 2 * width + at + head
                ]
                low = prob_ref[h * (blocks * (blocks + 1) // 2) + i * (i + 1) // 2 + j]
                prob = low.astype(F32)
                grad_prob = mm_nt(gm, value)
                both = prob * grad_prob
                centre = both if centre is None else centre + both
                kept.append((prob, grad_prob))
                part = mm_tn(low, gm)
                grad_values[j] = part if grad_values[j] is None else grad_values[j] + part
            centre = jnp.sum(centre, axis=-1, keepdims=True)
            acc = None
            for j in range(i + 1):
                prob, grad_prob = kept[j]
                score = prob * (grad_prob - centre)
                diagonals[i - j] = score if diagonals[i - j] is None else diagonals[i - j] + score
                score = score.astype(BF)
                key = qkv_ref[pl.ds(j * BLOCK, BLOCK), :][:, width + at : width + at + head]
                part = mm(score, key)
                acc = part if acc is None else acc + part
                part = mm_tn(score, q)
                grad_keys[j] = part if grad_keys[j] is None else grad_keys[j] + part
            grads_ref[rows, at : at + head] = (acc * 0.125).astype(BF)
        for j in range(blocks):
            rows = pl.ds(j * BLOCK, BLOCK)
            grads_ref[rows, width + at : width + at + head] = grad_keys[j].astype(BF)
            grads_ref[rows, 2 * width + at : 2 * width + at + head] = grad_values[j].astype(BF)
        for k in range(blocks):
            sums[k][h] = unskew_sum(diagonals[k])
    bucket_count = table_ref.shape[0]
    columns = None
    for k in range(blocks):
        labels = lax.broadcasted_iota(jnp.int32, (bucket_count, 2 * BLOCK), 0)
        hot = jnp.where(labels == brev_ref[k : k + 1, :], 1.0, 0.0)
        lines = jnp.concatenate(sums[k] + [jnp.zeros((8 - heads, 2 * BLOCK), F32)], axis=0)
        part = mm_nt(hot, lines, HIGH)
        columns = part if columns is None else columns + part
    table_ref[...] = columns
    gain_total = None
    weights = w_ref[...]
    gain = jnp.transpose(extras_ref[...].astype(F32))[0:1]
    for j in range(4):
        rows = pl.ds(pl.multiple_of(jnp.bitwise_xor(gy, j) * BLOCK, BLOCK), BLOCK)
        part = mm_nt(grads_ref[rows, :], weights)
        x = x_ref[rows, :].astype(F32)
        scale = lax.rsqrt(jnp.mean(x * x, axis=-1, keepdims=True) + EPS)
        unit = x * scale
        line = jnp.sum(part * unit, axis=0, keepdims=True)
        gain_total = line if gain_total is None else gain_total + line
        scaled = part * gain
        centre = jnp.mean(scaled * unit, axis=-1, keepdims=True)
        part = scale * (scaled - unit * centre)
        part = part + mm(one_hot_cols(pos_ref[rows, :], gy * own, own), d2_ref[...])
        target = send_ref if j % 2 else keep_ref
        target[j // 2] = part.astype(BF)
    small = small_ref[...]
    row = lax.broadcasted_iota(jnp.int32, small.shape, 0)
    small = jnp.where(row == 0, gain_total, small)
    spare = dw_buf.shape[1] - 3 * width
    small = jnp.concatenate(
        [small, jnp.zeros((LANES - small.shape[0], small.shape[1]), F32)], axis=0
    )
    small = jnp.transpose(small)[:, :spare]
    grads = mm_tn(h1_ref[...], grads_ref[...])
    dw_buf[...] = jnp.concatenate([grads, small], axis=1).astype(BF)
    if len(dw_refs) == 1:
        dw_refs[0][...] = dw_buf[...]
        return
    rows = dw_refs[0].shape[1]
    column = jnp.concatenate([columns[:, h : h + 1] for h in range(heads)], axis=0)
    column = jnp.broadcast_to(column, (rows, spare)).astype(BF)
    last = lax.broadcasted_iota(jnp.int32, (rows, spare), 1) == spare - 1
    for n in range(8):
        at = pl.multiple_of(jnp.bitwise_xor(gx_ref[0], n) * rows, 32)
        piece = dw_buf[pl.ds(at, rows), :]
        tail = jnp.where(last, column, piece[:, 3 * width :])
        dw_refs[n % 2][n // 2] = jnp.concatenate([piece[:, : 3 * width], tail], axis=1)


def unsort_kernel(gy_ref, pos_ref, x_ref, d0_ref, d1_ref, d2_ref, d3_ref, out_ref):
    own = d0_ref.shape[0]
    gy = gy_ref[0]
    for i in range(x_ref.shape[0] // BLOCK):
        rows = pl.ds(i * BLOCK, BLOCK)
        pos = pos_ref[rows, :]
        acc = x_ref[rows, :].astype(F32)
        for j, ref in enumerate((d0_ref, d1_ref, d2_ref, d3_ref)):
            acc = acc + mm(one_hot_cols(pos, jnp.bitwise_xor(gy, j) * own, own), ref[...])
        out_ref[rows, :] = acc


def finish_kernel(gy_ref, own_ref, other_ref, g_ref, out_ref):
    gy = gy_ref[0]
    for j in range(4):
        rows = pl.ds(pl.multiple_of(jnp.bitwise_xor(gy, j) * BLOCK, BLOCK), BLOCK)
        source = other_ref if j % 2 else own_ref
        out_ref[rows, :] = g_ref[rows, :].astype(F32) + source[j // 2].astype(F32)


def swap(x, axis, bit):
    size = lax.axis_size(axis)
    return lax.ppermute(x, axis, [(i, i ^ bit) for i in range(size)])


def gather_rows(chains, *fills):
    size = lax.axis_size("gx")
    if size != len(RING):
        return [
            lax.all_to_all(
                jnp.broadcast_to(x[None], (size,) + x.shape).reshape(-1, x.shape[1]),
                "gx",
                split_axis=0,
                concat_axis=0,
                tiled=True,
            )
            for x in chains
        ]
    ahead = [(RING[n], RING[(n + 1) % size]) for n in range(size)]
    back = [(b, a) for a, b in ahead]
    out = [[x] for x in chains]
    up, down = list(chains), list(chains)
    for step in range(3):
        for n in range(len(chains)):
            up[n] = lax.ppermute(up[n], "gx", ahead)
            down[n] = lax.ppermute(down[n], "gx", back)
            out[n] += [up[n], down[n]]
        if step < len(fills):
            up[0] = after(up[0], *fills[step])
    return sum([out[n] + [lax.ppermute(up[n], "gx", ahead)] for n in range(len(chains))], [])


def spread(parts, experts):
    if len(parts) == experts:
        return [parts[0]] + [swap(parts[k], "gx", 2 * k) for k in range(1, experts)]
    rows = parts[0].shape[0] // experts
    cut = [parts[0][k * rows : (k + 1) * rows] for k in range(experts)]
    return [jnp.concatenate(spread(cut, experts), axis=0)]


def sum_rows(parts):
    if len(parts) == 1:
        size = lax.axis_size("gx")
        arrived = lax.all_to_all(parts[0], "gx", split_axis=0, concat_axis=0, tiled=True)
        arrived = arrived.reshape(size, parts[0].shape[0] // size, parts[0].shape[1])
        return arrived.astype(F32).sum(axis=0)
    pair = add(parts[0], swap(parts[1], "gx", 1))
    total = pair[0]
    for n in range(1, pair.shape[0]):
        total = total + swap(pair[n].astype(BF), "gx", 2 * n).astype(F32)
    return total


def sum_all(x, axis):
    bit = 1
    while bit < lax.axis_size(axis):
        x = x + swap(x, axis, bit)
        bit *= 2
    return x


def after(x, *others):
    return lax.optimization_barrier((x, *others))[0]


def add(a, b):
    return a.astype(F32) + b.astype(F32)


def on_device(
    layer_input,
    w_query,
    w_key,
    w_value,
    w_output,
    attn_gain,
    moe_gain,
    router,
    rel_table,
    w_in,
    w_out,
    expert_ids,
    buckets,
    block_mask,
    grad_out,
):
    n_gx = lax.axis_size("gx")
    n_gy = lax.axis_size("gy")
    seq, model = layer_input.shape
    heads, bucket_count = rel_table.shape
    width = w_query.shape[1]
    shard = w_query.shape[0]
    experts = router.shape[1]
    hidden = w_in.shape[2]
    capacity = 5 * seq // (4 * experts)
    piece = capacity // (2 * n_gy)
    own = experts * 2 * piece
    blocks = seq // BLOCK
    pairs = blocks * (blocks + 1) // 2
    gy = lax.axis_index("gy").astype(jnp.int32).reshape(1)

    gx = lax.axis_index("gx").astype(jnp.int32).reshape(1)
    group = own // experts
    pieces = experts if group % 16 == 0 else 1

    qkv_w, extras = call(
        pack_kernel,
        "pack",
        [struct((shard, 3 * width), BF), struct((shard, LANES + width), BF)],
        [VM] * 7,
        (
            w_query,
            w_key,
            w_value,
            w_output,
            attn_gain.reshape(1, shard),
            moe_gain.reshape(1, shard),
            router,
        ),
        cost=1,
    )
    half_model = model // 2
    pack = jnp.concatenate([w_in[0], w_out[0][:, :half_model], w_out[0][:, half_model:]], axis=0)
    pack_x = swap(pack, "gy", 2)

    pos_row, pos_col, info = call(
        partial(place_kernel, experts, capacity, group),
        "place",
        [
            struct((1, seq), jnp.int32),
            struct((seq, 1), jnp.int32),
            struct((LANES, seq), BF),
        ],
        [SM, VM],
        (gx, after(expert_ids, qkv_w).reshape(1, seq)),
        cost=2,
    )
    backwards = jnp.concatenate([buckets[::-1], jnp.full((BLOCK,), -1, jnp.int32)])
    brev = jnp.stack(
        [
            backwards[seq - BLOCK * (k + 1) : seq - BLOCK * (k + 1) + 2 * BLOCK]
            for k in range(blocks)
        ]
    )
    table_pad = jnp.concatenate([rel_table, jnp.zeros((8 - heads, bucket_count), F32)], axis=0)
    weights = gather_rows((qkv_w, extras), (pos_row,), (brev, table_pad))
    parts = len(weights) // 2
    pack_y = swap(after(pack, weights[-1]), "gx", 1)
    extras, out_own = call(
        partial(unpack_kernel, parts),
        "unpack",
        [struct((model, LANES), BF), struct((model, width), BF)],
        [SM] + [ANY] * parts,
        (gx, *weights[parts:]),
        scratch=[
            pltpu.VMEM((model, LANES + width), BF),
            pltpu.SemaphoreType.DMA((parts,)),
        ],
        cost=2,
    )
    extras, pack_x = lax.optimization_barrier((extras, pack_x))
    out_core = swap(out_own, "gy", 1)
    out_x = swap(out_own, "gy", 2)
    pack_c = swap(pack, "gy", 1)
    pack_xc = swap(pack_x, "gy", 1)

    h1, qkv, prob, mixed, *sorted_parts, w_full = call(
        partial(attend_kernel, parts),
        "attend",
        [
            struct((seq, model), BF),
            struct((seq, 3 * width), BF),
            struct((heads * pairs, BLOCK, BLOCK), BF),
            struct((seq, width), BF),
        ]
        + [struct((own, width), BF)] * 4
        + [struct((model, 3 * width), BF)],
        [SM, SM, SM] + [VM] * 5 + [ANY] * parts,
        (
            gy,
            gx,
            block_mask,
            layer_input,
            extras,
            table_pad,
            brev,
            pos_row,
            *weights[:parts],
        ),
        scratch=[
            pltpu.VMEM((blocks, BLOCK, BLOCK), F32),
            pltpu.SemaphoreType.DMA((parts,)),
        ],
        cost=60,
    )
    mixed_pieces = [sorted_parts[0]] + [swap(sorted_parts[j], "gy", j) for j in (1, 2, 3)]
    xs, gs, infos = call(
        presort_kernel,
        "presort",
        [struct((own, model), BF), struct((own, model), BF), struct((own, LANES), F32)],
        [SM, VM, VM, VM, VM],
        (gy, after(pos_row, sorted_parts[0]), layer_input, grad_out, info),
        cost=5,
    )
    pack_d = swap(after(pack_x, sorted_parts[0]), "gx", 1)
    out_far = swap(after(out_x, sorted_parts[0]), "gy", 1)
    out_pieces = [out_own, out_core, out_x, out_far]
    mixed_pieces[0], pack_c, pack_xc = lax.optimization_barrier((mixed_pieces[0], pack_c, pack_xc))
    slot_shapes = [struct((own // pieces, model), BF)] * pieces
    routed = call(
        partial(route_kernel, experts, pieces),
        "route",
        slot_shapes
        + slot_shapes
        + [
            struct((own, model), F32),
            struct((own, LANES), F32),
            struct((own, LANES), F32),
        ],
        [VM] * 12,
        (*mixed_pieces, *out_pieces, xs, gs, infos, extras),
        cost=5,
    )
    h2, sg = routed[:pieces], routed[pieces : 2 * pieces]
    residual, router_prob, gate = routed[2 * pieces :]
    pack_yc = swap(after(pack_y, h2[0]), "gy", 1)
    rows_in = spread(h2, experts)
    near = [pack, pack_c, pack_x, pack_xc]
    sg = list(lax.optimization_barrier((*sg, *rows_in))[: len(sg)])
    grads_in = spread(sg, experts)

    def pack_scratch(shards, copies):
        return [
            pltpu.VMEM((shards, 2 * model, hidden), BF),
            pltpu.SemaphoreType.DMA((copies,)),
        ]

    kept_shapes = [struct((4, own, hidden), BF)] * 2
    begun, act_a, slope_a = call(
        partial(expert_kernel, pieces, (1, 1, 1, 1), False),
        "expert_near",
        [struct((own, model), F32)] + kept_shapes,
        [VM] * pieces + [ANY] * 4,
        (*rows_in, *near),
        scratch=pack_scratch(4, 4),
        cost=7,
    )
    pack_d, begun = lax.optimization_barrier((pack_d, begun, *grads_in))[:2]
    far = [pack_y, pack_yc, pack_d, swap(pack_d, "gy", 1)]
    *result, act_b, slope_b = call(
        partial(expert_kernel, pieces, (1, 1, 1, 1), True),
        "expert_far",
        slot_shapes + kept_shapes,
        [VM] * (pieces + 1) + [ANY] * 4,
        (*rows_in, begun, *far),
        scratch=pack_scratch(4, 4),
        cost=7.5,
    )
    result_back = spread(result, experts)
    ours = ((0, 0), (0, 2), (1, 2), (1, 0))
    theirs = ((0, 1), (0, 3), (1, 3), (1, 1))
    (out_sent,) = call(
        partial(outer_sent_kernel, pieces, theirs, True),
        "outer_out_sent",
        [struct((4, hidden, model), BF)],
        [VM] * (pieces + 2),
        (*grads_in, act_a, act_b),
        cost=4.7,
    )
    out_arrived = swap(out_sent, "gy", 1)
    slope_b = after(slope_b, out_sent)
    *grad_rows, grad_pre = call(
        partial(expert_back_kernel, pieces, (1,) * 8),
        "expert_back",
        slot_shapes + [struct((8, own, hidden), BF)],
        [VM] * (pieces + 2) + [ANY] * 8,
        (*grads_in, slope_a, slope_b, *near, *far),
        scratch=pack_scratch(8, 8),
        cost=12,
    )
    rows_back = spread(grad_rows, experts)
    small_rows = -(-(2 + experts) // 8) * 8
    held_args = (*grads_in, act_a, act_b, out_arrived)
    sent_args = (*rows_in, grad_pre)
    deliver_args = (*result_back, residual, xs, gs, infos, router_prob, gate, extras, *h2)
    out_mine, out_by_x, out_far_y, out_by_y, in_sent, d1, grad_hidden, router_part = call(
        partial(
            joined_kernel,
            ((len(held_args), 4), (len(sent_args), 1), (len(deliver_args), 3)),
            (
                partial(outer_held_kernel, pieces, ours, True),
                partial(
                    outer_sent_kernel, pieces, tuple((0, 4 * a + b) for a, b in theirs), False
                ),
                partial(deliver_kernel, experts, pieces),
            ),
        ),
        "fill_rows",
        [
            struct((hidden, model), F32),
            struct((hidden, model), BF),
            struct((hidden, model), BF),
            struct((hidden, model), BF),
            struct((4, model, hidden), BF),
            struct((own, model), BF),
            struct((own, model), F32),
            struct((small_rows, model), F32),
        ],
        [VM] * (len(held_args) + len(sent_args) + len(deliver_args)),
        (*held_args, *sent_args, *deliver_args),
        cost=13,
    )
    out_far_y = swap(out_far_y, "gx", 1)
    in_arrived = swap(in_sent, "gy", 1)
    *mixed_grads, d2, small, project_keep, project_send = call(
        partial(combine_kernel, pieces),
        "combine",
        [struct((own, width), BF)] * 4
        + [
            struct((own, model), BF),
            struct((small_rows, model), F32),
            struct((model, 2 * width), BF),
            struct((model, 2 * width), BF),
        ],
        [VM] * (pieces + 13),
        (
            *rows_back,
            grad_hidden,
            residual,
            gs,
            router_part,
            extras,
            *out_pieces,
            *mixed_pieces,
        ),
        cost=40,
    )
    grads_mixed = [mixed_grads[0]] + [swap(mixed_grads[j], "gy", j) for j in (1, 2, 3)]
    project_other = swap(project_send, "gy", 1)
    in_mine, in_by_x, in_far_y, in_by_y = call(
        partial(outer_held_kernel, pieces, tuple((0, 4 * a + b) for a, b in ours), False),
        "outer_in_held",
        [
            struct((model, hidden), F32),
            struct((model, hidden), BF),
            struct((model, hidden), BF),
            struct((model, hidden), BF),
        ],
        [VM] * (pieces + 2),
        (*rows_in, after(grad_pre, mixed_grads[0]), in_arrived),
        cost=1,
    )
    in_far_y = swap(in_far_y, "gx", 1)
    out_sum_x = add(out_by_x, after(out_far_y, in_mine)).astype(BF)
    grads_mixed[0], in_by_x, out_sum_x = lax.optimization_barrier(
        (grads_mixed[0], in_by_x, out_sum_x)
    )
    out_from_x = swap(out_sum_x, "gy", 2)
    d1_x = swap(after(d1, *grads_mixed[1:]), "gy", 2)
    spare = -(-3 * width // LANES) * LANES - 3 * width
    count = 2 if n_gx == len(RING) and heads * bucket_count == shard else 1
    dw_shape = (model, 3 * width + spare) if count == 1 else (4, shard, 3 * width + spare)
    *dw, keep, send, table = call(
        partial(attend_back_kernel, count),
        "attend_back",
        [struct(dw_shape, BF)] * count
        + [
            struct((2, BLOCK, model), BF),
            struct((2, BLOCK, model), BF),
            struct((bucket_count, 8), F32),
        ],
        [SM, SM] + [VM] * 14,
        (
            gy,
            gx,
            *grads_mixed,
            pos_col,
            prob,
            qkv,
            h1,
            layer_input,
            w_full,
            extras,
            brev,
            d2,
            small,
        ),
        scratch=[
            pltpu.VMEM((seq, width), BF),
            pltpu.VMEM((seq, 3 * width), BF),
            pltpu.VMEM((model, 3 * width + spare), BF),
        ],
        cost=60,
    )
    keep, send, in_far_y, out_from_x, d1_x = lax.optimization_barrier(
        (keep, send, in_far_y, out_from_x, d1_x)
    )
    half = add(keep, swap(send, "gy", 1)).astype(BF)
    half, out_by_y, d1, d1_x, project_keep, *dw = lax.optimization_barrier(
        (half, out_by_y, d1, d1_x, project_keep, *dw)
    )
    out_from_y = swap(out_by_y, "gx", 1)
    d1s = [d1, swap(d1, "gy", 1), d1_x, swap(d1_x, "gy", 1)]
    projected = add(project_keep, project_other).astype(BF)
    projected = lax.all_to_all(projected, "gx", split_axis=0, concat_axis=0, tiled=True)
    total = add(half, swap(half, "gy", 2)[::-1]).astype(BF)
    other = swap(total, "gy", 1)
    summed = sum_rows(dw)
    projected = projected.reshape(n_gx, shard, 2 * width).astype(F32).sum(axis=0)
    small = summed[:, 3 * width :]
    small = small + swap(small, "gy", 1)
    line = swap(jnp.concatenate([small, projected[:, width:]], axis=1), "gy", 2)
    small = small + line[:, :spare]
    grad_out_proj = projected[:, :width] + line[:, spare:]
    if count == 1:
        grad_table = sum_all(table, "gx")[:, :heads].T
    else:
        grad_table = summed[:, -1].reshape(heads, bucket_count)
    (layer_output,) = call(
        unsort_kernel,
        "unsort",
        [struct((seq, model), F32)],
        [SM] + [VM] * 6,
        (gy, pos_col, layer_input, *d1s),
        cost=7,
    )
    (grad_input,) = call(
        finish_kernel,
        "finish",
        [struct((seq, model), F32)],
        [SM] + [VM] * 3,
        (gy, total, other, grad_out),
        cost=4,
    )
    in_sum_x = add(after(in_by_x, half), in_far_y).astype(BF)
    in_from_x = swap(in_sum_x, "gy", 2)
    in_from_y = swap(after(in_by_y, half), "gx", 1)
    grad_w_out = add(add(out_mine, out_from_y), out_from_x)
    grad_w_in = add(add(in_mine, in_from_y), in_from_x)

    return (
        layer_output,
        grad_input,
        summed[:, :width],
        summed[:, width : 2 * width],
        summed[:, 2 * width : 3 * width],
        grad_out_proj,
        small[:, 0],
        small[:, 1],
        small[:, 2 : 2 + experts],
        grad_table,
        grad_w_in[None],
        grad_w_out[None],
    )


def solution(mesh):
    return jax.shard_map(
        on_device,
        mesh=mesh,
        in_specs=(
            P("gx", None),
            P("gx", "gy"),
            P("gx", "gy"),
            P("gx", "gy"),
            P("gx", "gy"),
            P("gx"),
            P("gx"),
            P("gx", None),
            P("gy", None),
            P("gx", None, "gy"),
            P("gx", "gy", None),
            P("gx", None),
            P(),
            P(),
            P("gx", None),
        ),
        out_specs=(
            P("gx", None),
            P("gx", None),
            P("gx", "gy"),
            P("gx", "gy"),
            P("gx", "gy"),
            P("gx", "gy"),
            P("gx"),
            P("gx"),
            P("gx", None),
            P("gy", None),
            P("gx", None, "gy"),
            P("gx", "gy", None),
        ),
        check_vma=False,
    )
```

```python
from functools import partial

import jax
import jax.numpy as jnp
from jax import lax
from jax.experimental import pallas as pl
from jax.experimental.pallas import tpu as pltpu
from jax.sharding import PartitionSpec as P

BLOCK = 256
EPS = 1e-06
LANES = 128
BF = jnp.bfloat16
F32 = jnp.float32
HIGH = lax.Precision.HIGHEST
VMEM_BYTES = 56 * 1024 * 1024
PEAK = 1.15e9
RING = (0, 2, 4, 6, 7, 5, 3, 1)
RING_STEPS = (0, -1, 1, -2, 2, -3, 3, -4)


def mm(left, right, precision=None):
    return lax.dot_general(
        left, right, (((1,), (0,)), ((), ())), precision=precision, preferred_element_type=F32
    )


def mm_nt(left, right, precision=None):
    return lax.dot_general(
        left, right, (((1,), (1,)), ((), ())), precision=precision, preferred_element_type=F32
    )


def mm_tn(left, right, precision=None):
    return lax.dot_general(
        left, right, (((0,), (0,)), ((), ())), precision=precision, preferred_element_type=F32
    )


VM = pl.BlockSpec(memory_space=pltpu.VMEM)
SM = pl.BlockSpec(memory_space=pltpu.SMEM)
ANY = pl.BlockSpec(memory_space=pl.ANY)


def call(kernel, name, outs, in_specs, args, scratch=(), cost=1):
    return pl.pallas_call(
        kernel,
        name=name,
        out_shape=list(outs),
        in_specs=in_specs,
        out_specs=[VM] * len(outs),
        scratch_shapes=list(scratch),
        compiler_params=pltpu.CompilerParams(vmem_limit_bytes=VMEM_BYTES),
        cost_estimate=pl.CostEstimate(
            flops=int(cost * PEAK), bytes_accessed=1, transcendentals=0
        ),
    )(*args)


def struct(shape, dtype):
    return jax.ShapeDtypeStruct(shape, dtype)


def one_hot_rows(pos_row, start, count):
    slots = lax.broadcasted_iota(jnp.int32, (count, pos_row.shape[1]), 0) + start
    return jnp.where(slots == pos_row, 1.0, 0.0).astype(BF)


def one_hot_cols(pos_col, start, count):
    slots = lax.broadcasted_iota(jnp.int32, (pos_col.shape[0], count), 1) + start
    return jnp.where(slots == pos_col, 1.0, 0.0).astype(BF)


def pack_kernel(q_ref, k_ref, v_ref, o_ref, attn_ref, moe_ref, router_ref, qkv_ref, extras_ref):
    qkv_ref[...] = jnp.concatenate([q_ref[...], k_ref[...], v_ref[...]], axis=1)
    experts, rows = router_ref.shape
    lines = jnp.concatenate(
        [
            attn_ref[...].astype(F32),
            moe_ref[...].astype(F32),
            router_ref[...].astype(F32),
            jnp.zeros((LANES - 2 - experts, rows), F32),
        ],
        axis=0,
    )
    lines = jnp.concatenate([lines, jnp.zeros((LANES, LANES - rows), F32)], axis=1)
    extras_ref[...] = jnp.concatenate(
        [jnp.transpose(lines)[:rows].astype(BF), o_ref[...]], axis=1
    )


def lane_prefix(values):
    row = lax.broadcasted_iota(jnp.int32, (LANES, LANES), 0)
    column = lax.broadcasted_iota(jnp.int32, (LANES, LANES), 1)
    sooner = jnp.where(row < column, 1.0, 0.0).astype(BF)
    carry = jnp.zeros((values.shape[0], 1), F32)
    out = []
    for start in range(0, values.shape[1], LANES):
        part = values[:, start : start + LANES]
        out.append(mm(part.astype(BF), sooner) + carry)
        carry = carry + jnp.sum(part, axis=1, keepdims=True)
    return jnp.concatenate(out, axis=1), carry


def place_kernel(experts, capacity, group, gx_ref, ids_ref, row_ref, col_ref, info_ref):
    seq = ids_ref.shape[1]
    ids = ids_ref[...]
    deep = -(-experts // 8) * 8
    label = lax.broadcasted_iota(jnp.int32, (deep, seq), 0)
    hot = jnp.where(label == ids, 1.0, 0.0)
    before, total = lane_prefix(hot)
    rank = jnp.sum(before * hot, axis=0, keepdims=True)
    kept = rank < capacity
    filled = jnp.minimum(total, 1.0 * capacity)
    empty = jnp.where(label[:, 0:1] < experts, capacity - filled, 0.0)
    row = lax.broadcasted_iota(jnp.int32, (deep, deep), 0)
    column = lax.broadcasted_iota(jnp.int32, (deep, deep), 1)
    sooner = jnp.where(column < row, 1.0, 0.0)
    begins = mm(sooner, jnp.broadcast_to(empty, (deep, LANES)), HIGH)[:, 0:1]
    lost = jnp.broadcast_to(jnp.where(kept, 0.0, 1.0), (8, seq))
    order = lane_prefix(lost)[0][0:1]
    inside = (order >= begins) & (order < begins + empty)
    spare_expert = jnp.sum(jnp.where(inside, label.astype(F32), 0.0), axis=0, keepdims=True)
    spare_rank = jnp.sum(jnp.where(inside, order - begins + filled, 0.0), axis=0, keepdims=True)
    expert = jnp.where(kept, ids.astype(F32), spare_expert).astype(jnp.int32)
    rank = jnp.where(kept, rank, spare_rank)
    block = jnp.floor((rank + 0.5) * (1.0 / group))
    near = jnp.bitwise_xor(expert, gx_ref[0] // 2).astype(F32)
    position = block * (experts * group) + near * group + rank - block * group
    row_ref[...] = position.astype(jnp.int32)
    tall = jnp.transpose(jnp.broadcast_to(position, (LANES, seq)))
    col_ref[...] = tall[:, 0:1].astype(jnp.int32)
    line = lax.broadcasted_iota(jnp.int32, (LANES, seq), 0)
    info = jnp.where(line == 0, jnp.where(kept, 1.0, 0.0), jnp.where(line - 2 == ids, 1.0, 0.0))
    info_ref[...] = info.astype(BF)


def presort_kernel(gy_ref, pos_ref, x_ref, g_ref, info_ref, xs_ref, gs_ref, infos_ref):
    own = xs_ref.shape[0]
    pick = one_hot_rows(pos_ref[...], gy_ref[0] * own, own)
    xs_ref[...] = mm(pick, x_ref[...]).astype(BF)
    gs_ref[...] = mm(pick, g_ref[...]).astype(BF)
    infos_ref[...] = mm_nt(pick, info_ref[...])


def ring_source(gx, step):
    spot = jnp.where(gx % 2 == 0, gx // 2, 7 - gx // 2)
    spot = jnp.bitwise_and(spot + step, 7)
    return jnp.where(spot < 4, 2 * spot, 2 * (7 - spot) + 1)


def assemble(pieces, gx_ref, target, sems):
    copies = []
    rows = pieces[0].shape[0]
    for n, piece in enumerate(pieces):
        place = target
        if len(pieces) > 1:
            at = pl.multiple_of(ring_source(gx_ref[0], RING_STEPS[n]) * rows, 32)
            place = target.at[pl.ds(at, rows), :]
        copy = pltpu.make_async_copy(piece, place, sems.at[n])
        copy.start()
        copies.append(copy)
    return copies


def unpack_kernel(count, *refs):
    gx_ref, pieces = refs[0], refs[1 : 1 + count]
    extras_ref, out_ref, buf, sems = refs[1 + count :]
    for copy in assemble(pieces, gx_ref, buf, sems):
        copy.wait()
    extras_ref[...] = buf[:, :LANES]
    out_ref[...] = buf[:, LANES:]


def attend_kernel(count, *refs):
    gy_ref, gx_ref, mask_ref, x_ref, extras_ref, table_ref, brev_ref, pos_ref = refs[:8]
    pieces = refs[8 : 8 + count]
    h1_ref, qkv_ref, prob_ref, mixed_ref, s0_ref, s1_ref, s2_ref, s3_ref = refs[
        8 + count : 16 + count
    ]
    w_ref, toep_ref, sems = refs[16 + count :]
    copies = assemble(pieces, gx_ref, w_ref, sems)
    seq = x_ref.shape[0]
    width = mixed_ref.shape[1]
    blocks = seq // BLOCK
    head = 64
    heads = width // head
    gain = jnp.transpose(extras_ref[...].astype(F32))[0:1]
    for copy in copies:
        copy.wait()
    for i in range(blocks):
        rows = pl.ds(i * BLOCK, BLOCK)
        x = x_ref[rows, :].astype(F32)
        scale = lax.rsqrt(jnp.mean(x * x, axis=-1, keepdims=True) + EPS)
        h1 = (x * scale * gain).astype(BF)
        h1_ref[rows, :] = h1
        out = mm(h1, w_ref[...])
        qkv_ref[rows, :] = jnp.concatenate(
            [out[:, :width].astype(BF) * jnp.asarray(0.125, BF), out[:, width:].astype(BF)], axis=1
        )
    bucket_count = table_ref.shape[1]
    biases = []
    for k in range(blocks):
        labels = lax.broadcasted_iota(jnp.int32, (bucket_count, 2 * BLOCK), 0)
        hot = jnp.where(labels == brev_ref[k : k + 1, :], 1.0, 0.0)
        biases.append(mm(table_ref[...], hot, HIGH))
    for h in range(heads):
        for k in range(blocks):
            line = jnp.broadcast_to(biases[k][h : h + 1, :], (BLOCK, 2 * BLOCK))
            skew = pltpu.roll(line, BLOCK + 1, 1, stride=1, stride_axis=0)[:, :BLOCK]
            if k == 0:
                r = lax.broadcasted_iota(jnp.int32, (BLOCK, BLOCK), 0)
                c = lax.broadcasted_iota(jnp.int32, (BLOCK, BLOCK), 1)
                skew = jnp.where(r >= c, skew, -1e30)
            toep_ref[k] = skew
        at = h * head
        for i in range(blocks):
            q = qkv_ref[pl.ds(i * BLOCK, BLOCK), :][:, at : at + head]
            scores = []
            peak = None
            for j in range(i + 1):
                key = qkv_ref[pl.ds(j * BLOCK, BLOCK), :][:, width + at : width + at + head]
                s = mm_nt(q, key) + toep_ref[i - j]
                if j < i:
                    s = s + jnp.where(mask_ref[i, j] == 1, 0.0, -1e30)
                scores.append(s)
                peak = s if peak is None else jnp.maximum(peak, s)
            peak = jnp.max(peak, axis=-1, keepdims=True)
            total = None
            terms = []
            for s in scores:
                e = jnp.exp(s - peak)
                terms.append(e)
                total = e if total is None else total + e
            inverse = 1.0 / jnp.sum(total, axis=-1, keepdims=True)
            acc = None
            for j in range(i + 1):
                prob = (terms[j] * inverse).astype(BF)
                prob_ref[h * (blocks * (blocks + 1) // 2) + i * (i + 1) // 2 + j] = prob
                value = qkv_ref[pl.ds(j * BLOCK, BLOCK), :][
                    :, 2 * width + at : 2 * width + at + head
                ]
                part = mm(prob, value)
                acc = part if acc is None else acc + part
            mixed_ref[pl.ds(i * BLOCK, BLOCK), at : at + head] = acc.astype(BF)
    own = s0_ref.shape[0]
    mixed = mixed_ref[...]
    for j, ref in enumerate((s0_ref, s1_ref, s2_ref, s3_ref)):
        start = jnp.bitwise_xor(gy_ref[0], j) * own
        ref[...] = mm(one_hot_rows(pos_ref[...], start, own), mixed).astype(BF)


def route_kernel(experts, pieces, *refs):
    mixed_refs, out_refs = refs[:4], refs[4:8]
    xs_ref, gs_ref, infos_ref, extras_ref = refs[8:12]
    h2_refs, sg_refs = refs[12 : 12 + pieces], refs[12 + pieces : 12 + 2 * pieces]
    res_ref, prob_ref, gate_ref = refs[12 + 2 * pieces :]
    attn = None
    for j in range(4):
        part = mm_nt(mixed_refs[j][...], out_refs[j][...])
        attn = part if attn is None else attn + part
    extras = extras_ref[...]
    gain = jnp.transpose(extras.astype(F32))[1:2]
    residual = xs_ref[...].astype(F32) + attn
    res_ref[...] = residual
    scale = lax.rsqrt(jnp.mean(residual * residual, axis=-1, keepdims=True) + EPS)
    h2 = (residual * scale * gain).astype(BF)
    logits = mm(h2, extras)
    lane = lax.broadcasted_iota(jnp.int32, logits.shape, 1)
    real = (lane >= 2) & (lane < 2 + experts)
    logits = jnp.where(real, logits, -1e30)
    e = jnp.exp(logits - jnp.max(logits, axis=-1, keepdims=True))
    prob = e / jnp.sum(e, axis=-1, keepdims=True)
    prob_ref[...] = prob
    info = infos_ref[...]
    keep = info[:, 0:1]
    gate = jnp.sum(jnp.where(real, prob * info, 0.0), axis=-1, keepdims=True)
    gate_ref[...] = jnp.broadcast_to(gate, gate_ref.shape)
    h2 = jnp.where(keep > 0.0, h2.astype(F32), 0.0).astype(BF)
    sg = jnp.where(keep > 0.0, gate * gs_ref[...].astype(F32), 0.0).astype(BF)
    split(h2, h2_refs)
    split(sg, sg_refs)


def split(value, refs):
    rows = refs[0].shape[0]
    for n, ref in enumerate(refs):
        ref[...] = value[n * rows : (n + 1) * rows, :]


def joined(refs):
    if len(refs) == 1:
        return refs[0][...]
    return jnp.concatenate([ref[...] for ref in refs], axis=0)


def fetch(packs, buf, sems, first):
    copies = []
    at = 0
    for n, pack in enumerate(packs):
        rows = pack.shape[0]
        copy = pltpu.make_async_copy(pack, buf.at[pl.ds(at, rows), :], sems.at[first + n])
        copy.start()
        copies.append(copy)
        at += rows
    return copies


def out_half(buf, j, n, hidden):
    model = buf.shape[1] // 2
    return buf[j, model + n * hidden : model + (n + 1) * hidden, :]


def expert_kernel(pieces, groups, last, *refs):
    row_refs = refs[:pieces]
    refs = refs[pieces:]
    if last:
        before_ref, refs = refs[0], refs[1:]
    total = sum(groups)
    packs, refs = refs[:total], refs[total:]
    outs = refs[: pieces if last else 1]
    act_ref, slope_ref, buf, sems = refs[len(outs) :]
    hidden = act_ref.shape[2]
    copies = []
    first = 0
    for j, size in enumerate(groups):
        copies.append(fetch(packs[first : first + size], buf.at[j], sems, first))
        first += size
    rows = joined(row_refs)
    left = before_ref[:, : rows.shape[1] // 2] if last else None
    right = before_ref[:, rows.shape[1] // 2 :] if last else None
    for j in range(len(groups)):
        for copy in copies[j]:
            copy.wait()
        pre = mm(rows, buf[j, : rows.shape[1], :])
        cdf = 0.5 * (1.0 + lax.erf(pre * 0.7071067811865476))
        slope = cdf + pre * (0.3989422804014327 * jnp.exp(-0.5 * pre * pre))
        act = (pre * cdf).astype(BF)
        act_ref[j] = act
        slope_ref[j] = slope.astype(BF)
        a = mm(act, out_half(buf, j, 0, hidden))
        b = mm(act, out_half(buf, j, 1, hidden))
        left = a if left is None else left + a
        right = b if right is None else right + b
    whole = jnp.concatenate([left, right], axis=1)
    if last:
        split(whole.astype(BF), outs)
    else:
        outs[0][...] = whole


def expert_back_kernel(pieces, groups, *refs):
    sg_refs = refs[:pieces]
    slopes = refs[pieces : pieces + 2]
    total = sum(groups)
    refs = refs[pieces + 2 :]
    packs, gr_refs = refs[:total], refs[total : total + pieces]
    gp_ref, buf, sems = refs[total + pieces :]
    hidden = gp_ref.shape[2]
    copies = []
    first = 0
    for j, size in enumerate(groups):
        copies.append(fetch(packs[first : first + size], buf.at[j], sems, first))
        first += size
    sg = joined(sg_refs)
    model = sg.shape[1]
    acc = None
    for j in range(len(groups)):
        for copy in copies[j]:
            copy.wait()
        grad = mm_nt(sg[:, : model // 2], out_half(buf, j, 0, hidden))
        grad = grad + mm_nt(sg[:, model // 2 :], out_half(buf, j, 1, hidden))
        grad = (grad * slopes[j // 4][j % 4].astype(F32)).astype(BF)
        gp_ref[j] = grad
        part = mm_nt(grad, buf[j, :model, :])
        acc = part if acc is None else acc + part
    split(acc.astype(BF), gr_refs)


def outer_sent_kernel(pieces, picks, flip, *refs):
    wide = joined(refs[:pieces])
    sources, out_ref = refs[pieces:-1], refs[-1]
    for n, (a, b) in enumerate(picks):
        thin = sources[a][b]
        out_ref[n] = (mm_tn(thin, wide) if flip else mm_tn(wide, thin)).astype(BF)


def outer_held_kernel(pieces, picks, flip, *refs):
    wide = joined(refs[:pieces])
    sources, arrived_ref = refs[pieces:-5], refs[-5]
    out_refs = refs[-4:]
    for n, (a, b) in enumerate(picks):
        thin = sources[a][b]
        value = mm_tn(thin, wide) if flip else mm_tn(wide, thin)
        value = value + arrived_ref[n].astype(F32)
        out_refs[n][...] = value.astype(out_refs[n].dtype)


def joined_kernel(counts, kernels, *refs):
    sources = refs[: sum(c[0] for c in counts)]
    results = refs[len(sources) :]
    for (taken, given), kernel in zip(counts, kernels):
        kernel(*sources[:taken], *results[:given])
        sources, results = sources[taken:], results[given:]


def deliver_kernel(experts, pieces, *refs):
    er_refs = refs[:pieces]
    res_ref, xs_ref, gs_ref, infos_ref, prob_ref, gate_ref, extras_ref = refs[
        pieces : pieces + 7
    ]
    h2_refs = refs[pieces + 7 : 2 * pieces + 7]
    d1_ref, gh_ref, router_ref = refs[2 * pieces + 7 :]
    prob = prob_ref[...]
    gate = gate_ref[...][:, 0:1]
    lane = lax.broadcasted_iota(jnp.int32, prob.shape, 1)
    real = (lane >= 2) & (lane < 2 + experts)
    hot = jnp.where(real, infos_ref[...], 0.0)
    result = joined(er_refs).astype(F32)
    d1_ref[...] = (res_ref[...] - xs_ref[...].astype(F32) + gate * result).astype(BF)
    grad_gate = jnp.sum(gs_ref[...].astype(F32) * result, axis=-1, keepdims=True)
    grad_logits = (prob * (hot - gate) * grad_gate).astype(BF)
    gh_ref[...] = mm_nt(grad_logits, extras_ref[...])
    router_ref[...] = mm_tn(grad_logits, joined(h2_refs))[: router_ref.shape[0]]


def combine_kernel(pieces, *refs):
    gr_refs = refs[:pieces]
    gh_ref, res_ref, gs_ref, router_ref, extras_ref = refs[pieces : pieces + 5]
    out_refs, mixed_refs = refs[pieces + 5 : pieces + 9], refs[pieces + 9 : pieces + 13]
    gm_refs = refs[pieces + 13 : pieces + 17]
    d2_ref, small_ref, keep_ref, send_ref = refs[pieces + 17 :]
    gain = jnp.transpose(extras_ref[...].astype(F32))[1:2]
    residual = res_ref[...]
    g = gs_ref[...].astype(F32)
    grad_h2 = gh_ref[...] + joined(gr_refs).astype(F32)
    scale = lax.rsqrt(jnp.mean(residual * residual, axis=-1, keepdims=True) + EPS)
    unit = residual * scale
    scaled = grad_h2 * gain
    centre = jnp.mean(scaled * unit, axis=-1, keepdims=True)
    d2 = (scale * (scaled - unit * centre)).astype(BF)
    d2_ref[...] = d2
    grad_attn = (g + d2.astype(F32)).astype(BF)
    for j in range(4):
        gm_refs[j][...] = mm(grad_attn, out_refs[j][...]).astype(BF)
    for target, j in ((keep_ref, 0), (send_ref, 1)):
        mixed = jnp.concatenate([mixed_refs[j][...], mixed_refs[j + 2][...]], axis=1)
        target[...] = mm_tn(grad_attn, mixed).astype(BF)
    grad_gain = jnp.sum(grad_h2 * unit, axis=0, keepdims=True)
    small = router_ref[...]
    row = lax.broadcasted_iota(jnp.int32, small.shape, 0)
    small_ref[...] = jnp.where(row == 1, grad_gain, small)


def unskew_sum(block):
    zeros = jnp.zeros((8, BLOCK), F32)
    acc = None
    for i in range(BLOCK // 8):
        piece = jnp.concatenate([block[8 * i : 8 * i + 8, :], zeros], axis=1)
        shift = BLOCK - 8 - 8 * i
        if shift:
            piece = pltpu.roll(piece, shift, 1)
        acc = piece if acc is None else acc + piece
    left = 7 - lax.broadcasted_iota(jnp.int32, acc.shape, 0)
    for bit in range(3):
        moved = pltpu.roll(acc, 1 << bit, 1)
        acc = jnp.where((left >> bit) & 1 == 1, moved, acc)
    return jnp.sum(acc, axis=0, keepdims=True)


def attend_back_kernel(count, *refs):
    gy_ref, gx_ref, g0_ref, g1_ref, g2_ref, g3_ref = refs[:6]
    pos_ref, prob_ref, qkv_ref, h1_ref, x_ref, w_ref, extras_ref, brev_ref = refs[6:14]
    d2_ref, small_ref = refs[14:16]
    dw_refs = refs[16 : 16 + count]
    keep_ref, send_ref, table_ref, gm_ref, grads_ref, dw_buf = refs[16 + count :]
    seq, width = gm_ref.shape
    blocks = seq // BLOCK
    head = 64
    heads = width // head
    own = g0_ref.shape[0]
    gy = gy_ref[0]
    for i in range(blocks):
        rows = pl.ds(i * BLOCK, BLOCK)
        pos = pos_ref[rows, :]
        acc = None
        for j, ref in enumerate((g0_ref, g1_ref, g2_ref, g3_ref)):
            part = mm(one_hot_cols(pos, jnp.bitwise_xor(gy, j) * own, own), ref[...])
            acc = part if acc is None else acc + part
        gm_ref[rows, :] = acc.astype(BF)
    sums = [[None] * heads for _ in range(blocks)]
    for h in range(heads):
        at = h * head
        diagonals = [None] * blocks
        grad_keys = [None] * blocks
        grad_values = [None] * blocks
        for i in range(blocks):
            rows = pl.ds(i * BLOCK, BLOCK)
            q = qkv_ref[rows, :][:, at : at + head]
            gm = gm_ref[rows, :][:, at : at + head]
            centre = None
            kept = []
            for j in range(i + 1):
                value = qkv_ref[pl.ds(j * BLOCK, BLOCK), :][
                    :, 2 * width + at : 2 * width + at + head
                ]
                low = prob_ref[h * (blocks * (blocks + 1) // 2) + i * (i + 1) // 2 + j]
                prob = low.astype(F32)
                grad_prob = mm_nt(gm, value)
                both = prob * grad_prob
                centre = both if centre is None else centre + both
                kept.append((prob, grad_prob))
                part = mm_tn(low, gm)
                grad_values[j] = part if grad_values[j] is None else grad_values[j] + part
            centre = jnp.sum(centre, axis=-1, keepdims=True)
            acc = None
            for j in range(i + 1):
                prob, grad_prob = kept[j]
                score = prob * (grad_prob - centre)
                diagonals[i - j] = score if diagonals[i - j] is None else diagonals[i - j] + score
                score = score.astype(BF)
                key = qkv_ref[pl.ds(j * BLOCK, BLOCK), :][:, width + at : width + at + head]
                part = mm(score, key)
                acc = part if acc is None else acc + part
                part = mm_tn(score, q)
                grad_keys[j] = part if grad_keys[j] is None else grad_keys[j] + part
            grads_ref[rows, at : at + head] = (acc * 0.125).astype(BF)
        for j in range(blocks):
            rows = pl.ds(j * BLOCK, BLOCK)
            grads_ref[rows, width + at : width + at + head] = grad_keys[j].astype(BF)
            grads_ref[rows, 2 * width + at : 2 * width + at + head] = grad_values[j].astype(BF)
        for k in range(blocks):
            sums[k][h] = unskew_sum(diagonals[k])
    bucket_count = table_ref.shape[0]
    columns = None
    for k in range(blocks):
        labels = lax.broadcasted_iota(jnp.int32, (bucket_count, 2 * BLOCK), 0)
        hot = jnp.where(labels == brev_ref[k : k + 1, :], 1.0, 0.0)
        lines = jnp.concatenate(sums[k] + [jnp.zeros((8 - heads, 2 * BLOCK), F32)], axis=0)
        part = mm_nt(hot, lines, HIGH)
        columns = part if columns is None else columns + part
    table_ref[...] = columns
    gain_total = None
    weights = w_ref[...]
    gain = jnp.transpose(extras_ref[...].astype(F32))[0:1]
    for j in range(4):
        rows = pl.ds(pl.multiple_of(jnp.bitwise_xor(gy, j) * BLOCK, BLOCK), BLOCK)
        part = mm_nt(grads_ref[rows, :], weights)
        x = x_ref[rows, :].astype(F32)
        scale = lax.rsqrt(jnp.mean(x * x, axis=-1, keepdims=True) + EPS)
        unit = x * scale
        line = jnp.sum(part * unit, axis=0, keepdims=True)
        gain_total = line if gain_total is None else gain_total + line
        scaled = part * gain
        centre = jnp.mean(scaled * unit, axis=-1, keepdims=True)
        part = scale * (scaled - unit * centre)
        part = part + mm(one_hot_cols(pos_ref[rows, :], gy * own, own), d2_ref[...])
        target = send_ref if j % 2 else keep_ref
        target[j // 2] = part.astype(BF)
    small = small_ref[...]
    row = lax.broadcasted_iota(jnp.int32, small.shape, 0)
    small = jnp.where(row == 0, gain_total, small)
    spare = dw_buf.shape[1] - 3 * width
    small = jnp.concatenate(
        [small, jnp.zeros((LANES - small.shape[0], small.shape[1]), F32)], axis=0
    )
    small = jnp.transpose(small)[:, :spare]
    grads = mm_tn(h1_ref[...], grads_ref[...])
    dw_buf[...] = jnp.concatenate([grads, small], axis=1).astype(BF)
    if len(dw_refs) == 1:
        dw_refs[0][...] = dw_buf[...]
        return
    rows = dw_refs[0].shape[1]
    column = jnp.concatenate([columns[:, h : h + 1] for h in range(heads)], axis=0)
    column = jnp.broadcast_to(column, (rows, spare)).astype(BF)
    last = lax.broadcasted_iota(jnp.int32, (rows, spare), 1) == spare - 1
    for n in range(8):
        at = pl.multiple_of(jnp.bitwise_xor(gx_ref[0], n) * rows, 32)
        piece = dw_buf[pl.ds(at, rows), :]
        tail = jnp.where(last, column, piece[:, 3 * width :])
        dw_refs[n % 2][n // 2] = jnp.concatenate([piece[:, : 3 * width], tail], axis=1)


def unsort_kernel(gy_ref, pos_ref, x_ref, d0_ref, d1_ref, d2_ref, d3_ref, out_ref):
    own = d0_ref.shape[0]
    gy = gy_ref[0]
    for i in range(x_ref.shape[0] // BLOCK):
        rows = pl.ds(i * BLOCK, BLOCK)
        pos = pos_ref[rows, :]
        acc = x_ref[rows, :].astype(F32)
        for j, ref in enumerate((d0_ref, d1_ref, d2_ref, d3_ref)):
            acc = acc + mm(one_hot_cols(pos, jnp.bitwise_xor(gy, j) * own, own), ref[...])
        out_ref[rows, :] = acc


def finish_kernel(gy_ref, own_ref, other_ref, g_ref, out_ref):
    gy = gy_ref[0]
    for j in range(4):
        rows = pl.ds(pl.multiple_of(jnp.bitwise_xor(gy, j) * BLOCK, BLOCK), BLOCK)
        source = other_ref if j % 2 else own_ref
        out_ref[rows, :] = g_ref[rows, :].astype(F32) + source[j // 2].astype(F32)


def close_kernel(experts, small_ref, line_ref, project_ref, *outs):
    first_ref, second_ref, route_ref, out_ref = outs
    rows, spare = small_ref.shape
    width = out_ref.shape[1]
    line = line_ref[...]
    out_ref[...] = project_ref[...][:, :width] + line[:, spare:]
    small = small_ref[...] + line[:, :spare]
    small = jnp.concatenate([small, jnp.zeros((rows, LANES - spare), F32)], axis=1)
    small = jnp.concatenate([small, jnp.zeros((LANES - rows, LANES), F32)], axis=0)
    small = jnp.transpose(small)[:, :rows]
    first_ref[...] = small[0:1]
    second_ref[...] = small[1:2]
    route_ref[...] = small[2 : 2 + experts]


def swap(x, axis, bit):
    size = lax.axis_size(axis)
    return lax.ppermute(x, axis, [(i, i ^ bit) for i in range(size)])


def gather_rows(chains, *fills):
    size = lax.axis_size("gx")
    if size != len(RING):
        return [
            lax.all_to_all(
                jnp.broadcast_to(x[None], (size,) + x.shape).reshape(-1, x.shape[1]),
                "gx",
                split_axis=0,
                concat_axis=0,
                tiled=True,
            )
            for x in chains
        ]
    ahead = [(RING[n], RING[(n + 1) % size]) for n in range(size)]
    back = [(b, a) for a, b in ahead]
    out = [[x] for x in chains]
    up, down = list(chains), list(chains)
    for step in range(3):
        for n in range(len(chains)):
            up[n] = lax.ppermute(up[n], "gx", ahead)
            down[n] = lax.ppermute(down[n], "gx", back)
            out[n] += [up[n], down[n]]
        if step < len(fills):
            up[0] = after(up[0], *fills[step])
    return sum([out[n] + [lax.ppermute(up[n], "gx", ahead)] for n in range(len(chains))], [])


def spread(parts, experts):
    if len(parts) == experts:
        return [parts[0]] + [swap(parts[k], "gx", 2 * k) for k in range(1, experts)]
    rows = parts[0].shape[0] // experts
    cut = [parts[0][k * rows : (k + 1) * rows] for k in range(experts)]
    return [jnp.concatenate(spread(cut, experts), axis=0)]


def sum_begin(parts, *fill):
    if len(parts) == 1:
        size = lax.axis_size("gx")
        arrived = lax.all_to_all(parts[0], "gx", split_axis=0, concat_axis=0, tiled=True)
        arrived = arrived.reshape(size, parts[0].shape[0] // size, parts[0].shape[1])
        return [arrived.astype(F32).sum(axis=0)], fill[0]
    pair = add(parts[0], after(swap(parts[1], "gx", 1), *fill)).astype(BF)
    return [pair[0]] + [swap(pair[n], "gx", 2 * n) for n in range(1, pair.shape[0])], pair


def sum_all(x, axis):
    bit = 1
    while bit < lax.axis_size(axis):
        x = x + swap(x, axis, bit)
        bit *= 2
    return x


def after(x, *others):
    return lax.optimization_barrier((x, *others))[0]


def add(a, b):
    return a.astype(F32) + b.astype(F32)


def on_device(
    layer_input,
    w_query,
    w_key,
    w_value,
    w_output,
    attn_gain,
    moe_gain,
    router,
    rel_table,
    w_in,
    w_out,
    expert_ids,
    buckets,
    block_mask,
    grad_out,
):
    n_gx = lax.axis_size("gx")
    n_gy = lax.axis_size("gy")
    seq, model = layer_input.shape
    heads, bucket_count = rel_table.shape
    width = w_query.shape[1]
    shard = w_query.shape[0]
    experts = router.shape[1]
    hidden = w_in.shape[2]
    capacity = 5 * seq // (4 * experts)
    piece = capacity // (2 * n_gy)
    own = experts * 2 * piece
    blocks = seq // BLOCK
    pairs = blocks * (blocks + 1) // 2
    gy = lax.axis_index("gy").astype(jnp.int32).reshape(1)

    gx = lax.axis_index("gx").astype(jnp.int32).reshape(1)
    group = own // experts
    pieces = experts if group % 16 == 0 else 1

    qkv_w, extras = call(
        pack_kernel,
        "pack",
        [struct((shard, 3 * width), BF), struct((shard, LANES + width), BF)],
        [VM] * 7,
        (
            w_query,
            w_key,
            w_value,
            w_output,
            attn_gain.reshape(1, shard),
            moe_gain.reshape(1, shard),
            router.T,
        ),
        cost=1,
    )
    half_model = model // 2
    rear = after(w_out, qkv_w)[0]
    pack = jnp.concatenate([w_in[0], rear[:, :half_model], rear[:, half_model:]], axis=0)
    pack_x = swap(pack, "gy", 2)

    pos_row, pos_col, info = call(
        partial(place_kernel, experts, capacity, group),
        "place",
        [
            struct((1, seq), jnp.int32),
            struct((seq, 1), jnp.int32),
            struct((LANES, seq), BF),
        ],
        [SM, VM],
        (gx, after(expert_ids, qkv_w).reshape(1, seq)),
        cost=2,
    )
    backwards = jnp.concatenate([buckets[::-1], jnp.full((BLOCK,), -1, jnp.int32)])
    brev = jnp.stack(
        [
            backwards[seq - BLOCK * (k + 1) : seq - BLOCK * (k + 1) + 2 * BLOCK]
            for k in range(blocks)
        ]
    )
    table_pad = jnp.concatenate([rel_table, jnp.zeros((8 - heads, bucket_count), F32)], axis=0)
    weights = gather_rows((qkv_w, extras), (pos_row,), (brev, table_pad))
    parts = len(weights) // 2
    pack_y = swap(after(pack, weights[-1]), "gx", 1)
    extras, out_own = call(
        partial(unpack_kernel, parts),
        "unpack",
        [struct((model, LANES), BF), struct((model, width), BF)],
        [SM] + [ANY] * parts,
        (gx, *weights[parts:]),
        scratch=[
            pltpu.VMEM((model, LANES + width), BF),
            pltpu.SemaphoreType.DMA((parts,)),
        ],
        cost=2,
    )
    extras, pack_x = lax.optimization_barrier((extras, pack_x))
    out_core = swap(out_own, "gy", 1)
    out_x = swap(out_own, "gy", 2)
    pack_c = swap(pack, "gy", 1)
    pack_xc = swap(pack_x, "gy", 1)

    h1, qkv, prob, mixed, *sorted_parts, w_full = call(
        partial(attend_kernel, parts),
        "attend",
        [
            struct((seq, model), BF),
            struct((seq, 3 * width), BF),
            struct((heads * pairs, BLOCK, BLOCK), BF),
            struct((seq, width), BF),
        ]
        + [struct((own, width), BF)] * 4
        + [struct((model, 3 * width), BF)],
        [SM, SM, SM] + [VM] * 5 + [ANY] * parts,
        (
            gy,
            gx,
            block_mask,
            layer_input,
            extras,
            table_pad,
            brev,
            pos_row,
            *weights[:parts],
        ),
        scratch=[
            pltpu.VMEM((blocks, BLOCK, BLOCK), F32),
            pltpu.SemaphoreType.DMA((parts,)),
        ],
        cost=60,
    )
    mixed_pieces = [sorted_parts[0]] + [swap(sorted_parts[j], "gy", j) for j in (1, 2, 3)]
    xs, gs, infos = call(
        presort_kernel,
        "presort",
        [struct((own, model), BF), struct((own, model), BF), struct((own, LANES), F32)],
        [SM, VM, VM, VM, VM],
        (gy, after(pos_row, sorted_parts[0]), layer_input, grad_out, info),
        cost=5,
    )
    pack_d = swap(after(pack_x, sorted_parts[0]), "gx", 1)
    out_far = swap(after(out_x, sorted_parts[0]), "gy", 1)
    out_pieces = [out_own, out_core, out_x, out_far]
    mixed_pieces[0], pack_c, pack_xc = lax.optimization_barrier((mixed_pieces[0], pack_c, pack_xc))
    slot_shapes = [struct((own // pieces, model), BF)] * pieces
    routed = call(
        partial(route_kernel, experts, pieces),
        "route",
        slot_shapes
        + slot_shapes
        + [
            struct((own, model), F32),
            struct((own, LANES), F32),
            struct((own, LANES), F32),
        ],
        [VM] * 12,
        (*mixed_pieces, *out_pieces, xs, gs, infos, extras),
        cost=5,
    )
    h2, sg = routed[:pieces], routed[pieces : 2 * pieces]
    residual, router_prob, gate = routed[2 * pieces :]
    pack_yc = swap(after(pack_y, h2[0]), "gy", 1)
    rows_in = spread(h2, experts)
    near = [pack, pack_c, pack_x, pack_xc]
    sg = list(lax.optimization_barrier((*sg, *rows_in))[: len(sg)])
    grads_in = spread(sg, experts)

    def pack_scratch(shards, copies):
        return [
            pltpu.VMEM((shards, 2 * model, hidden), BF),
            pltpu.SemaphoreType.DMA((copies,)),
        ]

    kept_shapes = [struct((4, own, hidden), BF)] * 2
    begun, act_a, slope_a = call(
        partial(expert_kernel, pieces, (1, 1, 1, 1), False),
        "expert_near",
        [struct((own, model), F32)] + kept_shapes,
        [VM] * pieces + [ANY] * 4,
        (*rows_in, *near),
        scratch=pack_scratch(4, 4),
        cost=7,
    )
    pack_d, begun = lax.optimization_barrier((pack_d, begun, *grads_in))[:2]
    far = [pack_y, pack_yc, pack_d, swap(pack_d, "gy", 1)]
    *result, act_b, slope_b = call(
        partial(expert_kernel, pieces, (1, 1, 1, 1), True),
        "expert_far",
        slot_shapes + kept_shapes,
        [VM] * (pieces + 1) + [ANY] * 4,
        (*rows_in, begun, *far),
        scratch=pack_scratch(4, 4),
        cost=7.5,
    )
    result_back = spread(result, experts)
    ours = ((0, 0), (0, 2), (1, 2), (1, 0))
    theirs = ((0, 1), (0, 3), (1, 3), (1, 1))
    (out_sent,) = call(
        partial(outer_sent_kernel, pieces, theirs, True),
        "outer_out_sent",
        [struct((4, hidden, model), BF)],
        [VM] * (pieces + 2),
        (*grads_in, act_a, act_b),
        cost=4.7,
    )
    out_arrived = swap(out_sent, "gy", 1)
    slope_b = after(slope_b, out_sent)
    *grad_rows, grad_pre = call(
        partial(expert_back_kernel, pieces, (1,) * 8),
        "expert_back",
        slot_shapes + [struct((8, own, hidden), BF)],
        [VM] * (pieces + 2) + [ANY] * 8,
        (*grads_in, slope_a, slope_b, *near, *far),
        scratch=pack_scratch(8, 8),
        cost=12,
    )
    rows_back = spread(grad_rows, experts)
    small_rows = -(-(2 + experts) // 8) * 8
    held_args = (*grads_in, act_a, act_b, out_arrived)
    sent_args = (*rows_in, grad_pre)
    deliver_args = (*result_back, residual, xs, gs, infos, router_prob, gate, extras, *h2)
    out_mine, out_by_x, out_far_y, out_by_y, in_sent, d1, grad_hidden, router_part = call(
        partial(
            joined_kernel,
            ((len(held_args), 4), (len(sent_args), 1), (len(deliver_args), 3)),
            (
                partial(outer_held_kernel, pieces, ours, True),
                partial(
                    outer_sent_kernel, pieces, tuple((0, 4 * a + b) for a, b in theirs), False
                ),
                partial(deliver_kernel, experts, pieces),
            ),
        ),
        "fill_rows",
        [
            struct((hidden, model), F32),
            struct((hidden, model), BF),
            struct((hidden, model), BF),
            struct((hidden, model), BF),
            struct((4, model, hidden), BF),
            struct((own, model), BF),
            struct((own, model), F32),
            struct((small_rows, model), F32),
        ],
        [VM] * (len(held_args) + len(sent_args) + len(deliver_args)),
        (*held_args, *sent_args, *deliver_args),
        cost=13,
    )
    out_far_y = swap(out_far_y, "gx", 1)
    in_arrived = swap(in_sent, "gy", 1)
    *mixed_grads, d2, small, project_keep, project_send = call(
        partial(combine_kernel, pieces),
        "combine",
        [struct((own, width), BF)] * 4
        + [
            struct((own, model), BF),
            struct((small_rows, model), F32),
            struct((model, 2 * width), BF),
            struct((model, 2 * width), BF),
        ],
        [VM] * (pieces + 13),
        (
            *rows_back,
            grad_hidden,
            residual,
            gs,
            router_part,
            extras,
            *out_pieces,
            *mixed_pieces,
        ),
        cost=40,
    )
    grads_mixed = [mixed_grads[0]] + [swap(mixed_grads[j], "gy", j) for j in (1, 2, 3)]
    project_other = swap(project_send, "gy", 1)
    in_mine, in_by_x, in_far_y, in_by_y = call(
        partial(outer_held_kernel, pieces, tuple((0, 4 * a + b) for a, b in ours), False),
        "outer_in_held",
        [
            struct((model, hidden), F32),
            struct((model, hidden), BF),
            struct((model, hidden), BF),
            struct((model, hidden), BF),
        ],
        [VM] * (pieces + 2),
        (*rows_in, after(grad_pre, mixed_grads[0]), in_arrived),
        cost=1,
    )
    grads_mixed[1:] = lax.optimization_barrier((*grads_mixed[1:], in_mine))[:-1]
    in_far_y = swap(in_far_y, "gx", 1)
    out_sum_x = add(out_by_x, after(out_far_y, in_mine)).astype(BF)
    projected = add(after(project_keep, in_mine), project_other).astype(BF)
    grads_mixed[0], in_by_x, out_sum_x, projected = lax.optimization_barrier(
        (grads_mixed[0], in_by_x, out_sum_x, projected)
    )
    projected = lax.all_to_all(projected, "gx", split_axis=0, concat_axis=0, tiled=True)
    out_from_x = swap(out_sum_x, "gy", 2)
    out_from_y = swap(out_by_y, "gx", 1)
    d1_x = swap(after(d1, *grads_mixed[1:]), "gy", 2)
    spare = -(-3 * width // LANES) * LANES - 3 * width
    count = 2 if n_gx == len(RING) and heads * bucket_count == shard else 1
    dw_shape = (model, 3 * width + spare) if count == 1 else (4, shard, 3 * width + spare)
    *dw, keep, send, table = call(
        partial(attend_back_kernel, count),
        "attend_back",
        [struct(dw_shape, BF)] * count
        + [
            struct((2, BLOCK, model), BF),
            struct((2, BLOCK, model), BF),
            struct((bucket_count, 8), F32),
        ],
        [SM, SM] + [VM] * 14,
        (
            gy,
            gx,
            *grads_mixed,
            pos_col,
            prob,
            qkv,
            h1,
            layer_input,
            w_full,
            extras,
            brev,
            d2,
            small,
        ),
        scratch=[
            pltpu.VMEM((seq, width), BF),
            pltpu.VMEM((seq, 3 * width), BF),
            pltpu.VMEM((model, 3 * width + spare), BF),
        ],
        cost=60,
    )
    keep, send, in_far_y, out_from_x, out_from_y, d1_x, projected, *dw = lax.optimization_barrier(
        (keep, send, in_far_y, out_from_x, out_from_y, d1_x, projected, *dw)
    )
    half = add(keep, swap(send, "gy", 1)).astype(BF)
    half, d1, d1_x, in_by_x = lax.optimization_barrier((half, d1, d1_x, in_by_x))
    half_far = swap(half, "gy", 2)
    in_sum_x = add(in_by_x, in_far_y).astype(BF)
    in_from_x = swap(in_sum_x, "gy", 2)
    d1s = [after(d1, in_sum_x), swap(d1, "gy", 1), d1_x, swap(d1_x, "gy", 1)]
    (layer_output,) = call(
        unsort_kernel,
        "unsort",
        [struct((seq, model), F32)],
        [SM] + [VM] * 6,
        (gy, pos_col, layer_input, *d1s),
        cost=1,
    )
    projected = projected.reshape(n_gx, shard, 2 * width).astype(F32).sum(axis=0)
    sums, dw_done = sum_begin(dw, layer_output)
    in_from_y = swap(after(in_by_y, dw_done), "gx", 1)
    half_far, *sums = lax.optimization_barrier((half_far, layer_output, *sums))
    sums = sums[1:]
    total = add(half, half_far[::-1]).astype(BF)
    other = swap(total, "gy", 1)
    (grad_input,) = call(
        finish_kernel,
        "finish",
        [struct((seq, model), F32)],
        [SM] + [VM] * 3,
        (gy, total, other, grad_out),
        cost=1,
    )
    summed = sums[0].astype(F32)
    for part in sums[1:]:
        summed = summed + part.astype(F32)
    small = summed[:, 3 * width :]
    small = small + swap(small, "gy", 1)
    line = swap(jnp.concatenate([small, projected[:, width:]], axis=1), "gy", 2)
    line = after(line, grad_input)
    grad_first, grad_second, grad_route, grad_out_proj = call(
        partial(close_kernel, experts),
        "close",
        [
            struct((1, shard), F32),
            struct((1, shard), F32),
            struct((experts, shard), F32),
            struct((shard, width), F32),
        ],
        [VM] * 3,
        (small, line, projected),
        cost=1,
    )
    grad_w_out = add(add(out_mine, out_from_y), out_from_x)
    in_from_x, in_from_y = lax.optimization_barrier((in_from_x, in_from_y, grad_input))[:2]
    grad_w_in = add(add(in_mine, in_from_y), in_from_x)
    if count == 1:
        grad_table = sum_all(table, "gx")[:, :heads].T
    else:
        grad_table = summed[:, -1].reshape(heads, bucket_count)

    return (
        layer_output,
        grad_input,
        summed[:, :width],
        summed[:, width : 2 * width],
        summed[:, 2 * width : 3 * width],
        grad_out_proj,
        grad_first.reshape(shard),
        grad_second.reshape(shard),
        grad_route.T,
        grad_table,
        grad_w_in[None],
        grad_w_out[None],
    )


def solution(mesh):
    return jax.shard_map(
        on_device,
        mesh=mesh,
        in_specs=(
            P("gx", None),
            P("gx", "gy"),
            P("gx", "gy"),
            P("gx", "gy"),
            P("gx", "gy"),
            P("gx"),
            P("gx"),
            P("gx", None),
            P("gy", None),
            P("gx", None, "gy"),
            P("gx", "gy", None),
            P("gx", None),
            P(),
            P(),
            P("gx", None),
        ),
        out_specs=(
            P("gx", None),
            P("gx", None),
            P("gx", "gy"),
            P("gx", "gy"),
            P("gx", "gy"),
            P("gx", "gy"),
            P("gx"),
            P("gx"),
            P("gx", None),
            P("gy", None),
            P("gx", None, "gy"),
            P("gx", "gy", None),
        ),
        check_vma=False,
    )
```

```python
from functools import partial

import jax
import jax.numpy as jnp
from jax import lax
from jax.experimental import pallas as pl
from jax.experimental.pallas import tpu as pltpu
from jax.sharding import PartitionSpec as P

BLOCK = 256
EPS = 1e-06
LANES = 128
BF = jnp.bfloat16
F32 = jnp.float32
HIGH = lax.Precision.HIGHEST
VMEM_BYTES = 56 * 1024 * 1024
PEAK = 1.15e9
RING = (0, 2, 4, 6, 7, 5, 3, 1)
RING_STEPS = (0, -1, 1, -2, 2, -3, 3, -4)


def mm(left, right, precision=None):
    return lax.dot_general(
        left, right, (((1,), (0,)), ((), ())), precision=precision, preferred_element_type=F32
    )


def mm_nt(left, right, precision=None):
    return lax.dot_general(
        left, right, (((1,), (1,)), ((), ())), precision=precision, preferred_element_type=F32
    )


def mm_tn(left, right, precision=None):
    return lax.dot_general(
        left, right, (((0,), (0,)), ((), ())), precision=precision, preferred_element_type=F32
    )


VM = pl.BlockSpec(memory_space=pltpu.VMEM)
SM = pl.BlockSpec(memory_space=pltpu.SMEM)
ANY = pl.BlockSpec(memory_space=pl.ANY)


def call(kernel, name, outs, in_specs, args, scratch=(), cost=1):
    return pl.pallas_call(
        kernel,
        name=name,
        out_shape=list(outs),
        in_specs=in_specs,
        out_specs=[VM] * len(outs),
        scratch_shapes=list(scratch),
        compiler_params=pltpu.CompilerParams(vmem_limit_bytes=VMEM_BYTES),
        cost_estimate=pl.CostEstimate(
            flops=int(cost * PEAK), bytes_accessed=1, transcendentals=0
        ),
    )(*args)


def struct(shape, dtype):
    return jax.ShapeDtypeStruct(shape, dtype)


def one_hot_rows(pos_row, start, count):
    slots = lax.broadcasted_iota(jnp.int32, (count, pos_row.shape[1]), 0) + start
    return jnp.where(slots == pos_row, 1.0, 0.0).astype(BF)


def one_hot_cols(pos_col, start, count):
    slots = lax.broadcasted_iota(jnp.int32, (pos_col.shape[0], count), 1) + start
    return jnp.where(slots == pos_col, 1.0, 0.0).astype(BF)


def pack_kernel(q_ref, k_ref, v_ref, o_ref, attn_ref, moe_ref, router_ref, qkv_ref, extras_ref):
    qkv_ref[...] = jnp.concatenate([q_ref[...], k_ref[...], v_ref[...]], axis=1)
    experts, rows = router_ref.shape
    lines = jnp.concatenate(
        [
            attn_ref[...].astype(F32),
            moe_ref[...].astype(F32),
            router_ref[...].astype(F32),
            jnp.zeros((LANES - 2 - experts, rows), F32),
        ],
        axis=0,
    )
    lines = jnp.concatenate([lines, jnp.zeros((LANES, LANES - rows), F32)], axis=1)
    extras_ref[...] = jnp.concatenate(
        [jnp.transpose(lines)[:rows].astype(BF), o_ref[...]], axis=1
    )


def lane_prefix(values):
    row = lax.broadcasted_iota(jnp.int32, (LANES, LANES), 0)
    column = lax.broadcasted_iota(jnp.int32, (LANES, LANES), 1)
    sooner = jnp.where(row < column, 1.0, 0.0).astype(BF)
    carry = jnp.zeros((values.shape[0], 1), F32)
    out = []
    for start in range(0, values.shape[1], LANES):
        part = values[:, start : start + LANES]
        out.append(mm(part.astype(BF), sooner) + carry)
        carry = carry + jnp.sum(part, axis=1, keepdims=True)
    return jnp.concatenate(out, axis=1), carry


def place_kernel(experts, capacity, group, gx_ref, ids_ref, row_ref, col_ref, info_ref):
    seq = ids_ref.shape[1]
    ids = ids_ref[...]
    deep = -(-experts // 8) * 8
    label = lax.broadcasted_iota(jnp.int32, (deep, seq), 0)
    hot = jnp.where(label == ids, 1.0, 0.0)
    before, total = lane_prefix(hot)
    rank = jnp.sum(before * hot, axis=0, keepdims=True)
    kept = rank < capacity
    filled = jnp.minimum(total, 1.0 * capacity)
    empty = jnp.where(label[:, 0:1] < experts, capacity - filled, 0.0)
    row = lax.broadcasted_iota(jnp.int32, (deep, deep), 0)
    column = lax.broadcasted_iota(jnp.int32, (deep, deep), 1)
    sooner = jnp.where(column < row, 1.0, 0.0)
    begins = mm(sooner, jnp.broadcast_to(empty, (deep, LANES)), HIGH)[:, 0:1]
    lost = jnp.broadcast_to(jnp.where(kept, 0.0, 1.0), (8, seq))
    order = lane_prefix(lost)[0][0:1]
    inside = (order >= begins) & (order < begins + empty)
    spare_expert = jnp.sum(jnp.where(inside, label.astype(F32), 0.0), axis=0, keepdims=True)
    spare_rank = jnp.sum(jnp.where(inside, order - begins + filled, 0.0), axis=0, keepdims=True)
    expert = jnp.where(kept, ids.astype(F32), spare_expert).astype(jnp.int32)
    rank = jnp.where(kept, rank, spare_rank)
    block = jnp.floor((rank + 0.5) * (1.0 / group))
    near = jnp.bitwise_xor(expert, gx_ref[0] // 2).astype(F32)
    position = block * (experts * group) + near * group + rank - block * group
    row_ref[...] = position.astype(jnp.int32)
    tall = jnp.transpose(jnp.broadcast_to(position, (LANES, seq)))
    col_ref[...] = tall[:, 0:1].astype(jnp.int32)
    line = lax.broadcasted_iota(jnp.int32, (LANES, seq), 0)
    info = jnp.where(line == 0, jnp.where(kept, 1.0, 0.0), jnp.where(line - 2 == ids, 1.0, 0.0))
    info_ref[...] = info.astype(BF)


def presort_kernel(gy_ref, pos_ref, x_ref, g_ref, info_ref, xs_ref, gs_ref, infos_ref):
    own = xs_ref.shape[0]
    pick = one_hot_rows(pos_ref[...], gy_ref[0] * own, own)
    xs_ref[...] = mm(pick, x_ref[...]).astype(BF)
    gs_ref[...] = mm(pick, g_ref[...]).astype(BF)
    infos_ref[...] = mm_nt(pick, info_ref[...])


def ring_source(gx, step):
    spot = jnp.where(gx % 2 == 0, gx // 2, 7 - gx // 2)
    spot = jnp.bitwise_and(spot + step, 7)
    return jnp.where(spot < 4, 2 * spot, 2 * (7 - spot) + 1)


def assemble(pieces, gx_ref, target, sems):
    copies = []
    rows = pieces[0].shape[0]
    for n, piece in enumerate(pieces):
        place = target
        if len(pieces) > 1:
            at = pl.multiple_of(ring_source(gx_ref[0], RING_STEPS[n]) * rows, 32)
            place = target.at[pl.ds(at, rows), :]
        copy = pltpu.make_async_copy(piece, place, sems.at[n])
        copy.start()
        copies.append(copy)
    return copies


def unpack_kernel(count, *refs):
    gx_ref, pieces = refs[0], refs[1 : 1 + count]
    extras_ref, out_ref, buf, sems = refs[1 + count :]
    for copy in assemble(pieces, gx_ref, buf, sems):
        copy.wait()
    extras_ref[...] = buf[:, :LANES]
    out_ref[...] = buf[:, LANES:]


def attend_kernel(count, *refs):
    gy_ref, gx_ref, mask_ref, x_ref, extras_ref, table_ref, brev_ref, pos_ref = refs[:8]
    pieces = refs[8 : 8 + count]
    h1_ref, qkv_ref, prob_ref, mixed_ref, s0_ref, s1_ref, s2_ref, s3_ref = refs[
        8 + count : 16 + count
    ]
    w_ref, toep_ref, sems = refs[16 + count :]
    copies = assemble(pieces, gx_ref, w_ref, sems)
    seq = x_ref.shape[0]
    width = mixed_ref.shape[1]
    blocks = seq // BLOCK
    head = 64
    heads = width // head
    gain = jnp.transpose(extras_ref[...].astype(F32))[0:1]
    for copy in copies:
        copy.wait()
    for i in range(blocks):
        rows = pl.ds(i * BLOCK, BLOCK)
        x = x_ref[rows, :].astype(F32)
        scale = lax.rsqrt(jnp.mean(x * x, axis=-1, keepdims=True) + EPS)
        h1 = (x * scale * gain).astype(BF)
        h1_ref[rows, :] = h1
        out = mm(h1, w_ref[...])
        qkv_ref[rows, :] = jnp.concatenate(
            [out[:, :width].astype(BF) * jnp.asarray(0.125, BF), out[:, width:].astype(BF)], axis=1
        )
    bucket_count = table_ref.shape[1]
    biases = []
    for k in range(blocks):
        labels = lax.broadcasted_iota(jnp.int32, (bucket_count, 2 * BLOCK), 0)
        hot = jnp.where(labels == brev_ref[k : k + 1, :], 1.0, 0.0)
        biases.append(mm(table_ref[...], hot, HIGH))
    for h in range(heads):
        for k in range(blocks):
            line = jnp.broadcast_to(biases[k][h : h + 1, :], (BLOCK, 2 * BLOCK))
            skew = pltpu.roll(line, BLOCK + 1, 1, stride=1, stride_axis=0)[:, :BLOCK]
            if k == 0:
                r = lax.broadcasted_iota(jnp.int32, (BLOCK, BLOCK), 0)
                c = lax.broadcasted_iota(jnp.int32, (BLOCK, BLOCK), 1)
                skew = jnp.where(r >= c, skew, -1e30)
            toep_ref[k] = skew
        at = h * head
        for i in range(blocks):
            q = qkv_ref[pl.ds(i * BLOCK, BLOCK), :][:, at : at + head]
            scores = []
            peak = None
            for j in range(i + 1):
                key = qkv_ref[pl.ds(j * BLOCK, BLOCK), :][:, width + at : width + at + head]
                s = mm_nt(q, key) + toep_ref[i - j]
                if j < i:
                    s = s + jnp.where(mask_ref[i, j] == 1, 0.0, -1e30)
                scores.append(s)
                peak = s if peak is None else jnp.maximum(peak, s)
            peak = jnp.max(peak, axis=-1, keepdims=True)
            total = None
            terms = []
            for s in scores:
                e = jnp.exp(s - peak)
                terms.append(e)
                total = e if total is None else total + e
            inverse = 1.0 / jnp.sum(total, axis=-1, keepdims=True)
            acc = None
            for j in range(i + 1):
                prob = (terms[j] * inverse).astype(BF)
                prob_ref[h * (blocks * (blocks + 1) // 2) + i * (i + 1) // 2 + j] = prob
                value = qkv_ref[pl.ds(j * BLOCK, BLOCK), :][
                    :, 2 * width + at : 2 * width + at + head
                ]
                part = mm(prob, value)
                acc = part if acc is None else acc + part
            mixed_ref[pl.ds(i * BLOCK, BLOCK), at : at + head] = acc.astype(BF)
    own = s0_ref.shape[0] * 2 // 3
    mixed = mixed_ref[...]
    for j, ref in enumerate((s0_ref, s1_ref, s2_ref, s3_ref)):
        start = jnp.bitwise_xor(gy_ref[0], j) * own
        ref[...] = fold(mm(one_hot_rows(pos_ref[...], start, own), mixed).astype(BF))


def route_kernel(experts, pieces, *refs):
    mixed_refs, out_refs = refs[:4], refs[4:8]
    xs_ref, gs_ref, infos_ref, extras_ref = refs[8:12]
    h2_refs, sg_refs = refs[12 : 12 + pieces], refs[12 + pieces : 12 + 2 * pieces]
    res_ref, prob_ref, gate_ref = refs[12 + 2 * pieces :]
    attn = None
    for j in range(4):
        part = mm_nt(unfold(mixed_refs[j][...]), out_refs[j][...])
        attn = part if attn is None else attn + part
    extras = extras_ref[...]
    gain = jnp.transpose(extras.astype(F32))[1:2]
    residual = xs_ref[...].astype(F32) + attn
    res_ref[...] = residual
    scale = lax.rsqrt(jnp.mean(residual * residual, axis=-1, keepdims=True) + EPS)
    h2 = (residual * scale * gain).astype(BF)
    logits = mm(h2, extras)
    lane = lax.broadcasted_iota(jnp.int32, logits.shape, 1)
    real = (lane >= 2) & (lane < 2 + experts)
    logits = jnp.where(real, logits, -1e30)
    e = jnp.exp(logits - jnp.max(logits, axis=-1, keepdims=True))
    prob = e / jnp.sum(e, axis=-1, keepdims=True)
    prob_ref[...] = prob
    info = infos_ref[...]
    keep = info[:, 0:1]
    gate = jnp.sum(jnp.where(real, prob * info, 0.0), axis=-1, keepdims=True)
    gate_ref[...] = jnp.broadcast_to(gate, gate_ref.shape)
    h2 = jnp.where(keep > 0.0, h2.astype(F32), 0.0).astype(BF)
    sg = jnp.where(keep > 0.0, gate * gs_ref[...].astype(F32), 0.0).astype(BF)
    split(h2, h2_refs)
    split(sg, sg_refs)


def fold(value):
    rows = value.shape[0]
    edge = value[:, LANES:]
    edge = jnp.concatenate([edge[: rows // 2], edge[rows // 2 :]], axis=1)
    return jnp.concatenate([value[:, :LANES], edge], axis=0)


def unfold(value):
    rows = value.shape[0] * 2 // 3
    edge = value[rows:]
    half = LANES // 2
    edge = jnp.concatenate([edge[:, :half], edge[:, half:]], axis=0)
    return jnp.concatenate([value[:rows], edge], axis=1)


def split(value, refs):
    rows = refs[0].shape[0]
    for n, ref in enumerate(refs):
        ref[...] = value[n * rows : (n + 1) * rows, :]


def joined(refs):
    if len(refs) == 1:
        return refs[0][...]
    return jnp.concatenate([ref[...] for ref in refs], axis=0)


def fetch(packs, win_buf, wout_buf, sems):
    copies = []
    model, hidden = win_buf.shape[0], packs[0].shape[1]
    for j, pack in enumerate(packs):
        place = pl.ds(j * hidden, hidden)
        cuts = (
            (pack.at[pl.ds(0, model), :], win_buf.at[:, place]),
            (pack.at[pl.ds(model, hidden), :], wout_buf.at[place, pl.ds(0, hidden)]),
            (pack.at[pl.ds(model + hidden, hidden), :], wout_buf.at[place, pl.ds(hidden, hidden)]),
        )
        for n, (source, target) in enumerate(cuts):
            copies.append(pltpu.make_async_copy(source, target, sems.at[3 * j + n]))
    return copies


def expert_kernel(pieces, last, *refs):
    row_refs = refs[:pieces]
    refs = refs[pieces:]
    if last:
        before_ref, refs = refs[0], refs[1:]
    packs, refs = refs[:4], refs[4:]
    outs = refs[: pieces if last else 1]
    act_ref, slope_ref, win_buf, wout_buf, sems = refs[len(outs) :]
    pair = 2 * packs[0].shape[1]
    copies = fetch(packs, win_buf, wout_buf, sems)
    for copy in copies:
        copy.start()
    rows = joined(row_refs)
    acc = before_ref[...] if last else None
    for j in range(2):
        place = slice(j * pair, (j + 1) * pair)
        mine = copies[6 * j : 6 * j + 6]
        mine[0].wait()
        mine[3].wait()
        pre = mm(rows, win_buf[:, place])
        cdf = 0.5 * (1.0 + lax.erf(pre * 0.7071067811865476))
        slope = cdf + pre * (0.3989422804014327 * jnp.exp(-0.5 * pre * pre))
        act = (pre * cdf).astype(BF)
        act_ref[:, place] = act
        slope_ref[:, place] = slope.astype(BF)
        for n in (1, 2, 4, 5):
            mine[n].wait()
        part = mm(act, wout_buf[place, :])
        acc = part if acc is None else acc + part
    if last:
        split(acc.astype(BF), outs)
    else:
        outs[0][...] = acc


def expert_back_kernel(pieces, *refs):
    sg_refs, slopes = refs[:pieces], refs[pieces : pieces + 2]
    packs, refs = refs[pieces + 2 : pieces + 10], refs[pieces + 10 :]
    gr_refs = refs[:pieces]
    gp_ref, win_buf, wout_buf, sems = refs[pieces:]
    pair = 2 * packs[0].shape[1]
    copies = fetch(packs, win_buf, wout_buf, sems)
    for j in range(4):
        for n in (1, 2, 4, 5, 0, 3):
            copies[6 * j + n].start()
    sg = joined(sg_refs)
    acc = None
    for j in range(4):
        place = slice(j * pair, (j + 1) * pair)
        near = slice(j % 2 * pair, (j % 2 + 1) * pair)
        mine = copies[6 * j : 6 * j + 6]
        for n in (1, 2, 4, 5):
            mine[n].wait()
        grad = mm_nt(sg, wout_buf[place, :])
        grad = (grad * slopes[j // 2][:, near].astype(F32)).astype(BF)
        gp_ref[:, place] = grad
        mine[0].wait()
        mine[3].wait()
        part = mm_nt(grad, win_buf[:, place])
        acc = part if acc is None else acc + part
    split(acc.astype(BF), gr_refs)


def outer_sent_kernel(pieces, picks, flip, *refs):
    wide = joined(refs[:pieces])
    sources, out_ref = refs[pieces:-1], refs[-1]
    hidden = out_ref.shape[1 if flip else 2]
    for n, (a, b) in enumerate(picks):
        thin = sources[a][:, b * hidden : (b + 1) * hidden]
        out_ref[n] = (mm_tn(thin, wide) if flip else mm_tn(wide, thin)).astype(BF)


def outer_held_kernel(pieces, picks, flip, *refs):
    wide = joined(refs[:pieces])
    sources, arrived_ref = refs[pieces:-5], refs[-5]
    out_refs = refs[-4:]
    hidden = out_refs[0].shape[0 if flip else 1]
    for n, (a, b) in enumerate(picks):
        thin = sources[a][:, b * hidden : (b + 1) * hidden]
        value = mm_tn(thin, wide) if flip else mm_tn(wide, thin)
        value = value + arrived_ref[n].astype(F32)
        out_refs[n][...] = value.astype(out_refs[n].dtype)


def joined_kernel(counts, kernels, *refs):
    sources = refs[: sum(c[0] for c in counts)]
    results = refs[len(sources) :]
    for (taken, given), kernel in zip(counts, kernels):
        kernel(*sources[:taken], *results[:given])
        sources, results = sources[taken:], results[given:]


def deliver_kernel(experts, pieces, *refs):
    er_refs = refs[:pieces]
    res_ref, xs_ref, gs_ref, infos_ref, prob_ref, gate_ref, extras_ref = refs[
        pieces : pieces + 7
    ]
    h2_refs = refs[pieces + 7 : 2 * pieces + 7]
    d1_ref, gh_ref, router_ref = refs[2 * pieces + 7 :]
    prob = prob_ref[...]
    gate = gate_ref[...][:, 0:1]
    lane = lax.broadcasted_iota(jnp.int32, prob.shape, 1)
    real = (lane >= 2) & (lane < 2 + experts)
    hot = jnp.where(real, infos_ref[...], 0.0)
    result = joined(er_refs).astype(F32)
    d1_ref[...] = (res_ref[...] - xs_ref[...].astype(F32) + gate * result).astype(BF)
    grad_gate = jnp.sum(gs_ref[...].astype(F32) * result, axis=-1, keepdims=True)
    grad_logits = (prob * (hot - gate) * grad_gate).astype(BF)
    gh_ref[...] = mm_nt(grad_logits, extras_ref[...])
    router_ref[...] = mm_tn(grad_logits, joined(h2_refs))[: router_ref.shape[0]]


def combine_kernel(pieces, *refs):
    gr_refs = refs[:pieces]
    gh_ref, res_ref, gs_ref, router_ref, extras_ref = refs[pieces : pieces + 5]
    out_refs, mixed_refs = refs[pieces + 5 : pieces + 9], refs[pieces + 9 : pieces + 13]
    gm_refs = refs[pieces + 13 : pieces + 17]
    d2_ref, small_ref, keep_ref, send_ref = refs[pieces + 17 :]
    gain = jnp.transpose(extras_ref[...].astype(F32))[1:2]
    residual = res_ref[...]
    g = gs_ref[...].astype(F32)
    grad_h2 = gh_ref[...] + joined(gr_refs).astype(F32)
    scale = lax.rsqrt(jnp.mean(residual * residual, axis=-1, keepdims=True) + EPS)
    unit = residual * scale
    scaled = grad_h2 * gain
    centre = jnp.mean(scaled * unit, axis=-1, keepdims=True)
    d2 = (scale * (scaled - unit * centre)).astype(BF)
    d2_ref[...] = d2
    grad_attn = (g + d2.astype(F32)).astype(BF)
    for j in range(4):
        gm_refs[j][...] = fold(mm(grad_attn, out_refs[j][...]).astype(BF))
    for target, j in ((keep_ref, 0), (send_ref, 1)):
        mixed = jnp.concatenate(
            [unfold(mixed_refs[j][...]), unfold(mixed_refs[j + 2][...])], axis=1
        )
        target[...] = mm_tn(grad_attn, mixed).astype(BF)
    grad_gain = jnp.sum(grad_h2 * unit, axis=0, keepdims=True)
    small = router_ref[...]
    row = lax.broadcasted_iota(jnp.int32, small.shape, 0)
    small_ref[...] = jnp.where(row == 1, grad_gain, small)


def unskew_sum(block):
    zeros = jnp.zeros((8, BLOCK), F32)
    acc = None
    for i in range(BLOCK // 8):
        piece = jnp.concatenate([block[8 * i : 8 * i + 8, :], zeros], axis=1)
        shift = BLOCK - 8 - 8 * i
        if shift:
            piece = pltpu.roll(piece, shift, 1)
        acc = piece if acc is None else acc + piece
    left = 7 - lax.broadcasted_iota(jnp.int32, acc.shape, 0)
    for bit in range(3):
        moved = pltpu.roll(acc, 1 << bit, 1)
        acc = jnp.where((left >> bit) & 1 == 1, moved, acc)
    return jnp.sum(acc, axis=0, keepdims=True)


def attend_back_kernel(count, *refs):
    gy_ref, gx_ref, g0_ref, g1_ref, g2_ref, g3_ref = refs[:6]
    pos_ref, prob_ref, qkv_ref, h1_ref, x_ref, w_ref, extras_ref, brev_ref = refs[6:14]
    d2_ref, small_ref = refs[14:16]
    dw_refs = refs[16 : 16 + count]
    keep_ref, send_ref, table_ref, gm_ref, grads_ref, dw_buf = refs[16 + count :]
    seq, width = gm_ref.shape
    blocks = seq // BLOCK
    head = 64
    heads = width // head
    own = g0_ref.shape[0] * 2 // 3
    gy = gy_ref[0]
    pieces = [unfold(ref[...]) for ref in (g0_ref, g1_ref, g2_ref, g3_ref)]
    for i in range(blocks):
        rows = pl.ds(i * BLOCK, BLOCK)
        pos = pos_ref[rows, :]
        acc = None
        for j, piece in enumerate(pieces):
            part = mm(one_hot_cols(pos, jnp.bitwise_xor(gy, j) * own, own), piece)
            acc = part if acc is None else acc + part
        gm_ref[rows, :] = acc.astype(BF)
    sums = [[None] * heads for _ in range(blocks)]
    for h in range(heads):
        at = h * head
        diagonals = [None] * blocks
        grad_keys = [None] * blocks
        grad_values = [None] * blocks
        for i in range(blocks):
            rows = pl.ds(i * BLOCK, BLOCK)
            q = qkv_ref[rows, :][:, at : at + head]
            gm = gm_ref[rows, :][:, at : at + head]
            centre = None
            kept = []
            for j in range(i + 1):
                value = qkv_ref[pl.ds(j * BLOCK, BLOCK), :][
                    :, 2 * width + at : 2 * width + at + head
                ]
                low = prob_ref[h * (blocks * (blocks + 1) // 2) + i * (i + 1) // 2 + j]
                prob = low.astype(F32)
                grad_prob = mm_nt(gm, value)
                both = prob * grad_prob
                centre = both if centre is None else centre + both
                kept.append((prob, grad_prob))
                part = mm_tn(low, gm)
                grad_values[j] = part if grad_values[j] is None else grad_values[j] + part
            centre = jnp.sum(centre, axis=-1, keepdims=True)
            acc = None
            for j in range(i + 1):
                prob, grad_prob = kept[j]
                score = prob * (grad_prob - centre)
                diagonals[i - j] = score if diagonals[i - j] is None else diagonals[i - j] + score
                score = score.astype(BF)
                key = qkv_ref[pl.ds(j * BLOCK, BLOCK), :][:, width + at : width + at + head]
                part = mm(score, key)
                acc = part if acc is None else acc + part
                part = mm_tn(score, q)
                grad_keys[j] = part if grad_keys[j] is None else grad_keys[j] + part
            grads_ref[rows, at : at + head] = (acc * 0.125).astype(BF)
        for j in range(blocks):
            rows = pl.ds(j * BLOCK, BLOCK)
            grads_ref[rows, width + at : width + at + head] = grad_keys[j].astype(BF)
            grads_ref[rows, 2 * width + at : 2 * width + at + head] = grad_values[j].astype(BF)
        for k in range(blocks):
            sums[k][h] = unskew_sum(diagonals[k])
    bucket_count = table_ref.shape[0]
    columns = None
    for k in range(blocks):
        labels = lax.broadcasted_iota(jnp.int32, (bucket_count, 2 * BLOCK), 0)
        hot = jnp.where(labels == brev_ref[k : k + 1, :], 1.0, 0.0)
        lines = jnp.concatenate(sums[k] + [jnp.zeros((8 - heads, 2 * BLOCK), F32)], axis=0)
        part = mm_nt(hot, lines, HIGH)
        columns = part if columns is None else columns + part
    table_ref[...] = columns
    gain_total = None
    weights = w_ref[...]
    gain = jnp.transpose(extras_ref[...].astype(F32))[0:1]
    for j in range(4):
        rows = pl.ds(pl.multiple_of(jnp.bitwise_xor(gy, j) * BLOCK, BLOCK), BLOCK)
        part = mm_nt(grads_ref[rows, :], weights)
        x = x_ref[rows, :].astype(F32)
        scale = lax.rsqrt(jnp.mean(x * x, axis=-1, keepdims=True) + EPS)
        unit = x * scale
        line = jnp.sum(part * unit, axis=0, keepdims=True)
        gain_total = line if gain_total is None else gain_total + line
        scaled = part * gain
        centre = jnp.mean(scaled * unit, axis=-1, keepdims=True)
        part = scale * (scaled - unit * centre)
        part = part + mm(one_hot_cols(pos_ref[rows, :], gy * own, own), d2_ref[...])
        target = send_ref if j % 2 else keep_ref
        target[j // 2] = part.astype(BF)
    small = small_ref[...]
    row = lax.broadcasted_iota(jnp.int32, small.shape, 0)
    small = jnp.where(row == 0, gain_total, small)
    spare = dw_buf.shape[1] - 3 * width
    small = jnp.concatenate(
        [small, jnp.zeros((LANES - small.shape[0], small.shape[1]), F32)], axis=0
    )
    small = jnp.transpose(small)[:, :spare]
    grads = mm_tn(h1_ref[...], grads_ref[...])
    dw_buf[...] = jnp.concatenate([grads, small], axis=1).astype(BF)
    if len(dw_refs) == 1:
        dw_refs[0][...] = dw_buf[...]
        return
    rows = dw_refs[0].shape[1]
    column = jnp.concatenate([columns[:, h : h + 1] for h in range(heads)], axis=0)
    column = jnp.broadcast_to(column, (rows, spare)).astype(BF)
    last = lax.broadcasted_iota(jnp.int32, (rows, spare), 1) == spare - 1
    for n in range(8):
        at = pl.multiple_of(jnp.bitwise_xor(gx_ref[0], n) * rows, 32)
        piece = dw_buf[pl.ds(at, rows), :]
        tail = jnp.where(last, column, piece[:, 3 * width :])
        dw_refs[n % 2][n // 2] = jnp.concatenate([piece[:, : 3 * width], tail], axis=1)


def unsort_kernel(gy_ref, pos_ref, x_ref, d0_ref, d1_ref, d2_ref, d3_ref, out_ref):
    own = d0_ref.shape[0]
    gy = gy_ref[0]
    for i in range(x_ref.shape[0] // BLOCK):
        rows = pl.ds(i * BLOCK, BLOCK)
        pos = pos_ref[rows, :]
        acc = x_ref[rows, :].astype(F32)
        for j, ref in enumerate((d0_ref, d1_ref, d2_ref, d3_ref)):
            acc = acc + mm(one_hot_cols(pos, jnp.bitwise_xor(gy, j) * own, own), ref[...])
        out_ref[rows, :] = acc


def finish_kernel(gy_ref, own_ref, other_ref, g_ref, out_ref):
    gy = gy_ref[0]
    for j in range(4):
        rows = pl.ds(pl.multiple_of(jnp.bitwise_xor(gy, j) * BLOCK, BLOCK), BLOCK)
        source = other_ref if j % 2 else own_ref
        out_ref[rows, :] = g_ref[rows, :].astype(F32) + source[j // 2].astype(F32)


def close_kernel(experts, small_ref, line_ref, project_ref, *outs):
    first_ref, second_ref, route_ref, out_ref = outs
    rows, spare = small_ref.shape
    width = out_ref.shape[1]
    line = line_ref[...]
    out_ref[...] = project_ref[...][:, :width] + line[:, spare:]
    small = small_ref[...] + line[:, :spare]
    small = jnp.concatenate([small, jnp.zeros((rows, LANES - spare), F32)], axis=1)
    small = jnp.concatenate([small, jnp.zeros((LANES - rows, LANES), F32)], axis=0)
    small = jnp.transpose(small)[:, :rows]
    first_ref[...] = small[0:1]
    second_ref[...] = small[1:2]
    route_ref[...] = small[2 : 2 + experts]


def swap(x, axis, bit):
    size = lax.axis_size(axis)
    return lax.ppermute(x, axis, [(i, i ^ bit) for i in range(size)])


def gather_rows(chains, *fills):
    size = lax.axis_size("gx")
    if size != len(RING):
        return [
            lax.all_to_all(
                jnp.broadcast_to(x[None], (size,) + x.shape).reshape(-1, x.shape[1]),
                "gx",
                split_axis=0,
                concat_axis=0,
                tiled=True,
            )
            for x in chains
        ]
    ahead = [(RING[n], RING[(n + 1) % size]) for n in range(size)]
    back = [(b, a) for a, b in ahead]
    out = [[x] for x in chains]
    up, down = list(chains), list(chains)
    for step in range(3):
        for n in range(len(chains)):
            up[n] = lax.ppermute(up[n], "gx", ahead)
            down[n] = lax.ppermute(down[n], "gx", back)
            out[n] += [up[n], down[n]]
        if step < len(fills):
            up[0] = after(up[0], *fills[step])
    return sum([out[n] + [lax.ppermute(up[n], "gx", ahead)] for n in range(len(chains))], [])


def spread(parts, experts):
    if len(parts) == experts:
        return [parts[0]] + [swap(parts[k], "gx", 2 * k) for k in range(1, experts)]
    rows = parts[0].shape[0] // experts
    cut = [parts[0][k * rows : (k + 1) * rows] for k in range(experts)]
    return [jnp.concatenate(spread(cut, experts), axis=0)]


def sum_begin(parts, *fill):
    if len(parts) == 1:
        size = lax.axis_size("gx")
        arrived = lax.all_to_all(parts[0], "gx", split_axis=0, concat_axis=0, tiled=True)
        arrived = arrived.reshape(size, parts[0].shape[0] // size, parts[0].shape[1])
        return [arrived.astype(F32).sum(axis=0)], fill[0]
    pair = add(parts[0], after(swap(parts[1], "gx", 1), *fill)).astype(BF)
    return [pair[0]] + [swap(pair[n], "gx", 2 * n) for n in range(1, pair.shape[0])], pair


def sum_all(x, axis):
    bit = 1
    while bit < lax.axis_size(axis):
        x = x + swap(x, axis, bit)
        bit *= 2
    return x


def after(x, *others):
    return lax.optimization_barrier((x, *others))[0]


def add(a, b):
    return a.astype(F32) + b.astype(F32)


def on_device(
    layer_input,
    w_query,
    w_key,
    w_value,
    w_output,
    attn_gain,
    moe_gain,
    router,
    rel_table,
    w_in,
    w_out,
    expert_ids,
    buckets,
    block_mask,
    grad_out,
):
    n_gx = lax.axis_size("gx")
    n_gy = lax.axis_size("gy")
    seq, model = layer_input.shape
    heads, bucket_count = rel_table.shape
    width = w_query.shape[1]
    shard = w_query.shape[0]
    experts = router.shape[1]
    hidden = w_in.shape[2]
    capacity = 5 * seq // (4 * experts)
    piece = capacity // (2 * n_gy)
    own = experts * 2 * piece
    blocks = seq // BLOCK
    pairs = blocks * (blocks + 1) // 2
    gy = lax.axis_index("gy").astype(jnp.int32).reshape(1)

    gx = lax.axis_index("gx").astype(jnp.int32).reshape(1)
    group = own // experts
    pieces = experts if group % 16 == 0 else 1

    qkv_w, extras = call(
        pack_kernel,
        "pack",
        [struct((shard, 3 * width), BF), struct((shard, LANES + width), BF)],
        [VM] * 7,
        (
            w_query,
            w_key,
            w_value,
            w_output,
            attn_gain.reshape(1, shard),
            moe_gain.reshape(1, shard),
            router.T,
        ),
        cost=1,
    )
    half_model = model // 2
    rear = after(w_out, qkv_w)[0]
    pack = jnp.concatenate([w_in[0], rear[:, :half_model], rear[:, half_model:]], axis=0)
    pack_x = swap(pack, "gy", 2)

    pos_row, pos_col, info = call(
        partial(place_kernel, experts, capacity, group),
        "place",
        [
            struct((1, seq), jnp.int32),
            struct((seq, 1), jnp.int32),
            struct((LANES, seq), BF),
        ],
        [SM, VM],
        (gx, after(expert_ids, qkv_w).reshape(1, seq)),
        cost=2,
    )
    backwards = jnp.concatenate([buckets[::-1], jnp.full((BLOCK,), -1, jnp.int32)])
    brev = jnp.stack(
        [
            backwards[seq - BLOCK * (k + 1) : seq - BLOCK * (k + 1) + 2 * BLOCK]
            for k in range(blocks)
        ]
    )
    table_pad = jnp.concatenate([rel_table, jnp.zeros((8 - heads, bucket_count), F32)], axis=0)
    weights = gather_rows((qkv_w, extras), (pos_row,), (brev, table_pad))
    parts = len(weights) // 2
    pack_y = swap(after(pack, weights[-1]), "gx", 1)
    extras, out_own = call(
        partial(unpack_kernel, parts),
        "unpack",
        [struct((model, LANES), BF), struct((model, width), BF)],
        [SM] + [ANY] * parts,
        (gx, *weights[parts:]),
        scratch=[
            pltpu.VMEM((model, LANES + width), BF),
            pltpu.SemaphoreType.DMA((parts,)),
        ],
        cost=2,
    )
    extras, pack_x = lax.optimization_barrier((extras, pack_x))
    out_core = swap(out_own, "gy", 1)
    out_x = swap(out_own, "gy", 2)
    pack_c = swap(pack, "gy", 1)
    pack_xc = swap(pack_x, "gy", 1)

    h1, qkv, prob, mixed, *sorted_parts, w_full = call(
        partial(attend_kernel, parts),
        "attend",
        [
            struct((seq, model), BF),
            struct((seq, 3 * width), BF),
            struct((heads * pairs, BLOCK, BLOCK), BF),
            struct((seq, width), BF),
        ]
        + [struct((own * 3 // 2, LANES), BF)] * 4
        + [struct((model, 3 * width), BF)],
        [SM, SM, SM] + [VM] * 5 + [ANY] * parts,
        (
            gy,
            gx,
            block_mask,
            layer_input,
            extras,
            table_pad,
            brev,
            pos_row,
            *weights[:parts],
        ),
        scratch=[
            pltpu.VMEM((blocks, BLOCK, BLOCK), F32),
            pltpu.SemaphoreType.DMA((parts,)),
        ],
        cost=60,
    )
    mixed_pieces = [sorted_parts[0]] + [swap(sorted_parts[j], "gy", j) for j in (1, 2, 3)]
    xs, gs, infos = call(
        presort_kernel,
        "presort",
        [struct((own, model), BF), struct((own, model), BF), struct((own, LANES), F32)],
        [SM, VM, VM, VM, VM],
        (gy, after(pos_row, sorted_parts[0]), layer_input, grad_out, info),
        cost=5,
    )
    pack_d = swap(after(pack_x, sorted_parts[0]), "gx", 1)
    out_far = swap(after(out_x, sorted_parts[0]), "gy", 1)
    out_pieces = [out_own, out_core, out_x, out_far]
    mixed_pieces[0], pack_c, pack_xc = lax.optimization_barrier((mixed_pieces[0], pack_c, pack_xc))
    slot_shapes = [struct((own // pieces, model), BF)] * pieces
    routed = call(
        partial(route_kernel, experts, pieces),
        "route",
        slot_shapes
        + slot_shapes
        + [
            struct((own, model), F32),
            struct((own, LANES), F32),
            struct((own, LANES), F32),
        ],
        [VM] * 12,
        (*mixed_pieces, *out_pieces, xs, gs, infos, extras),
        cost=5,
    )
    h2, sg = routed[:pieces], routed[pieces : 2 * pieces]
    residual, router_prob, gate = routed[2 * pieces :]
    pack_yc = swap(after(pack_y, h2[0]), "gy", 1)
    rows_in = spread(h2, experts)
    near = [pack, pack_c, pack_x, pack_xc]
    sg = list(lax.optimization_barrier((*sg, *rows_in))[: len(sg)])
    grads_in = spread(sg, experts)

    def pack_scratch(shards):
        return [
            pltpu.VMEM((model, shards * hidden), BF),
            pltpu.VMEM((shards * hidden, model), BF),
            pltpu.SemaphoreType.DMA((3 * shards,)),
        ]

    kept_shapes = [struct((own, 4 * hidden), BF)] * 2
    begun, act_a, slope_a = call(
        partial(expert_kernel, pieces, False),
        "expert_near",
        [struct((own, model), F32)] + kept_shapes,
        [VM] * pieces + [ANY] * 4,
        (*rows_in, *near),
        scratch=pack_scratch(4),
        cost=7,
    )
    pack_d, begun = lax.optimization_barrier((pack_d, begun, *grads_in))[:2]
    far = [pack_y, pack_yc, pack_d, swap(pack_d, "gy", 1)]
    *result, act_b, slope_b = call(
        partial(expert_kernel, pieces, True),
        "expert_far",
        slot_shapes + kept_shapes,
        [VM] * (pieces + 1) + [ANY] * 4,
        (*rows_in, begun, *far),
        scratch=pack_scratch(4),
        cost=7.5,
    )
    result_back = spread(result, experts)
    ours = ((0, 0), (0, 2), (1, 2), (1, 0))
    theirs = ((0, 1), (0, 3), (1, 3), (1, 1))
    (out_sent,) = call(
        partial(outer_sent_kernel, pieces, theirs, True),
        "outer_out_sent",
        [struct((4, hidden, model), BF)],
        [VM] * (pieces + 2),
        (*grads_in, act_a, act_b),
        cost=4.7,
    )
    out_arrived = swap(out_sent, "gy", 1)
    slope_b = after(slope_b, out_sent)
    *grad_rows, grad_pre = call(
        partial(expert_back_kernel, pieces),
        "expert_back",
        slot_shapes + [struct((own, 8 * hidden), BF)],
        [VM] * (pieces + 2) + [ANY] * 8,
        (*grads_in, slope_a, slope_b, *near, *far),
        scratch=pack_scratch(8),
        cost=12,
    )
    rows_back = spread(grad_rows, experts)
    small_rows = -(-(2 + experts) // 8) * 8
    held_args = (*grads_in, act_a, act_b, out_arrived)
    sent_args = (*rows_in, grad_pre)
    deliver_args = (*result_back, residual, xs, gs, infos, router_prob, gate, extras, *h2)
    out_mine, out_by_x, out_far_y, out_by_y, in_sent, d1, grad_hidden, router_part = call(
        partial(
            joined_kernel,
            ((len(held_args), 4), (len(sent_args), 1), (len(deliver_args), 3)),
            (
                partial(outer_held_kernel, pieces, ours, True),
                partial(
                    outer_sent_kernel, pieces, tuple((0, 4 * a + b) for a, b in theirs), False
                ),
                partial(deliver_kernel, experts, pieces),
            ),
        ),
        "fill_rows",
        [
            struct((hidden, model), F32),
            struct((hidden, model), BF),
            struct((hidden, model), BF),
            struct((hidden, model), BF),
            struct((4, model, hidden), BF),
            struct((own, model), BF),
            struct((own, model), F32),
            struct((small_rows, model), F32),
        ],
        [VM] * (len(held_args) + len(sent_args) + len(deliver_args)),
        (*held_args, *sent_args, *deliver_args),
        cost=13,
    )
    out_far_y = swap(out_far_y, "gx", 1)
    in_arrived = swap(in_sent, "gy", 1)
    *mixed_grads, d2, small, project_keep, project_send = call(
        partial(combine_kernel, pieces),
        "combine",
        [struct((own * 3 // 2, LANES), BF)] * 4
        + [
            struct((own, model), BF),
            struct((small_rows, model), F32),
            struct((model, 2 * width), BF),
            struct((model, 2 * width), BF),
        ],
        [VM] * (pieces + 13),
        (
            *rows_back,
            grad_hidden,
            residual,
            gs,
            router_part,
            extras,
            *out_pieces,
            *mixed_pieces,
        ),
        cost=40,
    )
    grads_mixed = [mixed_grads[0]] + [swap(mixed_grads[j], "gy", j) for j in (1, 2, 3)]
    project_other = swap(project_send, "gy", 1)
    in_mine, in_by_x, in_far_y, in_by_y = call(
        partial(outer_held_kernel, pieces, tuple((0, 4 * a + b) for a, b in ours), False),
        "outer_in_held",
        [
            struct((model, hidden), F32),
            struct((model, hidden), BF),
            struct((model, hidden), BF),
            struct((model, hidden), BF),
        ],
        [VM] * (pieces + 2),
        (*rows_in, after(grad_pre, mixed_grads[0]), in_arrived),
        cost=1,
    )
    grads_mixed[1:] = lax.optimization_barrier((*grads_mixed[1:], in_mine))[:-1]
    in_far_y = swap(in_far_y, "gx", 1)
    out_sum_x = add(out_by_x, after(out_far_y, in_mine)).astype(BF)
    projected = add(after(project_keep, in_mine), project_other).astype(BF)
    grads_mixed[0], in_by_x, out_sum_x, projected = lax.optimization_barrier(
        (grads_mixed[0], in_by_x, out_sum_x, projected)
    )
    projected = lax.all_to_all(projected, "gx", split_axis=0, concat_axis=0, tiled=True)
    out_from_x = swap(out_sum_x, "gy", 2)
    out_from_y = swap(out_by_y, "gx", 1)
    d1_x = swap(after(d1, *grads_mixed[1:]), "gy", 2)
    spare = -(-3 * width // LANES) * LANES - 3 * width
    count = 2 if n_gx == len(RING) and heads * bucket_count == shard else 1
    dw_shape = (model, 3 * width + spare) if count == 1 else (4, shard, 3 * width + spare)
    *dw, keep, send, table = call(
        partial(attend_back_kernel, count),
        "attend_back",
        [struct(dw_shape, BF)] * count
        + [
            struct((2, BLOCK, model), BF),
            struct((2, BLOCK, model), BF),
            struct((bucket_count, 8), F32),
        ],
        [SM, SM] + [VM] * 14,
        (
            gy,
            gx,
            *grads_mixed,
            pos_col,
            prob,
            qkv,
            h1,
            layer_input,
            w_full,
            extras,
            brev,
            d2,
            small,
        ),
        scratch=[
            pltpu.VMEM((seq, width), BF),
            pltpu.VMEM((seq, 3 * width), BF),
            pltpu.VMEM((model, 3 * width + spare), BF),
        ],
        cost=60,
    )
    keep, send, in_far_y, out_from_x, out_from_y, d1_x, projected, *dw = lax.optimization_barrier(
        (keep, send, in_far_y, out_from_x, out_from_y, d1_x, projected, *dw)
    )
    half = add(keep, swap(send, "gy", 1)).astype(BF)
    half, d1, d1_x, in_by_x = lax.optimization_barrier((half, d1, d1_x, in_by_x))
    half_far = swap(half, "gy", 2)
    in_sum_x = add(in_by_x, in_far_y).astype(BF)
    in_from_x = swap(in_sum_x, "gy", 2)
    d1s = [after(d1, in_sum_x), swap(d1, "gy", 1), d1_x, swap(d1_x, "gy", 1)]
    (layer_output,) = call(
        unsort_kernel,
        "unsort",
        [struct((seq, model), F32)],
        [SM] + [VM] * 6,
        (gy, pos_col, layer_input, *d1s),
        cost=1,
    )
    projected = projected.reshape(n_gx, shard, 2 * width).astype(F32).sum(axis=0)
    sums, dw_done = sum_begin(dw, layer_output)
    in_from_y = swap(after(in_by_y, dw_done), "gx", 1)
    half_far, *sums = lax.optimization_barrier((half_far, layer_output, *sums))
    sums = sums[1:]
    total = add(half, half_far[::-1]).astype(BF)
    other = swap(total, "gy", 1)
    (grad_input,) = call(
        finish_kernel,
        "finish",
        [struct((seq, model), F32)],
        [SM] + [VM] * 3,
        (gy, total, other, grad_out),
        cost=1,
    )
    summed = sums[0].astype(F32)
    for part in sums[1:]:
        summed = summed + part.astype(F32)
    small = summed[:, 3 * width :]
    small = small + swap(small, "gy", 1)
    line = swap(jnp.concatenate([small, projected[:, width:]], axis=1), "gy", 2)
    line = after(line, grad_input)
    grad_first, grad_second, grad_route, grad_out_proj = call(
        partial(close_kernel, experts),
        "close",
        [
            struct((1, shard), F32),
            struct((1, shard), F32),
            struct((experts, shard), F32),
            struct((shard, width), F32),
        ],
        [VM] * 3,
        (small, line, projected),
        cost=1,
    )
    grad_w_out = add(add(out_mine, out_from_y), out_from_x)
    in_from_x, in_from_y = lax.optimization_barrier((in_from_x, in_from_y, grad_input))[:2]
    grad_w_in = add(add(in_mine, in_from_y), in_from_x)
    if count == 1:
        grad_table = sum_all(table, "gx")[:, :heads].T
    else:
        grad_table = summed[:, -1].reshape(heads, bucket_count)

    return (
        layer_output,
        grad_input,
        summed[:, :width],
        summed[:, width : 2 * width],
        summed[:, 2 * width : 3 * width],
        grad_out_proj,
        grad_first.reshape(shard),
        grad_second.reshape(shard),
        grad_route.T,
        grad_table,
        grad_w_in[None],
        grad_w_out[None],
    )


def solution(mesh):
    return jax.shard_map(
        on_device,
        mesh=mesh,
        in_specs=(
            P("gx", None),
            P("gx", "gy"),
            P("gx", "gy"),
            P("gx", "gy"),
            P("gx", "gy"),
            P("gx"),
            P("gx"),
            P("gx", None),
            P("gy", None),
            P("gx", None, "gy"),
            P("gx", "gy", None),
            P("gx", None),
            P(),
            P(),
            P("gx", None),
        ),
        out_specs=(
            P("gx", None),
            P("gx", None),
            P("gx", "gy"),
            P("gx", "gy"),
            P("gx", "gy"),
            P("gx", "gy"),
            P("gx"),
            P("gx"),
            P("gx", None),
            P("gy", None),
            P("gx", None, "gy"),
            P("gx", "gy", None),
        ),
        check_vma=False,
    )
```

```python
from functools import partial

import jax
import jax.numpy as jnp
from jax import lax
from jax.experimental import pallas as pl
from jax.experimental.pallas import tpu as pltpu
from jax.sharding import PartitionSpec as P

BLOCK = 256
EPS = 1e-06
LANES = 128
BF = jnp.bfloat16
F32 = jnp.float32
HIGH = lax.Precision.HIGHEST
VMEM_BYTES = 28 * 1024 * 1024
VMEM_WHOLE = 56 * 1024 * 1024
ALONE = ("pack", "unpack", "attend", "attend_back")
PEAK = 1.15e9
RING = (0, 2, 4, 6, 7, 5, 3, 1)
RING_STEPS = (0, -1, 1, -2, 2, -3, 3, -4)


def mm(left, right, precision=None):
    return lax.dot_general(
        left, right, (((1,), (0,)), ((), ())), precision=precision, preferred_element_type=F32
    )


def mm_nt(left, right, precision=None):
    return lax.dot_general(
        left, right, (((1,), (1,)), ((), ())), precision=precision, preferred_element_type=F32
    )


def mm_tn(left, right, precision=None):
    return lax.dot_general(
        left, right, (((0,), (0,)), ((), ())), precision=precision, preferred_element_type=F32
    )


VM = pl.BlockSpec(memory_space=pltpu.VMEM)
SM = pl.BlockSpec(memory_space=pltpu.SMEM)
ANY = pl.BlockSpec(memory_space=pl.ANY)


def call(kernel, name, outs, in_specs, args, scratch=(), cost=1):
    return pl.pallas_call(
        kernel,
        name=name,
        out_shape=list(outs),
        in_specs=in_specs,
        out_specs=[VM] * len(outs),
        scratch_shapes=list(scratch),
        compiler_params=pltpu.CompilerParams(
            vmem_limit_bytes=VMEM_WHOLE if name in ALONE else VMEM_BYTES
        ),
        cost_estimate=pl.CostEstimate(
            flops=int(cost * PEAK), bytes_accessed=1, transcendentals=0
        ),
    )(*args)


def struct(shape, dtype):
    return jax.ShapeDtypeStruct(shape, dtype)


def one_hot_rows(pos_row, start, count):
    slots = lax.broadcasted_iota(jnp.int32, (count, pos_row.shape[1]), 0) + start
    return jnp.where(slots == pos_row, 1.0, 0.0).astype(BF)


def one_hot_cols(pos_col, start, count):
    slots = lax.broadcasted_iota(jnp.int32, (pos_col.shape[0], count), 1) + start
    return jnp.where(slots == pos_col, 1.0, 0.0).astype(BF)


def pack_kernel(q_ref, k_ref, v_ref, o_ref, attn_ref, moe_ref, router_ref, qkv_ref, extras_ref):
    qkv_ref[...] = jnp.concatenate([q_ref[...], k_ref[...], v_ref[...]], axis=1)
    experts, rows = router_ref.shape
    lines = jnp.concatenate(
        [
            attn_ref[...].astype(F32),
            moe_ref[...].astype(F32),
            router_ref[...].astype(F32),
            jnp.zeros((LANES - 2 - experts, rows), F32),
        ],
        axis=0,
    )
    lines = jnp.concatenate([lines, jnp.zeros((LANES, LANES - rows), F32)], axis=1)
    extras_ref[...] = jnp.concatenate(
        [jnp.transpose(lines)[:rows].astype(BF), o_ref[...]], axis=1
    )


def lane_prefix(values):
    row = lax.broadcasted_iota(jnp.int32, (LANES, LANES), 0)
    column = lax.broadcasted_iota(jnp.int32, (LANES, LANES), 1)
    sooner = jnp.where(row < column, 1.0, 0.0).astype(BF)
    carry = jnp.zeros((values.shape[0], 1), F32)
    out = []
    for start in range(0, values.shape[1], LANES):
        part = values[:, start : start + LANES]
        out.append(mm(part.astype(BF), sooner) + carry)
        carry = carry + jnp.sum(part, axis=1, keepdims=True)
    return jnp.concatenate(out, axis=1), carry


def place_kernel(experts, capacity, group, gx_ref, ids_ref, row_ref, col_ref, info_ref):
    seq = ids_ref.shape[1]
    ids = ids_ref[...]
    deep = -(-experts // 8) * 8
    label = lax.broadcasted_iota(jnp.int32, (deep, seq), 0)
    hot = jnp.where(label == ids, 1.0, 0.0)
    before, total = lane_prefix(hot)
    rank = jnp.sum(before * hot, axis=0, keepdims=True)
    kept = rank < capacity
    filled = jnp.minimum(total, 1.0 * capacity)
    empty = jnp.where(label[:, 0:1] < experts, capacity - filled, 0.0)
    row = lax.broadcasted_iota(jnp.int32, (deep, deep), 0)
    column = lax.broadcasted_iota(jnp.int32, (deep, deep), 1)
    sooner = jnp.where(column < row, 1.0, 0.0)
    begins = mm(sooner, jnp.broadcast_to(empty, (deep, LANES)), HIGH)[:, 0:1]
    lost = jnp.broadcast_to(jnp.where(kept, 0.0, 1.0), (8, seq))
    order = lane_prefix(lost)[0][0:1]
    inside = (order >= begins) & (order < begins + empty)
    spare_expert = jnp.sum(jnp.where(inside, label.astype(F32), 0.0), axis=0, keepdims=True)
    spare_rank = jnp.sum(jnp.where(inside, order - begins + filled, 0.0), axis=0, keepdims=True)
    expert = jnp.where(kept, ids.astype(F32), spare_expert).astype(jnp.int32)
    rank = jnp.where(kept, rank, spare_rank)
    block = jnp.floor((rank + 0.5) * (1.0 / group))
    near = jnp.bitwise_xor(expert, gx_ref[0] // 2).astype(F32)
    position = block * (experts * group) + near * group + rank - block * group
    row_ref[...] = position.astype(jnp.int32)
    tall = jnp.transpose(jnp.broadcast_to(position, (LANES, seq)))
    col_ref[...] = tall[:, 0:1].astype(jnp.int32)
    line = lax.broadcasted_iota(jnp.int32, (LANES, seq), 0)
    info = jnp.where(line == 0, jnp.where(kept, 1.0, 0.0), jnp.where(line - 2 == ids, 1.0, 0.0))
    info_ref[...] = info.astype(BF)


def presort_kernel(gy_ref, pos_ref, x_ref, g_ref, info_ref, xs_ref, gs_ref, infos_ref):
    own = xs_ref.shape[0]
    pick = one_hot_rows(pos_ref[...], gy_ref[0] * own, own)
    xs_ref[...] = mm(pick, x_ref[...]).astype(BF)
    gs_ref[...] = mm(pick, g_ref[...]).astype(BF)
    infos_ref[...] = mm_nt(pick, info_ref[...])


def ring_source(gx, step):
    spot = jnp.where(gx % 2 == 0, gx // 2, 7 - gx // 2)
    spot = jnp.bitwise_and(spot + step, 7)
    return jnp.where(spot < 4, 2 * spot, 2 * (7 - spot) + 1)


def assemble(pieces, gx_ref, target, sems):
    copies = []
    rows = pieces[0].shape[0]
    for n, piece in enumerate(pieces):
        place = target
        if len(pieces) > 1:
            at = pl.multiple_of(ring_source(gx_ref[0], RING_STEPS[n]) * rows, 32)
            place = target.at[pl.ds(at, rows), :]
        copy = pltpu.make_async_copy(piece, place, sems.at[n])
        copy.start()
        copies.append(copy)
    return copies


def unpack_kernel(count, *refs):
    gx_ref, pieces = refs[0], refs[1 : 1 + count]
    extras_ref, out_ref, buf, sems = refs[1 + count :]
    for copy in assemble(pieces, gx_ref, buf, sems):
        copy.wait()
    extras_ref[...] = buf[:, :LANES]
    out_ref[...] = buf[:, LANES:]


def attend_kernel(count, *refs):
    gy_ref, gx_ref, mask_ref, x_ref, extras_ref, table_ref, brev_ref, pos_ref = refs[:8]
    pieces = refs[8 : 8 + count]
    h1_ref, qkv_ref, prob_ref, mixed_ref, s0_ref, s1_ref, s2_ref, s3_ref = refs[
        8 + count : 16 + count
    ]
    w_ref, toep_ref, sems = refs[16 + count :]
    copies = assemble(pieces, gx_ref, w_ref, sems)
    seq = x_ref.shape[0]
    width = mixed_ref.shape[1]
    blocks = seq // BLOCK
    head = 64
    heads = width // head
    gain = jnp.transpose(extras_ref[...].astype(F32))[0:1]
    for copy in copies:
        copy.wait()
    for i in range(blocks):
        rows = pl.ds(i * BLOCK, BLOCK)
        x = x_ref[rows, :].astype(F32)
        scale = lax.rsqrt(jnp.mean(x * x, axis=-1, keepdims=True) + EPS)
        h1 = (x * scale * gain).astype(BF)
        h1_ref[rows, :] = h1
        out = mm(h1, w_ref[...])
        qkv_ref[rows, :] = jnp.concatenate(
            [out[:, :width].astype(BF) * jnp.asarray(0.125, BF), out[:, width:].astype(BF)], axis=1
        )
    bucket_count = table_ref.shape[1]
    biases = []
    for k in range(blocks):
        labels = lax.broadcasted_iota(jnp.int32, (bucket_count, 2 * BLOCK), 0)
        hot = jnp.where(labels == brev_ref[k : k + 1, :], 1.0, 0.0)
        biases.append(mm(table_ref[...], hot, HIGH))
    for h in range(heads):
        for k in range(blocks):
            line = jnp.broadcast_to(biases[k][h : h + 1, :], (BLOCK, 2 * BLOCK))
            skew = pltpu.roll(line, BLOCK + 1, 1, stride=1, stride_axis=0)[:, :BLOCK]
            if k == 0:
                r = lax.broadcasted_iota(jnp.int32, (BLOCK, BLOCK), 0)
                c = lax.broadcasted_iota(jnp.int32, (BLOCK, BLOCK), 1)
                skew = jnp.where(r >= c, skew, -1e30)
            toep_ref[k] = skew
        at = h * head
        for i in range(blocks):
            q = qkv_ref[pl.ds(i * BLOCK, BLOCK), :][:, at : at + head]
            scores = []
            peak = None
            for j in range(i + 1):
                key = qkv_ref[pl.ds(j * BLOCK, BLOCK), :][:, width + at : width + at + head]
                s = mm_nt(q, key) + toep_ref[i - j]
                if j < i:
                    s = s + jnp.where(mask_ref[i, j] == 1, 0.0, -1e30)
                scores.append(s)
                peak = s if peak is None else jnp.maximum(peak, s)
            peak = jnp.max(peak, axis=-1, keepdims=True)
            total = None
            terms = []
            for s in scores:
                e = jnp.exp(s - peak)
                terms.append(e)
                total = e if total is None else total + e
            inverse = 1.0 / jnp.sum(total, axis=-1, keepdims=True)
            acc = None
            for j in range(i + 1):
                prob = (terms[j] * inverse).astype(BF)
                prob_ref[h * (blocks * (blocks + 1) // 2) + i * (i + 1) // 2 + j] = prob
                value = qkv_ref[pl.ds(j * BLOCK, BLOCK), :][
                    :, 2 * width + at : 2 * width + at + head
                ]
                part = mm(prob, value)
                acc = part if acc is None else acc + part
            mixed_ref[pl.ds(i * BLOCK, BLOCK), at : at + head] = acc.astype(BF)
    own = s0_ref.shape[0] * 2 // 3
    mixed = mixed_ref[...]
    for j, ref in enumerate((s0_ref, s1_ref, s2_ref, s3_ref)):
        start = jnp.bitwise_xor(gy_ref[0], j) * own
        ref[...] = fold(mm(one_hot_rows(pos_ref[...], start, own), mixed).astype(BF))


def route_kernel(experts, pieces, *refs):
    mixed_refs, out_refs = refs[:4], refs[4:8]
    xs_ref, gs_ref, infos_ref, extras_ref = refs[8:12]
    h2_refs, sg_refs = refs[12 : 12 + pieces], refs[12 + pieces : 12 + 2 * pieces]
    res_ref, prob_ref, gate_ref = refs[12 + 2 * pieces :]
    attn = None
    for j in range(4):
        part = mm_nt(unfold(mixed_refs[j][...]), out_refs[j][...])
        attn = part if attn is None else attn + part
    extras = extras_ref[...]
    gain = jnp.transpose(extras.astype(F32))[1:2]
    residual = xs_ref[...].astype(F32) + attn
    res_ref[...] = residual
    scale = lax.rsqrt(jnp.mean(residual * residual, axis=-1, keepdims=True) + EPS)
    h2 = (residual * scale * gain).astype(BF)
    logits = mm(h2, extras)
    lane = lax.broadcasted_iota(jnp.int32, logits.shape, 1)
    real = (lane >= 2) & (lane < 2 + experts)
    logits = jnp.where(real, logits, -1e30)
    e = jnp.exp(logits - jnp.max(logits, axis=-1, keepdims=True))
    prob = e / jnp.sum(e, axis=-1, keepdims=True)
    prob_ref[...] = prob
    info = infos_ref[...]
    keep = info[:, 0:1]
    gate = jnp.sum(jnp.where(real, prob * info, 0.0), axis=-1, keepdims=True)
    gate_ref[...] = jnp.broadcast_to(gate, gate_ref.shape)
    h2 = jnp.where(keep > 0.0, h2.astype(F32), 0.0).astype(BF)
    sg = jnp.where(keep > 0.0, gate * gs_ref[...].astype(F32), 0.0).astype(BF)
    split(h2, h2_refs)
    split(sg, sg_refs)


def fold(value):
    rows = value.shape[0]
    edge = value[:, LANES:]
    edge = jnp.concatenate([edge[: rows // 2], edge[rows // 2 :]], axis=1)
    return jnp.concatenate([value[:, :LANES], edge], axis=0)


def unfold(value):
    rows = value.shape[0] * 2 // 3
    edge = value[rows:]
    half = LANES // 2
    edge = jnp.concatenate([edge[:, :half], edge[:, half:]], axis=0)
    return jnp.concatenate([value[:rows], edge], axis=1)


def split(value, refs):
    rows = refs[0].shape[0]
    for n, ref in enumerate(refs):
        ref[...] = value[n * rows : (n + 1) * rows, :]


def joined(refs):
    if len(refs) == 1:
        return refs[0][...]
    return jnp.concatenate([ref[...] for ref in refs], axis=0)


def fetch(packs, win_buf, wout_buf, sems):
    copies = []
    model, hidden = win_buf.shape[0], packs[0].shape[1]
    for j, pack in enumerate(packs):
        place = pl.ds(j * hidden, hidden)
        cuts = (
            (pack.at[pl.ds(0, model), :], win_buf.at[:, place]),
            (pack.at[pl.ds(model, hidden), :], wout_buf.at[place, pl.ds(0, hidden)]),
            (pack.at[pl.ds(model + hidden, hidden), :], wout_buf.at[place, pl.ds(hidden, hidden)]),
        )
        for n, (source, target) in enumerate(cuts):
            copies.append(pltpu.make_async_copy(source, target, sems.at[3 * j + n]))
    return copies


def expert_kernel(pieces, last, *refs):
    row_refs = refs[:pieces]
    refs = refs[pieces:]
    if last:
        before_ref, refs = refs[0], refs[1:]
    packs, refs = refs[:4], refs[4:]
    outs = refs[: pieces if last else 1]
    act_ref, slope_ref, win_buf, wout_buf, sems = refs[len(outs) :]
    pair = 2 * packs[0].shape[1]
    copies = fetch(packs, win_buf, wout_buf, sems)
    for copy in copies:
        copy.start()
    rows = joined(row_refs)
    acc = before_ref[...] if last else None
    for j in range(2):
        place = slice(j * pair, (j + 1) * pair)
        mine = copies[6 * j : 6 * j + 6]
        mine[0].wait()
        mine[3].wait()
        pre = mm(rows, win_buf[:, place])
        cdf = 0.5 * (1.0 + lax.erf(pre * 0.7071067811865476))
        slope = cdf + pre * (0.3989422804014327 * jnp.exp(-0.5 * pre * pre))
        act = (pre * cdf).astype(BF)
        act_ref[:, place] = act
        slope_ref[:, place] = slope.astype(BF)
        for n in (1, 2, 4, 5):
            mine[n].wait()
        part = mm(act, wout_buf[place, :])
        acc = part if acc is None else acc + part
    if last:
        split(acc.astype(BF), outs)
    else:
        outs[0][...] = acc


def expert_back_kernel(pieces, *refs):
    sg_refs, slopes = refs[:pieces], refs[pieces : pieces + 2]
    packs, refs = refs[pieces + 2 : pieces + 10], refs[pieces + 10 :]
    gr_refs = refs[:pieces]
    gp_ref, win_buf, wout_buf, sems = refs[pieces:]
    pair = 2 * packs[0].shape[1]
    copies = fetch(packs, win_buf, wout_buf, sems)
    for j in range(4):
        for n in (1, 2, 4, 5, 0, 3):
            copies[6 * j + n].start()
    sg = joined(sg_refs)
    acc = None
    for j in range(4):
        place = slice(j * pair, (j + 1) * pair)
        near = slice(j % 2 * pair, (j % 2 + 1) * pair)
        mine = copies[6 * j : 6 * j + 6]
        for n in (1, 2, 4, 5):
            mine[n].wait()
        grad = mm_nt(sg, wout_buf[place, :])
        grad = (grad * slopes[j // 2][:, near].astype(F32)).astype(BF)
        gp_ref[:, place] = grad
        mine[0].wait()
        mine[3].wait()
        part = mm_nt(grad, win_buf[:, place])
        acc = part if acc is None else acc + part
    split(acc.astype(BF), gr_refs)


def outer_sent_kernel(pieces, picks, flip, *refs):
    wide = joined(refs[:pieces])
    sources, out_ref = refs[pieces:-1], refs[-1]
    hidden = out_ref.shape[1 if flip else 2]
    for n, (a, b) in enumerate(picks):
        thin = sources[a][:, b * hidden : (b + 1) * hidden]
        out_ref[n] = (mm_tn(thin, wide) if flip else mm_tn(wide, thin)).astype(BF)


def outer_held_kernel(pieces, picks, flip, *refs):
    wide = joined(refs[:pieces])
    sources, arrived_ref = refs[pieces:-5], refs[-5]
    out_refs = refs[-4:]
    hidden = out_refs[0].shape[0 if flip else 1]
    for n, (a, b) in enumerate(picks):
        thin = sources[a][:, b * hidden : (b + 1) * hidden]
        value = mm_tn(thin, wide) if flip else mm_tn(wide, thin)
        value = value + arrived_ref[n].astype(F32)
        out_refs[n][...] = value.astype(out_refs[n].dtype)


def joined_kernel(counts, kernels, *refs):
    sources = refs[: sum(c[0] for c in counts)]
    results = refs[len(sources) :]
    for (taken, given), kernel in zip(counts, kernels):
        kernel(*sources[:taken], *results[:given])
        sources, results = sources[taken:], results[given:]


def deliver_kernel(experts, pieces, *refs):
    er_refs = refs[:pieces]
    res_ref, xs_ref, gs_ref, infos_ref, prob_ref, gate_ref, extras_ref = refs[
        pieces : pieces + 7
    ]
    h2_refs = refs[pieces + 7 : 2 * pieces + 7]
    d1_ref, gh_ref, router_ref = refs[2 * pieces + 7 :]
    prob = prob_ref[...]
    gate = gate_ref[...][:, 0:1]
    lane = lax.broadcasted_iota(jnp.int32, prob.shape, 1)
    real = (lane >= 2) & (lane < 2 + experts)
    hot = jnp.where(real, infos_ref[...], 0.0)
    result = joined(er_refs).astype(F32)
    d1_ref[...] = (res_ref[...] - xs_ref[...].astype(F32) + gate * result).astype(BF)
    grad_gate = jnp.sum(gs_ref[...].astype(F32) * result, axis=-1, keepdims=True)
    grad_logits = (prob * (hot - gate) * grad_gate).astype(BF)
    gh_ref[...] = mm_nt(grad_logits, extras_ref[...])
    router_ref[...] = mm_tn(grad_logits, joined(h2_refs))[: router_ref.shape[0]]


def combine_kernel(pieces, *refs):
    gr_refs = refs[:pieces]
    gh_ref, res_ref, gs_ref, router_ref, extras_ref = refs[pieces : pieces + 5]
    out_refs, mixed_refs = refs[pieces + 5 : pieces + 9], refs[pieces + 9 : pieces + 13]
    gm_refs = refs[pieces + 13 : pieces + 17]
    d2_ref, small_ref, keep_ref, send_ref = refs[pieces + 17 :]
    gain = jnp.transpose(extras_ref[...].astype(F32))[1:2]
    residual = res_ref[...]
    g = gs_ref[...].astype(F32)
    grad_h2 = gh_ref[...] + joined(gr_refs).astype(F32)
    scale = lax.rsqrt(jnp.mean(residual * residual, axis=-1, keepdims=True) + EPS)
    unit = residual * scale
    scaled = grad_h2 * gain
    centre = jnp.mean(scaled * unit, axis=-1, keepdims=True)
    d2 = (scale * (scaled - unit * centre)).astype(BF)
    d2_ref[...] = d2
    grad_attn = (g + d2.astype(F32)).astype(BF)
    for j in range(4):
        gm_refs[j][...] = fold(mm(grad_attn, out_refs[j][...]).astype(BF))
    for target, j in ((keep_ref, 0), (send_ref, 1)):
        mixed = jnp.concatenate(
            [unfold(mixed_refs[j][...]), unfold(mixed_refs[j + 2][...])], axis=1
        )
        target[...] = mm_tn(grad_attn, mixed).astype(BF)
    grad_gain = jnp.sum(grad_h2 * unit, axis=0, keepdims=True)
    small = router_ref[...]
    row = lax.broadcasted_iota(jnp.int32, small.shape, 0)
    small_ref[...] = jnp.where(row == 1, grad_gain, small)


def unskew_sum(block):
    zeros = jnp.zeros((8, BLOCK), F32)
    acc = None
    for i in range(BLOCK // 8):
        piece = jnp.concatenate([block[8 * i : 8 * i + 8, :], zeros], axis=1)
        shift = BLOCK - 8 - 8 * i
        if shift:
            piece = pltpu.roll(piece, shift, 1)
        acc = piece if acc is None else acc + piece
    left = 7 - lax.broadcasted_iota(jnp.int32, acc.shape, 0)
    for bit in range(3):
        moved = pltpu.roll(acc, 1 << bit, 1)
        acc = jnp.where((left >> bit) & 1 == 1, moved, acc)
    return jnp.sum(acc, axis=0, keepdims=True)


def attend_back_kernel(count, *refs):
    gy_ref, gx_ref, g0_ref, g1_ref, g2_ref, g3_ref = refs[:6]
    pos_ref, prob_ref, qkv_ref, h1_ref, x_ref, w_ref, extras_ref, brev_ref = refs[6:14]
    d2_ref, small_ref = refs[14:16]
    dw_refs = refs[16 : 16 + count]
    keep_ref, send_ref, table_ref, gm_ref, grads_ref, dw_buf = refs[16 + count :]
    seq, width = gm_ref.shape
    blocks = seq // BLOCK
    head = 64
    heads = width // head
    own = g0_ref.shape[0] * 2 // 3
    gy = gy_ref[0]
    pieces = [unfold(ref[...]) for ref in (g0_ref, g1_ref, g2_ref, g3_ref)]
    for i in range(blocks):
        rows = pl.ds(i * BLOCK, BLOCK)
        pos = pos_ref[rows, :]
        acc = None
        for j, piece in enumerate(pieces):
            part = mm(one_hot_cols(pos, jnp.bitwise_xor(gy, j) * own, own), piece)
            acc = part if acc is None else acc + part
        gm_ref[rows, :] = acc.astype(BF)
    sums = [[None] * heads for _ in range(blocks)]
    for h in range(heads):
        at = h * head
        diagonals = [None] * blocks
        grad_keys = [None] * blocks
        grad_values = [None] * blocks
        for i in range(blocks):
            rows = pl.ds(i * BLOCK, BLOCK)
            q = qkv_ref[rows, :][:, at : at + head]
            gm = gm_ref[rows, :][:, at : at + head]
            centre = None
            kept = []
            for j in range(i + 1):
                value = qkv_ref[pl.ds(j * BLOCK, BLOCK), :][
                    :, 2 * width + at : 2 * width + at + head
                ]
                low = prob_ref[h * (blocks * (blocks + 1) // 2) + i * (i + 1) // 2 + j]
                prob = low.astype(F32)
                grad_prob = mm_nt(gm, value)
                both = prob * grad_prob
                centre = both if centre is None else centre + both
                kept.append((prob, grad_prob))
                part = mm_tn(low, gm)
                grad_values[j] = part if grad_values[j] is None else grad_values[j] + part
            centre = jnp.sum(centre, axis=-1, keepdims=True)
            acc = None
            for j in range(i + 1):
                prob, grad_prob = kept[j]
                score = prob * (grad_prob - centre)
                diagonals[i - j] = score if diagonals[i - j] is None else diagonals[i - j] + score
                score = score.astype(BF)
                key = qkv_ref[pl.ds(j * BLOCK, BLOCK), :][:, width + at : width + at + head]
                part = mm(score, key)
                acc = part if acc is None else acc + part
                part = mm_tn(score, q)
                grad_keys[j] = part if grad_keys[j] is None else grad_keys[j] + part
            grads_ref[rows, at : at + head] = (acc * 0.125).astype(BF)
        for j in range(blocks):
            rows = pl.ds(j * BLOCK, BLOCK)
            grads_ref[rows, width + at : width + at + head] = grad_keys[j].astype(BF)
            grads_ref[rows, 2 * width + at : 2 * width + at + head] = grad_values[j].astype(BF)
        for k in range(blocks):
            sums[k][h] = unskew_sum(diagonals[k])
    bucket_count = table_ref.shape[0]
    columns = None
    for k in range(blocks):
        labels = lax.broadcasted_iota(jnp.int32, (bucket_count, 2 * BLOCK), 0)
        hot = jnp.where(labels == brev_ref[k : k + 1, :], 1.0, 0.0)
        lines = jnp.concatenate(sums[k] + [jnp.zeros((8 - heads, 2 * BLOCK), F32)], axis=0)
        part = mm_nt(hot, lines, HIGH)
        columns = part if columns is None else columns + part
    table_ref[...] = columns
    gain_total = None
    weights = w_ref[...]
    gain = jnp.transpose(extras_ref[...].astype(F32))[0:1]
    for j in range(4):
        rows = pl.ds(pl.multiple_of(jnp.bitwise_xor(gy, j) * BLOCK, BLOCK), BLOCK)
        part = mm_nt(grads_ref[rows, :], weights)
        x = x_ref[rows, :].astype(F32)
        scale = lax.rsqrt(jnp.mean(x * x, axis=-1, keepdims=True) + EPS)
        unit = x * scale
        line = jnp.sum(part * unit, axis=0, keepdims=True)
        gain_total = line if gain_total is None else gain_total + line
        scaled = part * gain
        centre = jnp.mean(scaled * unit, axis=-1, keepdims=True)
        part = scale * (scaled - unit * centre)
        part = part + mm(one_hot_cols(pos_ref[rows, :], gy * own, own), d2_ref[...])
        target = send_ref if j % 2 else keep_ref
        target[j // 2] = part.astype(BF)
    small = small_ref[...]
    row = lax.broadcasted_iota(jnp.int32, small.shape, 0)
    small = jnp.where(row == 0, gain_total, small)
    spare = dw_buf.shape[1] - 3 * width
    small = jnp.concatenate(
        [small, jnp.zeros((LANES - small.shape[0], small.shape[1]), F32)], axis=0
    )
    small = jnp.transpose(small)[:, :spare]
    grads = mm_tn(h1_ref[...], grads_ref[...])
    dw_buf[...] = jnp.concatenate([grads, small], axis=1).astype(BF)
    if len(dw_refs) == 1:
        dw_refs[0][...] = dw_buf[...]
        return
    rows = dw_refs[0].shape[1]
    column = jnp.concatenate([columns[:, h : h + 1] for h in range(heads)], axis=0)
    column = jnp.broadcast_to(column, (rows, spare)).astype(BF)
    last = lax.broadcasted_iota(jnp.int32, (rows, spare), 1) == spare - 1
    for n in range(8):
        at = pl.multiple_of(jnp.bitwise_xor(gx_ref[0], n) * rows, 32)
        piece = dw_buf[pl.ds(at, rows), :]
        tail = jnp.where(last, column, piece[:, 3 * width :])
        dw_refs[n % 2][n // 2] = jnp.concatenate([piece[:, : 3 * width], tail], axis=1)


def unsort_kernel(gy_ref, pos_ref, x_ref, d0_ref, d1_ref, d2_ref, d3_ref, out_ref):
    own = d0_ref.shape[0]
    gy = gy_ref[0]
    for i in range(x_ref.shape[0] // BLOCK):
        rows = pl.ds(i * BLOCK, BLOCK)
        pos = pos_ref[rows, :]
        acc = x_ref[rows, :].astype(F32)
        for j, ref in enumerate((d0_ref, d1_ref, d2_ref, d3_ref)):
            acc = acc + mm(one_hot_cols(pos, jnp.bitwise_xor(gy, j) * own, own), ref[...])
        out_ref[rows, :] = acc


def finish_kernel(gy_ref, own_ref, other_ref, g_ref, out_ref):
    gy = gy_ref[0]
    for j in range(4):
        rows = pl.ds(pl.multiple_of(jnp.bitwise_xor(gy, j) * BLOCK, BLOCK), BLOCK)
        source = other_ref if j % 2 else own_ref
        out_ref[rows, :] = g_ref[rows, :].astype(F32) + source[j // 2].astype(F32)


def close_kernel(experts, small_ref, line_ref, project_ref, *outs):
    first_ref, second_ref, route_ref, out_ref = outs
    rows, spare = small_ref.shape
    width = out_ref.shape[1]
    line = line_ref[...]
    out_ref[...] = project_ref[...][:, :width] + line[:, spare:]
    small = small_ref[...] + line[:, :spare]
    small = jnp.concatenate([small, jnp.zeros((rows, LANES - spare), F32)], axis=1)
    small = jnp.concatenate([small, jnp.zeros((LANES - rows, LANES), F32)], axis=0)
    small = jnp.transpose(small)[:, :rows]
    first_ref[...] = small[0:1]
    second_ref[...] = small[1:2]
    route_ref[...] = small[2 : 2 + experts]


def swap(x, axis, bit):
    size = lax.axis_size(axis)
    return lax.ppermute(x, axis, [(i, i ^ bit) for i in range(size)])


def gather_rows(chains, *fills):
    size = lax.axis_size("gx")
    if size != len(RING):
        return [
            lax.all_to_all(
                jnp.broadcast_to(x[None], (size,) + x.shape).reshape(-1, x.shape[1]),
                "gx",
                split_axis=0,
                concat_axis=0,
                tiled=True,
            )
            for x in chains
        ]
    ahead = [(RING[n], RING[(n + 1) % size]) for n in range(size)]
    back = [(b, a) for a, b in ahead]
    out = [[x] for x in chains]
    up, down = list(chains), list(chains)
    for step in range(3):
        for n in range(len(chains)):
            up[n] = lax.ppermute(up[n], "gx", ahead)
            down[n] = lax.ppermute(down[n], "gx", back)
            out[n] += [up[n], down[n]]
        if step < len(fills):
            up[0] = after(up[0], *fills[step])
    return sum([out[n] + [lax.ppermute(up[n], "gx", ahead)] for n in range(len(chains))], [])


def spread(parts, experts):
    if len(parts) == experts:
        return [parts[0]] + [swap(parts[k], "gx", 2 * k) for k in range(1, experts)]
    rows = parts[0].shape[0] // experts
    cut = [parts[0][k * rows : (k + 1) * rows] for k in range(experts)]
    return [jnp.concatenate(spread(cut, experts), axis=0)]


def sum_begin(parts, *fill):
    if len(parts) == 1:
        size = lax.axis_size("gx")
        arrived = lax.all_to_all(parts[0], "gx", split_axis=0, concat_axis=0, tiled=True)
        arrived = arrived.reshape(size, parts[0].shape[0] // size, parts[0].shape[1])
        return [arrived.astype(F32).sum(axis=0)], fill[0]
    pair = add(parts[0], after(swap(parts[1], "gx", 1), *fill)).astype(BF)
    return [pair[0]] + [swap(pair[n], "gx", 2 * n) for n in range(1, pair.shape[0])], pair


def sum_all(x, axis):
    bit = 1
    while bit < lax.axis_size(axis):
        x = x + swap(x, axis, bit)
        bit *= 2
    return x


def after(x, *others):
    return lax.optimization_barrier((x, *others))[0]


def add(a, b):
    return a.astype(F32) + b.astype(F32)


def on_device(
    layer_input,
    w_query,
    w_key,
    w_value,
    w_output,
    attn_gain,
    moe_gain,
    router,
    rel_table,
    w_in,
    w_out,
    expert_ids,
    buckets,
    block_mask,
    grad_out,
):
    n_gx = lax.axis_size("gx")
    n_gy = lax.axis_size("gy")
    seq, model = layer_input.shape
    heads, bucket_count = rel_table.shape
    width = w_query.shape[1]
    shard = w_query.shape[0]
    experts = router.shape[1]
    hidden = w_in.shape[2]
    capacity = 5 * seq // (4 * experts)
    piece = capacity // (2 * n_gy)
    own = experts * 2 * piece
    blocks = seq // BLOCK
    pairs = blocks * (blocks + 1) // 2
    gy = lax.axis_index("gy").astype(jnp.int32).reshape(1)

    gx = lax.axis_index("gx").astype(jnp.int32).reshape(1)
    group = own // experts
    pieces = experts if group % 16 == 0 else 1

    qkv_w, extras = call(
        pack_kernel,
        "pack",
        [struct((shard, 3 * width), BF), struct((shard, LANES + width), BF)],
        [VM] * 7,
        (
            w_query,
            w_key,
            w_value,
            w_output,
            attn_gain.reshape(1, shard),
            moe_gain.reshape(1, shard),
            router.T,
        ),
        cost=1,
    )
    half_model = model // 2
    rear = after(w_out, qkv_w)[0]
    pack = jnp.concatenate([w_in[0], rear[:, :half_model], rear[:, half_model:]], axis=0)
    pack_x = swap(pack, "gy", 2)

    pos_row, pos_col, info = call(
        partial(place_kernel, experts, capacity, group),
        "place",
        [
            struct((1, seq), jnp.int32),
            struct((seq, 1), jnp.int32),
            struct((LANES, seq), BF),
        ],
        [SM, VM],
        (gx, after(expert_ids, qkv_w).reshape(1, seq)),
        cost=2,
    )
    backwards = jnp.concatenate([buckets[::-1], jnp.full((BLOCK,), -1, jnp.int32)])
    brev = jnp.stack(
        [
            backwards[seq - BLOCK * (k + 1) : seq - BLOCK * (k + 1) + 2 * BLOCK]
            for k in range(blocks)
        ]
    )
    table_pad = jnp.concatenate([rel_table, jnp.zeros((8 - heads, bucket_count), F32)], axis=0)
    weights = gather_rows((qkv_w, extras), (pos_row,), (brev, table_pad))
    parts = len(weights) // 2
    pack_y = swap(after(pack, weights[-1]), "gx", 1)
    extras, out_own = call(
        partial(unpack_kernel, parts),
        "unpack",
        [struct((model, LANES), BF), struct((model, width), BF)],
        [SM] + [ANY] * parts,
        (gx, *weights[parts:]),
        scratch=[
            pltpu.VMEM((model, LANES + width), BF),
            pltpu.SemaphoreType.DMA((parts,)),
        ],
        cost=2,
    )
    extras, pack_x = lax.optimization_barrier((extras, pack_x))
    out_core = swap(out_own, "gy", 1)
    out_x = swap(out_own, "gy", 2)
    pack_c = swap(pack, "gy", 1)
    pack_xc = swap(pack_x, "gy", 1)

    h1, qkv, prob, mixed, *sorted_parts, w_full = call(
        partial(attend_kernel, parts),
        "attend",
        [
            struct((seq, model), BF),
            struct((seq, 3 * width), BF),
            struct((heads * pairs, BLOCK, BLOCK), BF),
            struct((seq, width), BF),
        ]
        + [struct((own * 3 // 2, LANES), BF)] * 4
        + [struct((model, 3 * width), BF)],
        [SM, SM, SM] + [VM] * 5 + [ANY] * parts,
        (
            gy,
            gx,
            block_mask,
            layer_input,
            extras,
            table_pad,
            brev,
            pos_row,
            *weights[:parts],
        ),
        scratch=[
            pltpu.VMEM((blocks, BLOCK, BLOCK), F32),
            pltpu.SemaphoreType.DMA((parts,)),
        ],
        cost=60,
    )
    mixed_pieces = [sorted_parts[0]] + [swap(sorted_parts[j], "gy", j) for j in (1, 2, 3)]
    xs, gs, infos = call(
        presort_kernel,
        "presort",
        [struct((own, model), BF), struct((own, model), BF), struct((own, LANES), F32)],
        [SM, VM, VM, VM, VM],
        (gy, after(pos_row, sorted_parts[0]), layer_input, grad_out, info),
        cost=5,
    )
    pack_d = swap(after(pack_x, sorted_parts[0]), "gx", 1)
    out_far = swap(after(out_x, sorted_parts[0]), "gy", 1)
    out_pieces = [out_own, out_core, out_x, out_far]
    mixed_pieces[0], pack_c, pack_xc = lax.optimization_barrier((mixed_pieces[0], pack_c, pack_xc))
    slot_shapes = [struct((own // pieces, model), BF)] * pieces
    routed = call(
        partial(route_kernel, experts, pieces),
        "route",
        slot_shapes
        + slot_shapes
        + [
            struct((own, model), F32),
            struct((own, LANES), F32),
            struct((own, LANES), F32),
        ],
        [VM] * 12,
        (*mixed_pieces, *out_pieces, xs, gs, infos, extras),
        cost=5,
    )
    h2, sg = routed[:pieces], routed[pieces : 2 * pieces]
    residual, router_prob, gate = routed[2 * pieces :]
    pack_yc = swap(after(pack_y, h2[0]), "gy", 1)
    rows_in = spread(h2, experts)
    near = [pack, pack_c, pack_x, pack_xc]
    sg = list(lax.optimization_barrier((*sg, *rows_in))[: len(sg)])
    grads_in = spread(sg, experts)

    def pack_scratch(shards):
        return [
            pltpu.VMEM((model, shards * hidden), BF),
            pltpu.VMEM((shards * hidden, model), BF),
            pltpu.SemaphoreType.DMA((3 * shards,)),
        ]

    kept_shapes = [struct((own, 4 * hidden), BF)] * 2
    begun, act_a, slope_a = call(
        partial(expert_kernel, pieces, False),
        "expert_near",
        [struct((own, model), F32)] + kept_shapes,
        [VM] * pieces + [ANY] * 4,
        (*rows_in, *near),
        scratch=pack_scratch(4),
        cost=7,
    )
    pack_d, begun = lax.optimization_barrier((pack_d, begun, *grads_in))[:2]
    far = [pack_y, pack_yc, pack_d, swap(pack_d, "gy", 1)]
    *result, act_b, slope_b = call(
        partial(expert_kernel, pieces, True),
        "expert_far",
        slot_shapes + kept_shapes,
        [VM] * (pieces + 1) + [ANY] * 4,
        (*rows_in, begun, *far),
        scratch=pack_scratch(4),
        cost=7.5,
    )
    result_back = spread(result, experts)
    ours = ((0, 0), (0, 2), (1, 2), (1, 0))
    theirs = ((0, 1), (0, 3), (1, 3), (1, 1))
    (out_sent,) = call(
        partial(outer_sent_kernel, pieces, theirs, True),
        "outer_out_sent",
        [struct((4, hidden, model), BF)],
        [VM] * (pieces + 2),
        (*grads_in, act_a, act_b),
        cost=4.7,
    )
    out_arrived = swap(out_sent, "gy", 1)
    slope_b = after(slope_b, out_sent)
    *grad_rows, grad_pre = call(
        partial(expert_back_kernel, pieces),
        "expert_back",
        slot_shapes + [struct((own, 8 * hidden), BF)],
        [VM] * (pieces + 2) + [ANY] * 8,
        (*grads_in, slope_a, slope_b, *near, *far),
        scratch=pack_scratch(8),
        cost=12,
    )
    rows_back = spread(grad_rows, experts)
    small_rows = -(-(2 + experts) // 8) * 8
    held_args = (*grads_in, act_a, act_b, out_arrived)
    sent_args = (*rows_in, grad_pre)
    deliver_args = (*result_back, residual, xs, gs, infos, router_prob, gate, extras, *h2)
    out_mine, out_by_x, out_far_y, out_by_y, in_sent, d1, grad_hidden, router_part = call(
        partial(
            joined_kernel,
            ((len(held_args), 4), (len(sent_args), 1), (len(deliver_args), 3)),
            (
                partial(outer_held_kernel, pieces, ours, True),
                partial(
                    outer_sent_kernel, pieces, tuple((0, 4 * a + b) for a, b in theirs), False
                ),
                partial(deliver_kernel, experts, pieces),
            ),
        ),
        "fill_rows",
        [
            struct((hidden, model), F32),
            struct((hidden, model), BF),
            struct((hidden, model), BF),
            struct((hidden, model), BF),
            struct((4, model, hidden), BF),
            struct((own, model), BF),
            struct((own, model), F32),
            struct((small_rows, model), F32),
        ],
        [VM] * (len(held_args) + len(sent_args) + len(deliver_args)),
        (*held_args, *sent_args, *deliver_args),
        cost=13,
    )
    out_far_y = swap(out_far_y, "gx", 1)
    in_arrived = swap(in_sent, "gy", 1)
    *mixed_grads, d2, small, project_keep, project_send = call(
        partial(combine_kernel, pieces),
        "combine",
        [struct((own * 3 // 2, LANES), BF)] * 4
        + [
            struct((own, model), BF),
            struct((small_rows, model), F32),
            struct((model, 2 * width), BF),
            struct((model, 2 * width), BF),
        ],
        [VM] * (pieces + 13),
        (
            *rows_back,
            grad_hidden,
            residual,
            gs,
            router_part,
            extras,
            *out_pieces,
            *mixed_pieces,
        ),
        cost=40,
    )
    grads_mixed = [mixed_grads[0]] + [swap(mixed_grads[j], "gy", j) for j in (1, 2, 3)]
    project_other = swap(project_send, "gy", 1)
    in_mine, in_by_x, in_far_y, in_by_y = call(
        partial(outer_held_kernel, pieces, tuple((0, 4 * a + b) for a, b in ours), False),
        "outer_in_held",
        [
            struct((model, hidden), F32),
            struct((model, hidden), BF),
            struct((model, hidden), BF),
            struct((model, hidden), BF),
        ],
        [VM] * (pieces + 2),
        (*rows_in, after(grad_pre, mixed_grads[0]), in_arrived),
        cost=1,
    )
    grads_mixed[1:] = lax.optimization_barrier((*grads_mixed[1:], in_mine))[:-1]
    in_far_y = swap(in_far_y, "gx", 1)
    out_sum_x = add(out_by_x, after(out_far_y, in_mine)).astype(BF)
    projected = add(after(project_keep, in_mine), project_other).astype(BF)
    grads_mixed[0], in_by_x, out_sum_x, projected = lax.optimization_barrier(
        (grads_mixed[0], in_by_x, out_sum_x, projected)
    )
    projected = lax.all_to_all(projected, "gx", split_axis=0, concat_axis=0, tiled=True)
    out_from_x = swap(out_sum_x, "gy", 2)
    out_from_y = swap(out_by_y, "gx", 1)
    d1_x = swap(after(d1, *grads_mixed[1:]), "gy", 2)
    spare = -(-3 * width // LANES) * LANES - 3 * width
    count = 2 if n_gx == len(RING) and heads * bucket_count == shard else 1
    dw_shape = (model, 3 * width + spare) if count == 1 else (4, shard, 3 * width + spare)
    *dw, keep, send, table = call(
        partial(attend_back_kernel, count),
        "attend_back",
        [struct(dw_shape, BF)] * count
        + [
            struct((2, BLOCK, model), BF),
            struct((2, BLOCK, model), BF),
            struct((bucket_count, 8), F32),
        ],
        [SM, SM] + [VM] * 14,
        (
            gy,
            gx,
            *grads_mixed,
            pos_col,
            prob,
            qkv,
            h1,
            layer_input,
            w_full,
            extras,
            brev,
            d2,
            small,
        ),
        scratch=[
            pltpu.VMEM((seq, width), BF),
            pltpu.VMEM((seq, 3 * width), BF),
            pltpu.VMEM((model, 3 * width + spare), BF),
        ],
        cost=60,
    )
    keep, send, in_far_y, out_from_x, out_from_y, d1_x, projected, *dw = lax.optimization_barrier(
        (keep, send, in_far_y, out_from_x, out_from_y, d1_x, projected, *dw)
    )
    half = add(keep, swap(send, "gy", 1)).astype(BF)
    half, d1, d1_x, in_by_x = lax.optimization_barrier((half, d1, d1_x, in_by_x))
    half_far = swap(half, "gy", 2)
    in_sum_x = add(in_by_x, in_far_y).astype(BF)
    in_from_x = swap(in_sum_x, "gy", 2)
    d1s = [after(d1, in_sum_x), swap(d1, "gy", 1), d1_x, swap(d1_x, "gy", 1)]
    (layer_output,) = call(
        unsort_kernel,
        "unsort",
        [struct((seq, model), F32)],
        [SM] + [VM] * 6,
        (gy, pos_col, layer_input, *d1s),
        cost=1,
    )
    projected = projected.reshape(n_gx, shard, 2 * width).astype(F32).sum(axis=0)
    sums, dw_done = sum_begin(dw, layer_output)
    in_from_y = swap(after(in_by_y, dw_done), "gx", 1)
    half_far, *sums = lax.optimization_barrier((half_far, layer_output, *sums))
    sums = sums[1:]
    total = add(half, half_far[::-1]).astype(BF)
    other = swap(total, "gy", 1)
    (grad_input,) = call(
        finish_kernel,
        "finish",
        [struct((seq, model), F32)],
        [SM] + [VM] * 3,
        (gy, total, other, grad_out),
        cost=1,
    )
    summed = sums[0].astype(F32)
    for part in sums[1:]:
        summed = summed + part.astype(F32)
    small = summed[:, 3 * width :]
    small = small + swap(small, "gy", 1)
    line = swap(jnp.concatenate([small, projected[:, width:]], axis=1), "gy", 2)
    line = after(line, grad_input)
    grad_first, grad_second, grad_route, grad_out_proj = call(
        partial(close_kernel, experts),
        "close",
        [
            struct((1, shard), F32),
            struct((1, shard), F32),
            struct((experts, shard), F32),
            struct((shard, width), F32),
        ],
        [VM] * 3,
        (small, line, projected),
        cost=1,
    )
    grad_w_out = add(add(out_mine, out_from_y), out_from_x)
    in_from_x, in_from_y = lax.optimization_barrier((in_from_x, in_from_y, grad_input))[:2]
    grad_w_in = add(add(in_mine, in_from_y), in_from_x)
    if count == 1:
        grad_table = sum_all(table, "gx")[:, :heads].T
    else:
        grad_table = summed[:, -1].reshape(heads, bucket_count)

    return (
        layer_output,
        grad_input,
        summed[:, :width],
        summed[:, width : 2 * width],
        summed[:, 2 * width : 3 * width],
        grad_out_proj,
        grad_first.reshape(shard),
        grad_second.reshape(shard),
        grad_route.T,
        grad_table,
        grad_w_in[None],
        grad_w_out[None],
    )


def solution(mesh):
    return jax.shard_map(
        on_device,
        mesh=mesh,
        in_specs=(
            P("gx", None),
            P("gx", "gy"),
            P("gx", "gy"),
            P("gx", "gy"),
            P("gx", "gy"),
            P("gx"),
            P("gx"),
            P("gx", None),
            P("gy", None),
            P("gx", None, "gy"),
            P("gx", "gy", None),
            P("gx", None),
            P(),
            P(),
            P("gx", None),
        ),
        out_specs=(
            P("gx", None),
            P("gx", None),
            P("gx", "gy"),
            P("gx", "gy"),
            P("gx", "gy"),
            P("gx", "gy"),
            P("gx"),
            P("gx"),
            P("gx", None),
            P("gy", None),
            P("gx", None, "gy"),
            P("gx", "gy", None),
        ),
        check_vma=False,
    )
```

```python
from functools import partial

import jax
import jax.numpy as jnp
from jax import lax
from jax.experimental import pallas as pl
from jax.experimental.pallas import tpu as pltpu
from jax.sharding import PartitionSpec as P

BLOCK = 256
EPS = 1e-06
LANES = 128
BF = jnp.bfloat16
F32 = jnp.float32
HIGH = lax.Precision.HIGHEST
VMEM_BYTES = 28 * 1024 * 1024
VMEM_WHOLE = 56 * 1024 * 1024
ALONE = ("pack", "unpack", "attend", "attend_back")
PEAK = 1.15e9
RING = (0, 2, 4, 6, 7, 5, 3, 1)
RING_STEPS = (0, -1, 1, -2, 2, -3, 3, -4)


def mm(left, right, precision=None):
    return lax.dot_general(
        left, right, (((1,), (0,)), ((), ())), precision=precision, preferred_element_type=F32
    )


def mm_nt(left, right, precision=None):
    return lax.dot_general(
        left, right, (((1,), (1,)), ((), ())), precision=precision, preferred_element_type=F32
    )


def mm_tn(left, right, precision=None):
    return lax.dot_general(
        left, right, (((0,), (0,)), ((), ())), precision=precision, preferred_element_type=F32
    )


VM = pl.BlockSpec(memory_space=pltpu.VMEM)
SM = pl.BlockSpec(memory_space=pltpu.SMEM)
ANY = pl.BlockSpec(memory_space=pl.ANY)


def call(kernel, name, outs, in_specs, args, scratch=(), cost=1, out_specs=None):
    return pl.pallas_call(
        kernel,
        name=name,
        out_shape=list(outs),
        in_specs=in_specs,
        out_specs=[VM] * len(outs) if out_specs is None else out_specs,
        scratch_shapes=list(scratch),
        compiler_params=pltpu.CompilerParams(
            vmem_limit_bytes=VMEM_WHOLE if name in ALONE else VMEM_BYTES
        ),
        cost_estimate=pl.CostEstimate(
            flops=int(cost * PEAK), bytes_accessed=1, transcendentals=0
        ),
    )(*args)


def struct(shape, dtype):
    return jax.ShapeDtypeStruct(shape, dtype)


def one_hot_rows(pos_row, start, count):
    slots = lax.broadcasted_iota(jnp.int32, (count, pos_row.shape[1]), 0) + start
    return jnp.where(slots == pos_row, 1.0, 0.0).astype(BF)


def one_hot_cols(pos_col, start, count):
    slots = lax.broadcasted_iota(jnp.int32, (pos_col.shape[0], count), 1) + start
    return jnp.where(slots == pos_col, 1.0, 0.0).astype(BF)


def pack_kernel(q_ref, k_ref, v_ref, o_ref, attn_ref, moe_ref, router_ref, qkv_ref, extras_ref):
    qkv_ref[...] = jnp.concatenate([q_ref[...], k_ref[...], v_ref[...]], axis=1)
    experts, rows = router_ref.shape
    lines = jnp.concatenate(
        [
            attn_ref[...].astype(F32),
            moe_ref[...].astype(F32),
            router_ref[...].astype(F32),
            jnp.zeros((LANES - 2 - experts, rows), F32),
        ],
        axis=0,
    )
    lines = jnp.concatenate([lines, jnp.zeros((LANES, LANES - rows), F32)], axis=1)
    extras_ref[...] = jnp.concatenate(
        [jnp.transpose(lines)[:rows].astype(BF), o_ref[...]], axis=1
    )


def lane_prefix(values):
    row = lax.broadcasted_iota(jnp.int32, (LANES, LANES), 0)
    column = lax.broadcasted_iota(jnp.int32, (LANES, LANES), 1)
    sooner = jnp.where(row < column, 1.0, 0.0).astype(BF)
    carry = jnp.zeros((values.shape[0], 1), F32)
    out = []
    for start in range(0, values.shape[1], LANES):
        part = values[:, start : start + LANES]
        out.append(mm(part.astype(BF), sooner) + carry)
        carry = carry + jnp.sum(part, axis=1, keepdims=True)
    return jnp.concatenate(out, axis=1), carry


def place_kernel(experts, capacity, group, gx_ref, ids_ref, row_ref, col_ref, info_ref):
    seq = ids_ref.shape[1]
    ids = ids_ref[...]
    deep = -(-experts // 8) * 8
    label = lax.broadcasted_iota(jnp.int32, (deep, seq), 0)
    hot = jnp.where(label == ids, 1.0, 0.0)
    before, total = lane_prefix(hot)
    rank = jnp.sum(before * hot, axis=0, keepdims=True)
    kept = rank < capacity
    filled = jnp.minimum(total, 1.0 * capacity)
    empty = jnp.where(label[:, 0:1] < experts, capacity - filled, 0.0)
    row = lax.broadcasted_iota(jnp.int32, (deep, deep), 0)
    column = lax.broadcasted_iota(jnp.int32, (deep, deep), 1)
    sooner = jnp.where(column < row, 1.0, 0.0)
    begins = mm(sooner, jnp.broadcast_to(empty, (deep, LANES)), HIGH)[:, 0:1]
    lost = jnp.broadcast_to(jnp.where(kept, 0.0, 1.0), (8, seq))
    order = lane_prefix(lost)[0][0:1]
    inside = (order >= begins) & (order < begins + empty)
    spare_expert = jnp.sum(jnp.where(inside, label.astype(F32), 0.0), axis=0, keepdims=True)
    spare_rank = jnp.sum(jnp.where(inside, order - begins + filled, 0.0), axis=0, keepdims=True)
    expert = jnp.where(kept, ids.astype(F32), spare_expert).astype(jnp.int32)
    rank = jnp.where(kept, rank, spare_rank)
    block = jnp.floor((rank + 0.5) * (1.0 / group))
    near = jnp.bitwise_xor(expert, gx_ref[0] // 2).astype(F32)
    position = block * (experts * group) + near * group + rank - block * group
    row_ref[...] = position.astype(jnp.int32)
    tall = jnp.transpose(jnp.broadcast_to(position, (LANES, seq)))
    col_ref[...] = tall[:, 0:1].astype(jnp.int32)
    line = lax.broadcasted_iota(jnp.int32, (LANES, seq), 0)
    info = jnp.where(line == 0, jnp.where(kept, 1.0, 0.0), jnp.where(line - 2 == ids, 1.0, 0.0))
    info_ref[...] = info.astype(BF)


def presort_kernel(gy_ref, pos_ref, x_ref, g_ref, info_ref, xs_ref, gs_ref, infos_ref):
    own = xs_ref.shape[0]
    pick = one_hot_rows(pos_ref[...], gy_ref[0] * own, own)
    xs_ref[...] = mm(pick, x_ref[...]).astype(BF)
    gs_ref[...] = mm(pick, g_ref[...]).astype(BF)
    infos_ref[...] = mm_nt(pick, info_ref[...])


def ring_source(gx, step):
    spot = jnp.where(gx % 2 == 0, gx // 2, 7 - gx // 2)
    spot = jnp.bitwise_and(spot + step, 7)
    return jnp.where(spot < 4, 2 * spot, 2 * (7 - spot) + 1)


def assemble(pieces, gx_ref, target, sems):
    copies = []
    rows = pieces[0].shape[0]
    for n, piece in enumerate(pieces):
        place = target
        if len(pieces) > 1:
            at = pl.multiple_of(ring_source(gx_ref[0], RING_STEPS[n]) * rows, 32)
            place = target.at[pl.ds(at, rows), :]
        copy = pltpu.make_async_copy(piece, place, sems.at[n])
        copy.start()
        copies.append(copy)
    return copies


def unpack_kernel(count, *refs):
    gx_ref, pieces = refs[0], refs[1 : 1 + count]
    extras_ref, out_ref, buf, sems = refs[1 + count :]
    for copy in assemble(pieces, gx_ref, buf, sems):
        copy.wait()
    extras_ref[...] = buf[:, :LANES]
    out_ref[...] = buf[:, LANES:]


def attend_kernel(count, *refs):
    gy_ref, gx_ref, mask_ref, x_ref, extras_ref, table_ref, brev_ref, pos_ref = refs[:8]
    pieces = refs[8 : 8 + count]
    h1_out, qkv_out, prob_out, mixed_ref, s0_ref, s1_ref, s2_ref, s3_ref, w_out = refs[
        8 + count : 17 + count
    ]
    toep_ref, h1_ref, qkv_ref, prob_ref, w_ref, sems, out_sems = refs[17 + count :]
    copies = assemble(pieces, gx_ref, w_ref, sems)
    seq = x_ref.shape[0]
    width = mixed_ref.shape[1]
    blocks = seq // BLOCK
    head = 64
    heads = width // head
    gain = jnp.transpose(extras_ref[...].astype(F32))[0:1]
    for copy in copies:
        copy.wait()
    leaving = [pltpu.make_async_copy(w_ref, w_out, out_sems.at[0])]
    leaving[0].start()
    for i in range(blocks):
        rows = pl.ds(i * BLOCK, BLOCK)
        x = x_ref[rows, :].astype(F32)
        scale = lax.rsqrt(jnp.mean(x * x, axis=-1, keepdims=True) + EPS)
        h1 = (x * scale * gain).astype(BF)
        h1_ref[rows, :] = h1
        out = mm(h1, w_ref[...])
        qkv_ref[rows, :] = jnp.concatenate(
            [out[:, :width].astype(BF) * jnp.asarray(0.125, BF), out[:, width:].astype(BF)], axis=1
        )
    for source, target in ((h1_ref, h1_out), (qkv_ref, qkv_out)):
        leaving.append(pltpu.make_async_copy(source, target, out_sems.at[len(leaving)]))
        leaving[-1].start()
    bucket_count = table_ref.shape[1]
    biases = []
    for k in range(blocks):
        labels = lax.broadcasted_iota(jnp.int32, (bucket_count, 2 * BLOCK), 0)
        hot = jnp.where(labels == brev_ref[k : k + 1, :], 1.0, 0.0)
        biases.append(mm(table_ref[...], hot, HIGH))
    for h in range(heads):
        for k in range(blocks):
            line = jnp.broadcast_to(biases[k][h : h + 1, :], (BLOCK, 2 * BLOCK))
            skew = pltpu.roll(line, BLOCK + 1, 1, stride=1, stride_axis=0)[:, :BLOCK]
            if k == 0:
                r = lax.broadcasted_iota(jnp.int32, (BLOCK, BLOCK), 0)
                c = lax.broadcasted_iota(jnp.int32, (BLOCK, BLOCK), 1)
                skew = jnp.where(r >= c, skew, -1e30)
            toep_ref[k] = skew
        at = h * head
        for i in range(blocks):
            q = qkv_ref[pl.ds(i * BLOCK, BLOCK), :][:, at : at + head]
            scores = []
            peak = None
            for j in range(i + 1):
                key = qkv_ref[pl.ds(j * BLOCK, BLOCK), :][:, width + at : width + at + head]
                s = mm_nt(q, key) + toep_ref[i - j]
                if j < i:
                    s = s + jnp.where(mask_ref[i, j] == 1, 0.0, -1e30)
                scores.append(s)
                peak = s if peak is None else jnp.maximum(peak, s)
            peak = jnp.max(peak, axis=-1, keepdims=True)
            total = None
            terms = []
            for s in scores:
                e = jnp.exp(s - peak)
                terms.append(e)
                total = e if total is None else total + e
            inverse = 1.0 / jnp.sum(total, axis=-1, keepdims=True)
            acc = None
            for j in range(i + 1):
                prob = (terms[j] * inverse).astype(BF)
                prob_ref[h * (blocks * (blocks + 1) // 2) + i * (i + 1) // 2 + j] = prob
                value = qkv_ref[pl.ds(j * BLOCK, BLOCK), :][
                    :, 2 * width + at : 2 * width + at + head
                ]
                part = mm(prob, value)
                acc = part if acc is None else acc + part
            mixed_ref[pl.ds(i * BLOCK, BLOCK), at : at + head] = acc.astype(BF)
        done = pl.ds(h * (blocks * (blocks + 1) // 2), blocks * (blocks + 1) // 2)
        leaving.append(
            pltpu.make_async_copy(
                prob_ref.at[done], prob_out.at[done], out_sems.at[len(leaving)]
            )
        )
        leaving[-1].start()
    own = s0_ref.shape[0] * 2 // 3
    mixed = mixed_ref[...]
    for j, ref in enumerate((s0_ref, s1_ref, s2_ref, s3_ref)):
        start = jnp.bitwise_xor(gy_ref[0], j) * own
        ref[...] = fold(mm(one_hot_rows(pos_ref[...], start, own), mixed).astype(BF))
    for copy in leaving:
        copy.wait()


def route_kernel(experts, pieces, *refs):
    mixed_refs, out_refs = refs[:4], refs[4:8]
    xs_ref, gs_ref, infos_ref, extras_ref = refs[8:12]
    h2_refs, sg_refs = refs[12 : 12 + pieces], refs[12 + pieces : 12 + 2 * pieces]
    res_ref, prob_ref, gate_ref = refs[12 + 2 * pieces :]
    attn = None
    for j in range(4):
        part = mm_nt(unfold(mixed_refs[j][...]), out_refs[j][...])
        attn = part if attn is None else attn + part
    extras = extras_ref[...]
    gain = jnp.transpose(extras.astype(F32))[1:2]
    residual = xs_ref[...].astype(F32) + attn
    res_ref[...] = residual
    scale = lax.rsqrt(jnp.mean(residual * residual, axis=-1, keepdims=True) + EPS)
    h2 = (residual * scale * gain).astype(BF)
    logits = mm(h2, extras)
    lane = lax.broadcasted_iota(jnp.int32, logits.shape, 1)
    real = (lane >= 2) & (lane < 2 + experts)
    logits = jnp.where(real, logits, -1e30)
    e = jnp.exp(logits - jnp.max(logits, axis=-1, keepdims=True))
    prob = e / jnp.sum(e, axis=-1, keepdims=True)
    prob_ref[...] = prob
    info = infos_ref[...]
    keep = info[:, 0:1]
    gate = jnp.sum(jnp.where(real, prob * info, 0.0), axis=-1, keepdims=True)
    gate_ref[...] = jnp.broadcast_to(gate, gate_ref.shape)
    h2 = jnp.where(keep > 0.0, h2.astype(F32), 0.0).astype(BF)
    sg = jnp.where(keep > 0.0, gate * gs_ref[...].astype(F32), 0.0).astype(BF)
    split(h2, h2_refs)
    split(sg, sg_refs)


def fold(value):
    rows = value.shape[0]
    edge = value[:, LANES:]
    edge = jnp.concatenate([edge[: rows // 2], edge[rows // 2 :]], axis=1)
    return jnp.concatenate([value[:, :LANES], edge], axis=0)


def unfold(value):
    rows = value.shape[0] * 2 // 3
    edge = value[rows:]
    half = LANES // 2
    edge = jnp.concatenate([edge[:, :half], edge[:, half:]], axis=0)
    return jnp.concatenate([value[:rows], edge], axis=1)


def split(value, refs):
    rows = refs[0].shape[0]
    for n, ref in enumerate(refs):
        ref[...] = value[n * rows : (n + 1) * rows, :]


def joined(refs):
    if len(refs) == 1:
        return refs[0][...]
    return jnp.concatenate([ref[...] for ref in refs], axis=0)


def fetch(packs, win_buf, wout_buf, sems):
    copies = []
    model, hidden = win_buf.shape[0], packs[0].shape[1]
    for j, pack in enumerate(packs):
        place = pl.ds(j * hidden, hidden)
        cuts = (
            (pack.at[pl.ds(0, model), :], win_buf.at[:, place]),
            (pack.at[pl.ds(model, hidden), :], wout_buf.at[place, pl.ds(0, hidden)]),
            (pack.at[pl.ds(model + hidden, hidden), :], wout_buf.at[place, pl.ds(hidden, hidden)]),
        )
        for n, (source, target) in enumerate(cuts):
            copies.append(pltpu.make_async_copy(source, target, sems.at[3 * j + n]))
    return copies


def expert_kernel(pieces, last, *refs):
    row_refs = refs[:pieces]
    refs = refs[pieces:]
    if last:
        before_ref, refs = refs[0], refs[1:]
    packs, refs = refs[:4], refs[4:]
    outs = refs[: pieces if last else 1]
    act_ref, slope_ref, win_buf, wout_buf, sems = refs[len(outs) :]
    pair = 2 * packs[0].shape[1]
    copies = fetch(packs, win_buf, wout_buf, sems)
    for copy in copies:
        copy.start()
    rows = joined(row_refs)
    acc = before_ref[...] if last else None
    for j in range(2):
        place = slice(j * pair, (j + 1) * pair)
        mine = copies[6 * j : 6 * j + 6]
        mine[0].wait()
        mine[3].wait()
        pre = mm(rows, win_buf[:, place])
        cdf = 0.5 * (1.0 + lax.erf(pre * 0.7071067811865476))
        slope = cdf + pre * (0.3989422804014327 * jnp.exp(-0.5 * pre * pre))
        act = (pre * cdf).astype(BF)
        act_ref[:, place] = act
        slope_ref[:, place] = slope.astype(BF)
        for n in (1, 2, 4, 5):
            mine[n].wait()
        part = mm(act, wout_buf[place, :])
        acc = part if acc is None else acc + part
    if last:
        split(acc.astype(BF), outs)
    else:
        outs[0][...] = acc


def expert_back_kernel(pieces, *refs):
    sg_refs, slopes = refs[:pieces], refs[pieces : pieces + 2]
    packs, refs = refs[pieces + 2 : pieces + 10], refs[pieces + 10 :]
    gr_refs = refs[:pieces]
    gp_ref, win_buf, wout_buf, sems = refs[pieces:]
    pair = 2 * packs[0].shape[1]
    copies = fetch(packs, win_buf, wout_buf, sems)
    for j in range(4):
        for n in (1, 2, 4, 5, 0, 3):
            copies[6 * j + n].start()
    sg = joined(sg_refs)
    acc = None
    for j in range(4):
        place = slice(j * pair, (j + 1) * pair)
        near = slice(j % 2 * pair, (j % 2 + 1) * pair)
        mine = copies[6 * j : 6 * j + 6]
        for n in (1, 2, 4, 5):
            mine[n].wait()
        grad = mm_nt(sg, wout_buf[place, :])
        grad = (grad * slopes[j // 2][:, near].astype(F32)).astype(BF)
        gp_ref[:, place] = grad
        mine[0].wait()
        mine[3].wait()
        part = mm_nt(grad, win_buf[:, place])
        acc = part if acc is None else acc + part
    split(acc.astype(BF), gr_refs)


def outer_sent_kernel(pieces, picks, flip, *refs):
    wide = joined(refs[:pieces])
    sources, out_ref = refs[pieces:-1], refs[-1]
    hidden = out_ref.shape[1 if flip else 2]
    for n, (a, b) in enumerate(picks):
        thin = sources[a][:, b * hidden : (b + 1) * hidden]
        out_ref[n] = (mm_tn(thin, wide) if flip else mm_tn(wide, thin)).astype(BF)


def outer_held_kernel(pieces, picks, flip, *refs):
    wide = joined(refs[:pieces])
    sources, arrived_ref = refs[pieces:-5], refs[-5]
    out_refs = refs[-4:]
    hidden = out_refs[0].shape[0 if flip else 1]
    for n, (a, b) in enumerate(picks):
        thin = sources[a][:, b * hidden : (b + 1) * hidden]
        value = mm_tn(thin, wide) if flip else mm_tn(wide, thin)
        value = value + arrived_ref[n].astype(F32)
        out_refs[n][...] = value.astype(out_refs[n].dtype)


def joined_kernel(counts, kernels, *refs):
    sources = refs[: sum(c[0] for c in counts)]
    results = refs[len(sources) :]
    for (taken, given), kernel in zip(counts, kernels):
        kernel(*sources[:taken], *results[:given])
        sources, results = sources[taken:], results[given:]


def deliver_kernel(experts, pieces, *refs):
    er_refs = refs[:pieces]
    res_ref, xs_ref, gs_ref, infos_ref, prob_ref, gate_ref, extras_ref = refs[
        pieces : pieces + 7
    ]
    h2_refs = refs[pieces + 7 : 2 * pieces + 7]
    d1_ref, gh_ref, router_ref = refs[2 * pieces + 7 :]
    prob = prob_ref[...]
    gate = gate_ref[...][:, 0:1]
    lane = lax.broadcasted_iota(jnp.int32, prob.shape, 1)
    real = (lane >= 2) & (lane < 2 + experts)
    hot = jnp.where(real, infos_ref[...], 0.0)
    result = joined(er_refs).astype(F32)
    d1_ref[...] = (res_ref[...] - xs_ref[...].astype(F32) + gate * result).astype(BF)
    grad_gate = jnp.sum(gs_ref[...].astype(F32) * result, axis=-1, keepdims=True)
    grad_logits = (prob * (hot - gate) * grad_gate).astype(BF)
    gh_ref[...] = mm_nt(grad_logits, extras_ref[...])
    router_ref[...] = mm_tn(grad_logits, joined(h2_refs))[: router_ref.shape[0]]


def combine_kernel(pieces, *refs):
    gr_refs = refs[:pieces]
    gh_ref, res_ref, gs_ref, router_ref, extras_ref = refs[pieces : pieces + 5]
    out_refs, mixed_refs = refs[pieces + 5 : pieces + 9], refs[pieces + 9 : pieces + 13]
    gm_refs = refs[pieces + 13 : pieces + 17]
    d2_ref, small_ref, keep_ref, send_ref = refs[pieces + 17 :]
    gain = jnp.transpose(extras_ref[...].astype(F32))[1:2]
    residual = res_ref[...]
    g = gs_ref[...].astype(F32)
    grad_h2 = gh_ref[...] + joined(gr_refs).astype(F32)
    scale = lax.rsqrt(jnp.mean(residual * residual, axis=-1, keepdims=True) + EPS)
    unit = residual * scale
    scaled = grad_h2 * gain
    centre = jnp.mean(scaled * unit, axis=-1, keepdims=True)
    d2 = (scale * (scaled - unit * centre)).astype(BF)
    d2_ref[...] = d2
    grad_attn = (g + d2.astype(F32)).astype(BF)
    for j in range(4):
        gm_refs[j][...] = fold(mm(grad_attn, out_refs[j][...]).astype(BF))
    for target, j in ((keep_ref, 0), (send_ref, 1)):
        mixed = jnp.concatenate(
            [unfold(mixed_refs[j][...]), unfold(mixed_refs[j + 2][...])], axis=1
        )
        target[...] = mm_tn(grad_attn, mixed).astype(BF)
    grad_gain = jnp.sum(grad_h2 * unit, axis=0, keepdims=True)
    small = router_ref[...]
    row = lax.broadcasted_iota(jnp.int32, small.shape, 0)
    small_ref[...] = jnp.where(row == 1, grad_gain, small)


def unskew_sum(block):
    zeros = jnp.zeros((8, BLOCK), F32)
    acc = None
    for i in range(BLOCK // 8):
        piece = jnp.concatenate([block[8 * i : 8 * i + 8, :], zeros], axis=1)
        shift = BLOCK - 8 - 8 * i
        if shift:
            piece = pltpu.roll(piece, shift, 1)
        acc = piece if acc is None else acc + piece
    left = 7 - lax.broadcasted_iota(jnp.int32, acc.shape, 0)
    for bit in range(3):
        moved = pltpu.roll(acc, 1 << bit, 1)
        acc = jnp.where((left >> bit) & 1 == 1, moved, acc)
    return jnp.sum(acc, axis=0, keepdims=True)


def attend_back_kernel(count, *refs):
    gy_ref, gx_ref, g0_ref, g1_ref, g2_ref, g3_ref = refs[:6]
    pos_ref, prob_in, qkv_ref, h1_in, x_in, w_in, extras_ref, brev_ref = refs[6:14]
    d2_ref, small_ref = refs[14:16]
    dw_refs = refs[16 : 16 + count]
    keep_ref, send_ref, table_ref, gm_ref, grads_ref, dw_buf = refs[16 + count : 22 + count]
    prob_ref, h1_ref, x_ref, w_ref, sems = refs[22 + count :]
    seq, width = gm_ref.shape
    blocks = seq // BLOCK
    head = 64
    heads = width // head
    own = g0_ref.shape[0] * 2 // 3
    gy = gy_ref[0]
    per_head = blocks * (blocks + 1) // 2
    coming = []
    for h in range(heads):
        cut = pl.ds(h * per_head, per_head)
        coming.append(
            pltpu.make_async_copy(prob_in.at[cut], prob_ref.at[cut], sems.at[len(coming)])
        )
    for source, target in ((w_in, w_ref), (x_in, x_ref), (h1_in, h1_ref)):
        coming.append(pltpu.make_async_copy(source, target, sems.at[len(coming)]))
    for copy in coming:
        copy.start()
    pieces = [unfold(ref[...]) for ref in (g0_ref, g1_ref, g2_ref, g3_ref)]
    for i in range(blocks):
        rows = pl.ds(i * BLOCK, BLOCK)
        pos = pos_ref[rows, :]
        acc = None
        for j, piece in enumerate(pieces):
            part = mm(one_hot_cols(pos, jnp.bitwise_xor(gy, j) * own, own), piece)
            acc = part if acc is None else acc + part
        gm_ref[rows, :] = acc.astype(BF)
    sums = [[None] * heads for _ in range(blocks)]
    for h in range(heads):
        at = h * head
        coming[h].wait()
        diagonals = [None] * blocks
        grad_keys = [None] * blocks
        grad_values = [None] * blocks
        for i in range(blocks):
            rows = pl.ds(i * BLOCK, BLOCK)
            q = qkv_ref[rows, :][:, at : at + head]
            gm = gm_ref[rows, :][:, at : at + head]
            centre = None
            kept = []
            for j in range(i + 1):
                value = qkv_ref[pl.ds(j * BLOCK, BLOCK), :][
                    :, 2 * width + at : 2 * width + at + head
                ]
                low = prob_ref[h * (blocks * (blocks + 1) // 2) + i * (i + 1) // 2 + j]
                prob = low.astype(F32)
                grad_prob = mm_nt(gm, value)
                both = prob * grad_prob
                centre = both if centre is None else centre + both
                kept.append((prob, grad_prob))
                part = mm_tn(low, gm)
                grad_values[j] = part if grad_values[j] is None else grad_values[j] + part
            centre = jnp.sum(centre, axis=-1, keepdims=True)
            acc = None
            for j in range(i + 1):
                prob, grad_prob = kept[j]
                score = prob * (grad_prob - centre)
                diagonals[i - j] = score if diagonals[i - j] is None else diagonals[i - j] + score
                score = score.astype(BF)
                key = qkv_ref[pl.ds(j * BLOCK, BLOCK), :][:, width + at : width + at + head]
                part = mm(score, key)
                acc = part if acc is None else acc + part
                part = mm_tn(score, q)
                grad_keys[j] = part if grad_keys[j] is None else grad_keys[j] + part
            grads_ref[rows, at : at + head] = (acc * 0.125).astype(BF)
        for j in range(blocks):
            rows = pl.ds(j * BLOCK, BLOCK)
            grads_ref[rows, width + at : width + at + head] = grad_keys[j].astype(BF)
            grads_ref[rows, 2 * width + at : 2 * width + at + head] = grad_values[j].astype(BF)
        for k in range(blocks):
            sums[k][h] = unskew_sum(diagonals[k])
    bucket_count = table_ref.shape[0]
    columns = None
    for k in range(blocks):
        labels = lax.broadcasted_iota(jnp.int32, (bucket_count, 2 * BLOCK), 0)
        hot = jnp.where(labels == brev_ref[k : k + 1, :], 1.0, 0.0)
        lines = jnp.concatenate(sums[k] + [jnp.zeros((8 - heads, 2 * BLOCK), F32)], axis=0)
        part = mm_nt(hot, lines, HIGH)
        columns = part if columns is None else columns + part
    table_ref[...] = columns
    for copy in coming[heads:]:
        copy.wait()
    gain_total = None
    weights = w_ref[...]
    gain = jnp.transpose(extras_ref[...].astype(F32))[0:1]
    for j in range(4):
        rows = pl.ds(pl.multiple_of(jnp.bitwise_xor(gy, j) * BLOCK, BLOCK), BLOCK)
        part = mm_nt(grads_ref[rows, :], weights)
        x = x_ref[rows, :].astype(F32)
        scale = lax.rsqrt(jnp.mean(x * x, axis=-1, keepdims=True) + EPS)
        unit = x * scale
        line = jnp.sum(part * unit, axis=0, keepdims=True)
        gain_total = line if gain_total is None else gain_total + line
        scaled = part * gain
        centre = jnp.mean(scaled * unit, axis=-1, keepdims=True)
        part = scale * (scaled - unit * centre)
        part = part + mm(one_hot_cols(pos_ref[rows, :], gy * own, own), d2_ref[...])
        target = send_ref if j % 2 else keep_ref
        target[j // 2] = part.astype(BF)
    small = small_ref[...]
    row = lax.broadcasted_iota(jnp.int32, small.shape, 0)
    small = jnp.where(row == 0, gain_total, small)
    spare = dw_buf.shape[1] - 3 * width
    small = jnp.concatenate(
        [small, jnp.zeros((LANES - small.shape[0], small.shape[1]), F32)], axis=0
    )
    small = jnp.transpose(small)[:, :spare]
    grads = mm_tn(h1_ref[...], grads_ref[...])
    dw_buf[...] = jnp.concatenate([grads, small], axis=1).astype(BF)
    if len(dw_refs) == 1:
        dw_refs[0][...] = dw_buf[...]
        return
    rows = dw_refs[0].shape[1]
    column = jnp.concatenate([columns[:, h : h + 1] for h in range(heads)], axis=0)
    column = jnp.broadcast_to(column, (rows, spare)).astype(BF)
    last = lax.broadcasted_iota(jnp.int32, (rows, spare), 1) == spare - 1
    for n in range(8):
        at = pl.multiple_of(jnp.bitwise_xor(gx_ref[0], n) * rows, 32)
        piece = dw_buf[pl.ds(at, rows), :]
        tail = jnp.where(last, column, piece[:, 3 * width :])
        dw_refs[n % 2][n // 2] = jnp.concatenate([piece[:, : 3 * width], tail], axis=1)


def unsort_kernel(gy_ref, pos_ref, x_ref, d0_ref, d1_ref, d2_ref, d3_ref, out_ref):
    own = d0_ref.shape[0]
    gy = gy_ref[0]
    for i in range(x_ref.shape[0] // BLOCK):
        rows = pl.ds(i * BLOCK, BLOCK)
        pos = pos_ref[rows, :]
        acc = x_ref[rows, :].astype(F32)
        for j, ref in enumerate((d0_ref, d1_ref, d2_ref, d3_ref)):
            acc = acc + mm(one_hot_cols(pos, jnp.bitwise_xor(gy, j) * own, own), ref[...])
        out_ref[rows, :] = acc


def finish_kernel(gy_ref, own_ref, other_ref, g_ref, out_ref):
    gy = gy_ref[0]
    for j in range(4):
        rows = pl.ds(pl.multiple_of(jnp.bitwise_xor(gy, j) * BLOCK, BLOCK), BLOCK)
        source = other_ref if j % 2 else own_ref
        out_ref[rows, :] = g_ref[rows, :].astype(F32) + source[j // 2].astype(F32)


def close_kernel(experts, small_ref, line_ref, project_ref, *outs):
    first_ref, second_ref, route_ref, out_ref = outs
    rows, spare = small_ref.shape
    width = out_ref.shape[1]
    line = line_ref[...]
    out_ref[...] = project_ref[...][:, :width] + line[:, spare:]
    small = small_ref[...] + line[:, :spare]
    small = jnp.concatenate([small, jnp.zeros((rows, LANES - spare), F32)], axis=1)
    small = jnp.concatenate([small, jnp.zeros((LANES - rows, LANES), F32)], axis=0)
    small = jnp.transpose(small)[:, :rows]
    first_ref[...] = small[0:1]
    second_ref[...] = small[1:2]
    route_ref[...] = small[2 : 2 + experts]


def swap(x, axis, bit):
    size = lax.axis_size(axis)
    return lax.ppermute(x, axis, [(i, i ^ bit) for i in range(size)])


def gather_rows(chains, *fills):
    size = lax.axis_size("gx")
    if size != len(RING):
        return [
            lax.all_to_all(
                jnp.broadcast_to(x[None], (size,) + x.shape).reshape(-1, x.shape[1]),
                "gx",
                split_axis=0,
                concat_axis=0,
                tiled=True,
            )
            for x in chains
        ]
    ahead = [(RING[n], RING[(n + 1) % size]) for n in range(size)]
    back = [(b, a) for a, b in ahead]
    out = [[x] for x in chains]
    up, down = list(chains), list(chains)
    for step in range(3):
        for n in range(len(chains)):
            up[n] = lax.ppermute(up[n], "gx", ahead)
            down[n] = lax.ppermute(down[n], "gx", back)
            out[n] += [up[n], down[n]]
        if step < len(fills):
            up[0] = after(up[0], *fills[step])
    return sum([out[n] + [lax.ppermute(up[n], "gx", ahead)] for n in range(len(chains))], [])


def spread(parts, experts):
    if len(parts) == experts:
        return [parts[0]] + [swap(parts[k], "gx", 2 * k) for k in range(1, experts)]
    rows = parts[0].shape[0] // experts
    cut = [parts[0][k * rows : (k + 1) * rows] for k in range(experts)]
    return [jnp.concatenate(spread(cut, experts), axis=0)]


def sum_begin(parts, *fill):
    if len(parts) == 1:
        size = lax.axis_size("gx")
        arrived = lax.all_to_all(parts[0], "gx", split_axis=0, concat_axis=0, tiled=True)
        arrived = arrived.reshape(size, parts[0].shape[0] // size, parts[0].shape[1])
        return [arrived.astype(F32).sum(axis=0)], fill[0]
    pair = add(parts[0], after(swap(parts[1], "gx", 1), *fill)).astype(BF)
    return [pair[0]] + [swap(pair[n], "gx", 2 * n) for n in range(1, pair.shape[0])], pair


def sum_all(x, axis):
    bit = 1
    while bit < lax.axis_size(axis):
        x = x + swap(x, axis, bit)
        bit *= 2
    return x


def after(x, *others):
    return lax.optimization_barrier((x, *others))[0]


def add(a, b):
    return a.astype(F32) + b.astype(F32)


def on_device(
    layer_input,
    w_query,
    w_key,
    w_value,
    w_output,
    attn_gain,
    moe_gain,
    router,
    rel_table,
    w_in,
    w_out,
    expert_ids,
    buckets,
    block_mask,
    grad_out,
):
    n_gx = lax.axis_size("gx")
    n_gy = lax.axis_size("gy")
    seq, model = layer_input.shape
    heads, bucket_count = rel_table.shape
    width = w_query.shape[1]
    shard = w_query.shape[0]
    experts = router.shape[1]
    hidden = w_in.shape[2]
    capacity = 5 * seq // (4 * experts)
    piece = capacity // (2 * n_gy)
    own = experts * 2 * piece
    blocks = seq // BLOCK
    pairs = blocks * (blocks + 1) // 2
    gy = lax.axis_index("gy").astype(jnp.int32).reshape(1)

    gx = lax.axis_index("gx").astype(jnp.int32).reshape(1)
    group = own // experts
    pieces = experts if group % 16 == 0 else 1

    qkv_w, extras = call(
        pack_kernel,
        "pack",
        [struct((shard, 3 * width), BF), struct((shard, LANES + width), BF)],
        [VM] * 7,
        (
            w_query,
            w_key,
            w_value,
            w_output,
            attn_gain.reshape(1, shard),
            moe_gain.reshape(1, shard),
            router.T,
        ),
        cost=1,
    )
    half_model = model // 2
    rear = after(w_out, qkv_w)[0]
    pack = jnp.concatenate([w_in[0], rear[:, :half_model], rear[:, half_model:]], axis=0)
    pack_x = swap(pack, "gy", 2)

    pos_row, pos_col, info = call(
        partial(place_kernel, experts, capacity, group),
        "place",
        [
            struct((1, seq), jnp.int32),
            struct((seq, 1), jnp.int32),
            struct((LANES, seq), BF),
        ],
        [SM, VM],
        (gx, after(expert_ids, qkv_w).reshape(1, seq)),
        cost=2,
    )
    backwards = jnp.concatenate([buckets[::-1], jnp.full((BLOCK,), -1, jnp.int32)])
    brev = jnp.stack(
        [
            backwards[seq - BLOCK * (k + 1) : seq - BLOCK * (k + 1) + 2 * BLOCK]
            for k in range(blocks)
        ]
    )
    table_pad = jnp.concatenate([rel_table, jnp.zeros((8 - heads, bucket_count), F32)], axis=0)
    weights = gather_rows((qkv_w, extras), (pos_row,), (brev, table_pad))
    parts = len(weights) // 2
    pack_y = swap(after(pack, weights[-1]), "gx", 1)
    extras, out_own = call(
        partial(unpack_kernel, parts),
        "unpack",
        [struct((model, LANES), BF), struct((model, width), BF)],
        [SM] + [ANY] * parts,
        (gx, *weights[parts:]),
        scratch=[
            pltpu.VMEM((model, LANES + width), BF),
            pltpu.SemaphoreType.DMA((parts,)),
        ],
        cost=2,
    )
    extras, pack_x = lax.optimization_barrier((extras, pack_x))
    out_core = swap(out_own, "gy", 1)
    out_x = swap(out_own, "gy", 2)
    pack_c = swap(pack, "gy", 1)
    pack_xc = swap(pack_x, "gy", 1)

    h1, qkv, prob, mixed, *sorted_parts, w_full = call(
        partial(attend_kernel, parts),
        "attend",
        [
            struct((seq, model), BF),
            struct((seq, 3 * width), BF),
            struct((heads * pairs, BLOCK, BLOCK), BF),
            struct((seq, width), BF),
        ]
        + [struct((own * 3 // 2, LANES), BF)] * 4
        + [struct((model, 3 * width), BF)],
        [SM, SM, SM] + [VM] * 5 + [ANY] * parts,
        (
            gy,
            gx,
            block_mask,
            layer_input,
            extras,
            table_pad,
            brev,
            pos_row,
            *weights[:parts],
        ),
        scratch=[
            pltpu.VMEM((blocks, BLOCK, BLOCK), F32),
            pltpu.VMEM((seq, model), BF),
            pltpu.VMEM((seq, 3 * width), BF),
            pltpu.VMEM((heads * pairs, BLOCK, BLOCK), BF),
            pltpu.VMEM((model, 3 * width), BF),
            pltpu.SemaphoreType.DMA((parts,)),
            pltpu.SemaphoreType.DMA((3 + heads,)),
        ],
        out_specs=[ANY] * 3 + [VM] * 5 + [ANY],
        cost=60,
    )
    mixed_pieces = [sorted_parts[0]] + [swap(sorted_parts[j], "gy", j) for j in (1, 2, 3)]
    xs, gs, infos = call(
        presort_kernel,
        "presort",
        [struct((own, model), BF), struct((own, model), BF), struct((own, LANES), F32)],
        [SM, VM, VM, VM, VM],
        (gy, after(pos_row, sorted_parts[0]), layer_input, grad_out, info),
        cost=5,
    )
    pack_d = swap(after(pack_x, sorted_parts[0]), "gx", 1)
    out_far = swap(after(out_x, sorted_parts[0]), "gy", 1)
    out_pieces = [out_own, out_core, out_x, out_far]
    mixed_pieces[0], pack_c, pack_xc = lax.optimization_barrier((mixed_pieces[0], pack_c, pack_xc))
    slot_shapes = [struct((own // pieces, model), BF)] * pieces
    routed = call(
        partial(route_kernel, experts, pieces),
        "route",
        slot_shapes
        + slot_shapes
        + [
            struct((own, model), F32),
            struct((own, LANES), F32),
            struct((own, LANES), F32),
        ],
        [VM] * 12,
        (*mixed_pieces, *out_pieces, xs, gs, infos, extras),
        cost=5,
    )
    h2, sg = routed[:pieces], routed[pieces : 2 * pieces]
    residual, router_prob, gate = routed[2 * pieces :]
    pack_yc = swap(after(pack_y, h2[0]), "gy", 1)
    rows_in = spread(h2, experts)
    near = [pack, pack_c, pack_x, pack_xc]
    sg = list(lax.optimization_barrier((*sg, *rows_in))[: len(sg)])
    grads_in = spread(sg, experts)

    def pack_scratch(shards):
        return [
            pltpu.VMEM((model, shards * hidden), BF),
            pltpu.VMEM((shards * hidden, model), BF),
            pltpu.SemaphoreType.DMA((3 * shards,)),
        ]

    kept_shapes = [struct((own, 4 * hidden), BF)] * 2
    begun, act_a, slope_a = call(
        partial(expert_kernel, pieces, False),
        "expert_near",
        [struct((own, model), F32)] + kept_shapes,
        [VM] * pieces + [ANY] * 4,
        (*rows_in, *near),
        scratch=pack_scratch(4),
        cost=7,
    )
    pack_d, begun = lax.optimization_barrier((pack_d, begun, *grads_in))[:2]
    far = [pack_y, pack_yc, pack_d, swap(pack_d, "gy", 1)]
    *result, act_b, slope_b = call(
        partial(expert_kernel, pieces, True),
        "expert_far",
        slot_shapes + kept_shapes,
        [VM] * (pieces + 1) + [ANY] * 4,
        (*rows_in, begun, *far),
        scratch=pack_scratch(4),
        cost=7.5,
    )
    result_back = spread(result, experts)
    ours = ((0, 0), (0, 2), (1, 2), (1, 0))
    theirs = ((0, 1), (0, 3), (1, 3), (1, 1))
    (out_sent,) = call(
        partial(outer_sent_kernel, pieces, theirs, True),
        "outer_out_sent",
        [struct((4, hidden, model), BF)],
        [VM] * (pieces + 2),
        (*grads_in, act_a, act_b),
        cost=4.7,
    )
    out_arrived = swap(out_sent, "gy", 1)
    slope_b = after(slope_b, out_sent)
    *grad_rows, grad_pre = call(
        partial(expert_back_kernel, pieces),
        "expert_back",
        slot_shapes + [struct((own, 8 * hidden), BF)],
        [VM] * (pieces + 2) + [ANY] * 8,
        (*grads_in, slope_a, slope_b, *near, *far),
        scratch=pack_scratch(8),
        cost=12,
    )
    rows_back = spread(grad_rows, experts)
    small_rows = -(-(2 + experts) // 8) * 8
    held_args = (*grads_in, act_a, act_b, out_arrived)
    sent_args = (*rows_in, grad_pre)
    deliver_args = (*result_back, residual, xs, gs, infos, router_prob, gate, extras, *h2)
    out_mine, out_by_x, out_far_y, out_by_y, in_sent, d1, grad_hidden, router_part = call(
        partial(
            joined_kernel,
            ((len(held_args), 4), (len(sent_args), 1), (len(deliver_args), 3)),
            (
                partial(outer_held_kernel, pieces, ours, True),
                partial(
                    outer_sent_kernel, pieces, tuple((0, 4 * a + b) for a, b in theirs), False
                ),
                partial(deliver_kernel, experts, pieces),
            ),
        ),
        "fill_rows",
        [
            struct((hidden, model), F32),
            struct((hidden, model), BF),
            struct((hidden, model), BF),
            struct((hidden, model), BF),
            struct((4, model, hidden), BF),
            struct((own, model), BF),
            struct((own, model), F32),
            struct((small_rows, model), F32),
        ],
        [VM] * (len(held_args) + len(sent_args) + len(deliver_args)),
        (*held_args, *sent_args, *deliver_args),
        cost=13,
    )
    out_far_y = swap(out_far_y, "gx", 1)
    in_arrived = swap(in_sent, "gy", 1)
    *mixed_grads, d2, small, project_keep, project_send = call(
        partial(combine_kernel, pieces),
        "combine",
        [struct((own * 3 // 2, LANES), BF)] * 4
        + [
            struct((own, model), BF),
            struct((small_rows, model), F32),
            struct((model, 2 * width), BF),
            struct((model, 2 * width), BF),
        ],
        [VM] * (pieces + 13),
        (
            *rows_back,
            grad_hidden,
            residual,
            gs,
            router_part,
            extras,
            *out_pieces,
            *mixed_pieces,
        ),
        cost=40,
    )
    grads_mixed = [mixed_grads[0]] + [swap(mixed_grads[j], "gy", j) for j in (1, 2, 3)]
    project_other = swap(project_send, "gy", 1)
    in_mine, in_by_x, in_far_y, in_by_y = call(
        partial(outer_held_kernel, pieces, tuple((0, 4 * a + b) for a, b in ours), False),
        "outer_in_held",
        [
            struct((model, hidden), F32),
            struct((model, hidden), BF),
            struct((model, hidden), BF),
            struct((model, hidden), BF),
        ],
        [VM] * (pieces + 2),
        (*rows_in, after(grad_pre, mixed_grads[0]), in_arrived),
        cost=1,
    )
    grads_mixed[1:] = lax.optimization_barrier((*grads_mixed[1:], in_mine))[:-1]
    in_far_y = swap(in_far_y, "gx", 1)
    out_sum_x = add(out_by_x, after(out_far_y, in_mine)).astype(BF)
    projected = add(after(project_keep, in_mine), project_other).astype(BF)
    grads_mixed[0], in_by_x, out_sum_x, projected = lax.optimization_barrier(
        (grads_mixed[0], in_by_x, out_sum_x, projected)
    )
    projected = lax.all_to_all(projected, "gx", split_axis=0, concat_axis=0, tiled=True)
    out_from_x = swap(out_sum_x, "gy", 2)
    out_from_y = swap(out_by_y, "gx", 1)
    d1_x = swap(after(d1, *grads_mixed[1:]), "gy", 2)
    spare = -(-3 * width // LANES) * LANES - 3 * width
    count = 2 if n_gx == len(RING) and heads * bucket_count == shard else 1
    dw_shape = (model, 3 * width + spare) if count == 1 else (4, shard, 3 * width + spare)
    *dw, keep, send, table = call(
        partial(attend_back_kernel, count),
        "attend_back",
        [struct(dw_shape, BF)] * count
        + [
            struct((2, BLOCK, model), BF),
            struct((2, BLOCK, model), BF),
            struct((bucket_count, 8), F32),
        ],
        [SM, SM] + [VM] * 5 + [ANY, VM, ANY, ANY, ANY] + [VM] * 4,
        (
            gy,
            gx,
            *grads_mixed,
            pos_col,
            prob,
            qkv,
            h1,
            layer_input,
            w_full,
            extras,
            brev,
            d2,
            small,
        ),
        scratch=[
            pltpu.VMEM((seq, width), BF),
            pltpu.VMEM((seq, 3 * width), BF),
            pltpu.VMEM((model, 3 * width + spare), BF),
            pltpu.VMEM((heads * pairs, BLOCK, BLOCK), BF),
            pltpu.VMEM((seq, model), BF),
            pltpu.VMEM((seq, model), BF),
            pltpu.VMEM((model, 3 * width), BF),
            pltpu.SemaphoreType.DMA((heads + 3,)),
        ],
        cost=60,
    )
    keep, send, in_far_y, out_from_x, out_from_y, d1_x, projected, *dw = lax.optimization_barrier(
        (keep, send, in_far_y, out_from_x, out_from_y, d1_x, projected, *dw)
    )
    half = add(keep, swap(send, "gy", 1)).astype(BF)
    half, d1, d1_x, in_by_x = lax.optimization_barrier((half, d1, d1_x, in_by_x))
    half_far = swap(half, "gy", 2)
    in_sum_x = add(in_by_x, in_far_y).astype(BF)
    in_from_x = swap(in_sum_x, "gy", 2)
    d1s = [after(d1, in_sum_x), swap(d1, "gy", 1), d1_x, swap(d1_x, "gy", 1)]
    (layer_output,) = call(
        unsort_kernel,
        "unsort",
        [struct((seq, model), F32)],
        [SM] + [VM] * 6,
        (gy, pos_col, layer_input, *d1s),
        cost=1,
    )
    projected = projected.reshape(n_gx, shard, 2 * width).astype(F32).sum(axis=0)
    sums, dw_done = sum_begin(dw, layer_output)
    in_from_y = swap(after(in_by_y, dw_done), "gx", 1)
    half_far, *sums = lax.optimization_barrier((half_far, layer_output, *sums))
    sums = sums[1:]
    total = add(half, half_far[::-1]).astype(BF)
    other = swap(total, "gy", 1)
    (grad_input,) = call(
        finish_kernel,
        "finish",
        [struct((seq, model), F32)],
        [SM] + [VM] * 3,
        (gy, total, other, grad_out),
        cost=1,
    )
    summed = sums[0].astype(F32)
    for part in sums[1:]:
        summed = summed + part.astype(F32)
    small = summed[:, 3 * width :]
    small = small + swap(small, "gy", 1)
    line = swap(jnp.concatenate([small, projected[:, width:]], axis=1), "gy", 2)
    line = after(line, grad_input)
    grad_first, grad_second, grad_route, grad_out_proj = call(
        partial(close_kernel, experts),
        "close",
        [
            struct((1, shard), F32),
            struct((1, shard), F32),
            struct((experts, shard), F32),
            struct((shard, width), F32),
        ],
        [VM] * 3,
        (small, line, projected),
        cost=1,
    )
    grad_w_out = add(add(out_mine, out_from_y), out_from_x)
    in_from_x, in_from_y = lax.optimization_barrier((in_from_x, in_from_y, grad_input))[:2]
    grad_w_in = add(add(in_mine, in_from_y), in_from_x)
    if count == 1:
        grad_table = sum_all(table, "gx")[:, :heads].T
    else:
        grad_table = summed[:, -1].reshape(heads, bucket_count)

    return (
        layer_output,
        grad_input,
        summed[:, :width],
        summed[:, width : 2 * width],
        summed[:, 2 * width : 3 * width],
        grad_out_proj,
        grad_first.reshape(shard),
        grad_second.reshape(shard),
        grad_route.T,
        grad_table,
        grad_w_in[None],
        grad_w_out[None],
    )


def solution(mesh):
    return jax.shard_map(
        on_device,
        mesh=mesh,
        in_specs=(
            P("gx", None),
            P("gx", "gy"),
            P("gx", "gy"),
            P("gx", "gy"),
            P("gx", "gy"),
            P("gx"),
            P("gx"),
            P("gx", None),
            P("gy", None),
            P("gx", None, "gy"),
            P("gx", "gy", None),
            P("gx", None),
            P(),
            P(),
            P("gx", None),
        ),
        out_specs=(
            P("gx", None),
            P("gx", None),
            P("gx", "gy"),
            P("gx", "gy"),
            P("gx", "gy"),
            P("gx", "gy"),
            P("gx"),
            P("gx"),
            P("gx", None),
            P("gy", None),
            P("gx", None, "gy"),
            P("gx", "gy", None),
        ),
        check_vma=False,
    )
```

```python
from functools import partial

import jax
import jax.numpy as jnp
from jax import lax
from jax.experimental import pallas as pl
from jax.experimental.pallas import tpu as pltpu
from jax.sharding import PartitionSpec as P

BLOCK = 256
EPS = 1e-06
LANES = 128
BF = jnp.bfloat16
F32 = jnp.float32
HIGH = lax.Precision.HIGHEST
VMEM_BYTES = 28 * 1024 * 1024
VMEM_WHOLE = 56 * 1024 * 1024
ALONE = ("pack", "unpack", "attend", "attend_back")
PEAK = 1.15e9
RING = (0, 2, 4, 6, 7, 5, 3, 1)
RING_STEPS = (0, -1, 1, -2, 2, -3, 3, -4)


def mm(left, right, precision=None):
    return lax.dot_general(
        left, right, (((1,), (0,)), ((), ())), precision=precision, preferred_element_type=F32
    )


def mm_nt(left, right, precision=None):
    return lax.dot_general(
        left, right, (((1,), (1,)), ((), ())), precision=precision, preferred_element_type=F32
    )


def mm_tn(left, right, precision=None):
    return lax.dot_general(
        left, right, (((0,), (0,)), ((), ())), precision=precision, preferred_element_type=F32
    )


VM = pl.BlockSpec(memory_space=pltpu.VMEM)
SM = pl.BlockSpec(memory_space=pltpu.SMEM)
ANY = pl.BlockSpec(memory_space=pl.ANY)


def call(kernel, name, outs, in_specs, args, scratch=(), cost=1, out_specs=None):
    return pl.pallas_call(
        kernel,
        name=name,
        out_shape=list(outs),
        in_specs=in_specs,
        out_specs=[VM] * len(outs) if out_specs is None else out_specs,
        scratch_shapes=list(scratch),
        compiler_params=pltpu.CompilerParams(
            vmem_limit_bytes=VMEM_WHOLE if name in ALONE else VMEM_BYTES
        ),
        cost_estimate=pl.CostEstimate(
            flops=int(cost * PEAK), bytes_accessed=1, transcendentals=0
        ),
    )(*args)


def struct(shape, dtype):
    return jax.ShapeDtypeStruct(shape, dtype)


def one_hot_rows(pos_row, start, count):
    slots = lax.broadcasted_iota(jnp.int32, (count, pos_row.shape[1]), 0) + start
    return jnp.where(slots == pos_row, 1.0, 0.0).astype(BF)


def one_hot_cols(pos_col, start, count):
    slots = lax.broadcasted_iota(jnp.int32, (pos_col.shape[0], count), 1) + start
    return jnp.where(slots == pos_col, 1.0, 0.0).astype(BF)


def pack_kernel(q_ref, k_ref, v_ref, o_ref, attn_ref, moe_ref, router_ref, qkv_ref, extras_ref):
    qkv_ref[...] = jnp.concatenate([q_ref[...], k_ref[...], v_ref[...]], axis=1)
    experts, rows = router_ref.shape
    lines = jnp.concatenate(
        [
            attn_ref[...].astype(F32),
            moe_ref[...].astype(F32),
            router_ref[...].astype(F32),
            jnp.zeros((LANES - 2 - experts, rows), F32),
        ],
        axis=0,
    )
    lines = jnp.concatenate([lines, jnp.zeros((LANES, LANES - rows), F32)], axis=1)
    extras_ref[...] = jnp.concatenate(
        [jnp.transpose(lines)[:rows].astype(BF), o_ref[...]], axis=1
    )


def lane_prefix(values):
    row = lax.broadcasted_iota(jnp.int32, (LANES, LANES), 0)
    column = lax.broadcasted_iota(jnp.int32, (LANES, LANES), 1)
    sooner = jnp.where(row < column, 1.0, 0.0).astype(BF)
    carry = jnp.zeros((values.shape[0], 1), F32)
    out = []
    for start in range(0, values.shape[1], LANES):
        part = values[:, start : start + LANES]
        out.append(mm(part.astype(BF), sooner) + carry)
        carry = carry + jnp.sum(part, axis=1, keepdims=True)
    return jnp.concatenate(out, axis=1), carry


def place_kernel(experts, capacity, group, gx_ref, ids_ref, row_ref, col_ref, info_ref):
    seq = ids_ref.shape[1]
    ids = ids_ref[...]
    deep = -(-experts // 8) * 8
    label = lax.broadcasted_iota(jnp.int32, (deep, seq), 0)
    hot = jnp.where(label == ids, 1.0, 0.0)
    before, total = lane_prefix(hot)
    rank = jnp.sum(before * hot, axis=0, keepdims=True)
    kept = rank < capacity
    filled = jnp.minimum(total, 1.0 * capacity)
    empty = jnp.where(label[:, 0:1] < experts, capacity - filled, 0.0)
    row = lax.broadcasted_iota(jnp.int32, (deep, deep), 0)
    column = lax.broadcasted_iota(jnp.int32, (deep, deep), 1)
    sooner = jnp.where(column < row, 1.0, 0.0)
    begins = mm(sooner, jnp.broadcast_to(empty, (deep, LANES)), HIGH)[:, 0:1]
    lost = jnp.broadcast_to(jnp.where(kept, 0.0, 1.0), (8, seq))
    order = lane_prefix(lost)[0][0:1]
    inside = (order >= begins) & (order < begins + empty)
    spare_expert = jnp.sum(jnp.where(inside, label.astype(F32), 0.0), axis=0, keepdims=True)
    spare_rank = jnp.sum(jnp.where(inside, order - begins + filled, 0.0), axis=0, keepdims=True)
    expert = jnp.where(kept, ids.astype(F32), spare_expert).astype(jnp.int32)
    rank = jnp.where(kept, rank, spare_rank)
    block = jnp.floor((rank + 0.5) * (1.0 / group))
    near = jnp.bitwise_xor(expert, gx_ref[0] // 2).astype(F32)
    position = block * (experts * group) + near * group + rank - block * group
    row_ref[...] = position.astype(jnp.int32)
    tall = jnp.transpose(jnp.broadcast_to(position, (LANES, seq)))
    col_ref[...] = tall[:, 0:1].astype(jnp.int32)
    line = lax.broadcasted_iota(jnp.int32, (LANES, seq), 0)
    info = jnp.where(line == 0, jnp.where(kept, 1.0, 0.0), jnp.where(line - 2 == ids, 1.0, 0.0))
    info_ref[...] = info.astype(BF)


def presort_kernel(gy_ref, pos_ref, x_ref, g_ref, info_ref, xs_ref, gs_ref, infos_ref):
    own = xs_ref.shape[0]
    pick = one_hot_rows(pos_ref[...], gy_ref[0] * own, own)
    xs_ref[...] = mm(pick, x_ref[...]).astype(BF)
    gs_ref[...] = mm(pick, g_ref[...]).astype(BF)
    infos_ref[...] = mm_nt(pick, info_ref[...])


def ring_source(gx, step):
    spot = jnp.where(gx % 2 == 0, gx // 2, 7 - gx // 2)
    spot = jnp.bitwise_and(spot + step, 7)
    return jnp.where(spot < 4, 2 * spot, 2 * (7 - spot) + 1)


def assemble(pieces, gx_ref, target, sems):
    copies = []
    rows = pieces[0].shape[0]
    for n, piece in enumerate(pieces):
        place = target
        if len(pieces) > 1:
            at = pl.multiple_of(ring_source(gx_ref[0], RING_STEPS[n]) * rows, 32)
            place = target.at[pl.ds(at, rows), :]
        copy = pltpu.make_async_copy(piece, place, sems.at[n])
        copy.start()
        copies.append(copy)
    return copies


def unpack_kernel(count, *refs):
    gx_ref, pieces = refs[0], refs[1 : 1 + count]
    extras_ref, out_ref, buf, sems = refs[1 + count :]
    for copy in assemble(pieces, gx_ref, buf, sems):
        copy.wait()
    extras_ref[...] = buf[:, :LANES]
    out_ref[...] = buf[:, LANES:]


def attend_kernel(count, *refs):
    gy_ref, gx_ref, mask_ref, x_ref, extras_ref, table_ref, brev_ref, pos_ref = refs[:8]
    pieces = refs[8 : 8 + count]
    h1_out, qkv_out, prob_out, mixed_ref, s0_ref, s1_ref, s2_ref, s3_ref, w_out = refs[
        8 + count : 17 + count
    ]
    toep_ref, h1_ref, qkv_ref, prob_ref, w_ref, sems, out_sems = refs[17 + count :]
    copies = assemble(pieces, gx_ref, w_ref, sems)
    seq = x_ref.shape[0]
    width = mixed_ref.shape[1]
    blocks = seq // BLOCK
    head = 64
    heads = width // head
    gain = jnp.transpose(extras_ref[...].astype(F32))[0:1]
    for copy in copies:
        copy.wait()
    leaving = [pltpu.make_async_copy(w_ref, w_out, out_sems.at[0])]
    leaving[0].start()
    for i in range(blocks):
        rows = pl.ds(i * BLOCK, BLOCK)
        x = x_ref[rows, :].astype(F32)
        scale = lax.rsqrt(jnp.mean(x * x, axis=-1, keepdims=True) + EPS)
        h1 = (x * scale * gain).astype(BF)
        h1_ref[rows, :] = h1
        out = mm(h1, w_ref[...])
        qkv_ref[rows, :] = jnp.concatenate(
            [out[:, :width].astype(BF) * jnp.asarray(0.125, BF), out[:, width:].astype(BF)], axis=1
        )
    for source, target in ((h1_ref, h1_out), (qkv_ref, qkv_out)):
        leaving.append(pltpu.make_async_copy(source, target, out_sems.at[len(leaving)]))
        leaving[-1].start()
    bucket_count = table_ref.shape[1]
    biases = []
    for k in range(blocks):
        labels = lax.broadcasted_iota(jnp.int32, (bucket_count, 2 * BLOCK), 0)
        hot = jnp.where(labels == brev_ref[k : k + 1, :], 1.0, 0.0)
        biases.append(mm(table_ref[...], hot, HIGH))
    for h in range(heads):
        for k in range(blocks):
            line = jnp.broadcast_to(biases[k][h : h + 1, :], (BLOCK, 2 * BLOCK))
            skew = pltpu.roll(line, BLOCK + 1, 1, stride=1, stride_axis=0)[:, :BLOCK]
            if k == 0:
                r = lax.broadcasted_iota(jnp.int32, (BLOCK, BLOCK), 0)
                c = lax.broadcasted_iota(jnp.int32, (BLOCK, BLOCK), 1)
                skew = jnp.where(r >= c, skew, -1e30)
            toep_ref[k] = skew
        at = h * head
        for i in range(blocks):
            q = qkv_ref[pl.ds(i * BLOCK, BLOCK), :][:, at : at + head]
            scores = []
            peak = None
            for j in range(i + 1):
                key = qkv_ref[pl.ds(j * BLOCK, BLOCK), :][:, width + at : width + at + head]
                s = mm_nt(q, key) + toep_ref[i - j]
                if j < i:
                    s = s + jnp.where(mask_ref[i, j] == 1, 0.0, -1e30)
                scores.append(s)
                peak = s if peak is None else jnp.maximum(peak, s)
            peak = jnp.max(peak, axis=-1, keepdims=True)
            total = None
            terms = []
            for s in scores:
                e = jnp.exp(s - peak)
                terms.append(e)
                total = e if total is None else total + e
            inverse = 1.0 / jnp.sum(total, axis=-1, keepdims=True)
            acc = None
            for j in range(i + 1):
                prob = (terms[j] * inverse).astype(BF)
                prob_ref[h * (blocks * (blocks + 1) // 2) + i * (i + 1) // 2 + j] = prob
                value = qkv_ref[pl.ds(j * BLOCK, BLOCK), :][
                    :, 2 * width + at : 2 * width + at + head
                ]
                part = mm(prob, value)
                acc = part if acc is None else acc + part
            mixed_ref[pl.ds(i * BLOCK, BLOCK), at : at + head] = acc.astype(BF)
        done = pl.ds(h * (blocks * (blocks + 1) // 2), blocks * (blocks + 1) // 2)
        leaving.append(
            pltpu.make_async_copy(
                prob_ref.at[done], prob_out.at[done], out_sems.at[len(leaving)]
            )
        )
        leaving[-1].start()
    own = s0_ref.shape[0] * 2 // 3
    mixed = mixed_ref[...]
    for j, ref in enumerate((s0_ref, s1_ref, s2_ref, s3_ref)):
        start = jnp.bitwise_xor(gy_ref[0], j) * own
        ref[...] = fold(mm(one_hot_rows(pos_ref[...], start, own), mixed).astype(BF))
    for copy in leaving:
        copy.wait()


def route_kernel(experts, pieces, *refs):
    mixed_refs, out_refs = refs[:4], refs[4:8]
    xs_ref, gs_ref, infos_ref, extras_ref = refs[8:12]
    h2_refs, sg_refs = refs[12 : 12 + pieces], refs[12 + pieces : 12 + 2 * pieces]
    res_ref, prob_ref, gate_ref = refs[12 + 2 * pieces :]
    attn = None
    for j in range(4):
        part = mm_nt(unfold(mixed_refs[j][...]), out_refs[j][...])
        attn = part if attn is None else attn + part
    extras = extras_ref[...]
    gain = jnp.transpose(extras.astype(F32))[1:2]
    residual = xs_ref[...].astype(F32) + attn
    res_ref[...] = residual
    scale = lax.rsqrt(jnp.mean(residual * residual, axis=-1, keepdims=True) + EPS)
    h2 = (residual * scale * gain).astype(BF)
    logits = mm(h2, extras)
    lane = lax.broadcasted_iota(jnp.int32, logits.shape, 1)
    real = (lane >= 2) & (lane < 2 + experts)
    logits = jnp.where(real, logits, -1e30)
    e = jnp.exp(logits - jnp.max(logits, axis=-1, keepdims=True))
    prob = e / jnp.sum(e, axis=-1, keepdims=True)
    prob_ref[...] = prob
    info = infos_ref[...]
    keep = info[:, 0:1]
    gate = jnp.sum(jnp.where(real, prob * info, 0.0), axis=-1, keepdims=True)
    gate_ref[...] = jnp.broadcast_to(gate, gate_ref.shape)
    h2 = jnp.where(keep > 0.0, h2.astype(F32), 0.0).astype(BF)
    sg = jnp.where(keep > 0.0, gate * gs_ref[...].astype(F32), 0.0).astype(BF)
    split(h2, h2_refs)
    split(sg, sg_refs)


def fold(value):
    rows = value.shape[0]
    edge = value[:, LANES:]
    edge = jnp.concatenate([edge[: rows // 2], edge[rows // 2 :]], axis=1)
    return jnp.concatenate([value[:, :LANES], edge], axis=0)


def unfold(value):
    rows = value.shape[0] * 2 // 3
    edge = value[rows:]
    half = LANES // 2
    edge = jnp.concatenate([edge[:, :half], edge[:, half:]], axis=0)
    return jnp.concatenate([value[:rows], edge], axis=1)


def split(value, refs):
    rows = refs[0].shape[0]
    for n, ref in enumerate(refs):
        ref[...] = value[n * rows : (n + 1) * rows, :]


def joined(refs):
    if len(refs) == 1:
        return refs[0][...]
    return jnp.concatenate([ref[...] for ref in refs], axis=0)


def fetch(packs, win_buf, wout_buf, sems):
    copies = []
    model, hidden = win_buf.shape[0], packs[0].shape[1]
    for j, pack in enumerate(packs):
        place = pl.ds(j * hidden, hidden)
        cuts = (
            (pack.at[pl.ds(0, model), :], win_buf.at[:, place]),
            (pack.at[pl.ds(model, hidden), :], wout_buf.at[place, pl.ds(0, hidden)]),
            (pack.at[pl.ds(model + hidden, hidden), :], wout_buf.at[place, pl.ds(hidden, hidden)]),
        )
        for n, (source, target) in enumerate(cuts):
            copies.append(pltpu.make_async_copy(source, target, sems.at[3 * j + n]))
    return copies


def expert_kernel(pieces, last, *refs):
    row_refs = refs[:pieces]
    refs = refs[pieces:]
    if last:
        before_ref, refs = refs[0], refs[1:]
    packs, refs = refs[:4], refs[4:]
    outs = refs[: pieces if last else 1]
    act_ref, slope_ref, win_buf, wout_buf, sems = refs[len(outs) :]
    pair = 2 * packs[0].shape[1]
    copies = fetch(packs, win_buf, wout_buf, sems)
    for copy in copies:
        copy.start()
    rows = joined(row_refs)
    acc = before_ref[...] if last else None
    for j in range(2):
        place = slice(j * pair, (j + 1) * pair)
        mine = copies[6 * j : 6 * j + 6]
        mine[0].wait()
        mine[3].wait()
        pre = mm(rows, win_buf[:, place])
        cdf = 0.5 * (1.0 + lax.erf(pre * 0.7071067811865476))
        slope = cdf + pre * (0.3989422804014327 * jnp.exp(-0.5 * pre * pre))
        act = (pre * cdf).astype(BF)
        act_ref[:, place] = act
        slope_ref[:, place] = slope.astype(BF)
        for n in (1, 2, 4, 5):
            mine[n].wait()
        part = mm(act, wout_buf[place, :])
        acc = part if acc is None else acc + part
    if last:
        split(acc.astype(BF), outs)
    else:
        outs[0][...] = acc


def expert_back_kernel(pieces, *refs):
    sg_refs, slopes = refs[:pieces], refs[pieces : pieces + 2]
    packs, refs = refs[pieces + 2 : pieces + 10], refs[pieces + 10 :]
    gr_refs = refs[:pieces]
    gp_ref, win_buf, wout_buf, sems = refs[pieces:]
    pair = 2 * packs[0].shape[1]
    copies = fetch(packs, win_buf, wout_buf, sems)
    for j in range(4):
        for n in (1, 2, 4, 5, 0, 3):
            copies[6 * j + n].start()
    sg = joined(sg_refs)
    acc = None
    for j in range(4):
        place = slice(j * pair, (j + 1) * pair)
        near = slice(j % 2 * pair, (j % 2 + 1) * pair)
        mine = copies[6 * j : 6 * j + 6]
        for n in (1, 2, 4, 5):
            mine[n].wait()
        grad = mm_nt(sg, wout_buf[place, :])
        grad = (grad * slopes[j // 2][:, near].astype(F32)).astype(BF)
        gp_ref[:, place] = grad
        mine[0].wait()
        mine[3].wait()
        part = mm_nt(grad, win_buf[:, place])
        acc = part if acc is None else acc + part
    split(acc.astype(BF), gr_refs)


def outer_sent_kernel(pieces, picks, flip, *refs):
    wide = joined(refs[:pieces])
    sources, out_ref = refs[pieces:-1], refs[-1]
    hidden = out_ref.shape[1 if flip else 2]
    for n, (a, b) in enumerate(picks):
        thin = sources[a][:, b * hidden : (b + 1) * hidden]
        out_ref[n] = (mm_tn(thin, wide) if flip else mm_tn(wide, thin)).astype(BF)


def outer_held_kernel(pieces, picks, flip, *refs):
    wide = joined(refs[:pieces])
    sources, arrived_ref = refs[pieces:-5], refs[-5]
    out_refs = refs[-4:]
    hidden = out_refs[0].shape[0 if flip else 1]
    for n, (a, b) in enumerate(picks):
        thin = sources[a][:, b * hidden : (b + 1) * hidden]
        value = mm_tn(thin, wide) if flip else mm_tn(wide, thin)
        value = value + arrived_ref[n].astype(F32)
        out_refs[n][...] = value.astype(out_refs[n].dtype)


def joined_kernel(counts, kernels, *refs):
    sources = refs[: sum(c[0] for c in counts)]
    results = refs[len(sources) :]
    for (taken, given), kernel in zip(counts, kernels):
        kernel(*sources[:taken], *results[:given])
        sources, results = sources[taken:], results[given:]


def deliver_kernel(experts, pieces, *refs):
    er_refs = refs[:pieces]
    res_ref, xs_ref, gs_ref, infos_ref, prob_ref, gate_ref, extras_ref = refs[
        pieces : pieces + 7
    ]
    h2_refs = refs[pieces + 7 : 2 * pieces + 7]
    d1_ref, gh_ref, router_ref = refs[2 * pieces + 7 :]
    prob = prob_ref[...]
    gate = gate_ref[...][:, 0:1]
    lane = lax.broadcasted_iota(jnp.int32, prob.shape, 1)
    real = (lane >= 2) & (lane < 2 + experts)
    hot = jnp.where(real, infos_ref[...], 0.0)
    result = joined(er_refs).astype(F32)
    d1_ref[...] = (res_ref[...] - xs_ref[...].astype(F32) + gate * result).astype(BF)
    grad_gate = jnp.sum(gs_ref[...].astype(F32) * result, axis=-1, keepdims=True)
    grad_logits = (prob * (hot - gate) * grad_gate).astype(BF)
    gh_ref[...] = mm_nt(grad_logits, extras_ref[...])
    router_ref[...] = mm_tn(grad_logits, joined(h2_refs))[: router_ref.shape[0]]


def combine_kernel(pieces, *refs):
    gr_refs = refs[:pieces]
    gh_ref, res_ref, gs_ref, router_ref, extras_ref = refs[pieces : pieces + 5]
    out_refs, mixed_refs = refs[pieces + 5 : pieces + 9], refs[pieces + 9 : pieces + 13]
    gm_refs = refs[pieces + 13 : pieces + 17]
    d2_ref, small_ref, keep_ref, send_ref = refs[pieces + 17 :]
    gain = jnp.transpose(extras_ref[...].astype(F32))[1:2]
    residual = res_ref[...]
    g = gs_ref[...].astype(F32)
    grad_h2 = gh_ref[...] + joined(gr_refs).astype(F32)
    scale = lax.rsqrt(jnp.mean(residual * residual, axis=-1, keepdims=True) + EPS)
    unit = residual * scale
    scaled = grad_h2 * gain
    centre = jnp.mean(scaled * unit, axis=-1, keepdims=True)
    d2 = (scale * (scaled - unit * centre)).astype(BF)
    d2_ref[...] = d2
    grad_attn = (g + d2.astype(F32)).astype(BF)
    for j in range(4):
        gm_refs[j][...] = fold(mm(grad_attn, out_refs[j][...]).astype(BF))
    for target, j in ((keep_ref, 0), (send_ref, 1)):
        mixed = jnp.concatenate(
            [unfold(mixed_refs[j][...]), unfold(mixed_refs[j + 2][...])], axis=1
        )
        target[...] = mm_tn(grad_attn, mixed).astype(BF)
    grad_gain = jnp.sum(grad_h2 * unit, axis=0, keepdims=True)
    small = router_ref[...]
    row = lax.broadcasted_iota(jnp.int32, small.shape, 0)
    small_ref[...] = jnp.where(row == 1, grad_gain, small)


def unskew_sum(block):
    zeros = jnp.zeros((8, BLOCK), F32)
    acc = None
    for i in range(BLOCK // 8):
        piece = jnp.concatenate([block[8 * i : 8 * i + 8, :], zeros], axis=1)
        shift = BLOCK - 8 - 8 * i
        if shift:
            piece = pltpu.roll(piece, shift, 1)
        acc = piece if acc is None else acc + piece
    left = 7 - lax.broadcasted_iota(jnp.int32, acc.shape, 0)
    for bit in range(3):
        moved = pltpu.roll(acc, 1 << bit, 1)
        acc = jnp.where((left >> bit) & 1 == 1, moved, acc)
    return jnp.sum(acc, axis=0, keepdims=True)


def attend_back_kernel(count, *refs):
    gy_ref, gx_ref, g0_ref, g1_ref, g2_ref, g3_ref = refs[:6]
    pos_ref, prob_in, qkv_ref, h1_in, x_in, w_in, extras_ref, brev_ref = refs[6:14]
    d2_ref, small_ref = refs[14:16]
    dw_refs = refs[16 : 16 + count]
    keep_ref, send_ref, table_ref, gm_ref, grads_ref, dw_buf = refs[16 + count : 22 + count]
    prob_ref, h1_ref, x_ref, w_ref, sems = refs[22 + count :]
    seq, width = gm_ref.shape
    blocks = seq // BLOCK
    head = 64
    heads = width // head
    own = g0_ref.shape[0] * 2 // 3
    gy = gy_ref[0]
    per_head = blocks * (blocks + 1) // 2
    coming = []
    for h in range(heads):
        cut = pl.ds(h * per_head, per_head)
        coming.append(
            pltpu.make_async_copy(prob_in.at[cut], prob_ref.at[cut], sems.at[len(coming)])
        )
    for source, target in ((w_in, w_ref), (x_in, x_ref), (h1_in, h1_ref)):
        coming.append(pltpu.make_async_copy(source, target, sems.at[len(coming)]))
    for copy in coming:
        copy.start()
    pieces = [unfold(ref[...]) for ref in (g0_ref, g1_ref, g2_ref, g3_ref)]
    for i in range(blocks):
        rows = pl.ds(i * BLOCK, BLOCK)
        pos = pos_ref[rows, :]
        acc = None
        for j, piece in enumerate(pieces):
            part = mm(one_hot_cols(pos, jnp.bitwise_xor(gy, j) * own, own), piece)
            acc = part if acc is None else acc + part
        gm_ref[rows, :] = acc.astype(BF)
    sums = [[None] * heads for _ in range(blocks)]
    for h in range(heads):
        at = h * head
        coming[h].wait()
        diagonals = [None] * blocks
        grad_keys = [None] * blocks
        grad_values = [None] * blocks
        for i in range(blocks):
            rows = pl.ds(i * BLOCK, BLOCK)
            q = qkv_ref[rows, :][:, at : at + head]
            gm = gm_ref[rows, :][:, at : at + head]
            centre = None
            kept = []
            for j in range(i + 1):
                value = qkv_ref[pl.ds(j * BLOCK, BLOCK), :][
                    :, 2 * width + at : 2 * width + at + head
                ]
                low = prob_ref[h * (blocks * (blocks + 1) // 2) + i * (i + 1) // 2 + j]
                prob = low.astype(F32)
                grad_prob = mm_nt(gm, value)
                both = prob * grad_prob
                centre = both if centre is None else centre + both
                kept.append((prob, grad_prob))
                part = mm_tn(low, gm)
                grad_values[j] = part if grad_values[j] is None else grad_values[j] + part
            centre = jnp.sum(centre, axis=-1, keepdims=True)
            acc = None
            for j in range(i + 1):
                prob, grad_prob = kept[j]
                score = prob * (grad_prob - centre)
                diagonals[i - j] = score if diagonals[i - j] is None else diagonals[i - j] + score
                score = score.astype(BF)
                key = qkv_ref[pl.ds(j * BLOCK, BLOCK), :][:, width + at : width + at + head]
                part = mm(score, key)
                acc = part if acc is None else acc + part
                part = mm_tn(score, q)
                grad_keys[j] = part if grad_keys[j] is None else grad_keys[j] + part
            grads_ref[rows, at : at + head] = (acc * 0.125).astype(BF)
        for j in range(blocks):
            rows = pl.ds(j * BLOCK, BLOCK)
            grads_ref[rows, width + at : width + at + head] = grad_keys[j].astype(BF)
            grads_ref[rows, 2 * width + at : 2 * width + at + head] = grad_values[j].astype(BF)
        for k in range(blocks):
            sums[k][h] = unskew_sum(diagonals[k])
    bucket_count = table_ref.shape[0]
    columns = None
    for k in range(blocks):
        labels = lax.broadcasted_iota(jnp.int32, (bucket_count, 2 * BLOCK), 0)
        hot = jnp.where(labels == brev_ref[k : k + 1, :], 1.0, 0.0)
        lines = jnp.concatenate(sums[k] + [jnp.zeros((8 - heads, 2 * BLOCK), F32)], axis=0)
        part = mm_nt(hot, lines, HIGH)
        columns = part if columns is None else columns + part
    table_ref[...] = columns
    for copy in coming[heads:]:
        copy.wait()
    gain_total = None
    weights = w_ref[...]
    gain = jnp.transpose(extras_ref[...].astype(F32))[0:1]
    for j in range(4):
        rows = pl.ds(pl.multiple_of(jnp.bitwise_xor(gy, j) * BLOCK, BLOCK), BLOCK)
        part = mm_nt(grads_ref[rows, :], weights)
        x = x_ref[rows, :].astype(F32)
        scale = lax.rsqrt(jnp.mean(x * x, axis=-1, keepdims=True) + EPS)
        unit = x * scale
        line = jnp.sum(part * unit, axis=0, keepdims=True)
        gain_total = line if gain_total is None else gain_total + line
        scaled = part * gain
        centre = jnp.mean(scaled * unit, axis=-1, keepdims=True)
        part = scale * (scaled - unit * centre)
        part = part + mm(one_hot_cols(pos_ref[rows, :], gy * own, own), d2_ref[...])
        target = send_ref if j % 2 else keep_ref
        target[j // 2] = part.astype(BF)
    small = small_ref[...]
    row = lax.broadcasted_iota(jnp.int32, small.shape, 0)
    small = jnp.where(row == 0, gain_total, small)
    spare = dw_buf.shape[1] - 3 * width
    small = jnp.concatenate(
        [small, jnp.zeros((LANES - small.shape[0], small.shape[1]), F32)], axis=0
    )
    small = jnp.transpose(small)[:, :spare]
    grads = mm_tn(h1_ref[...], grads_ref[...])
    dw_buf[...] = jnp.concatenate([grads, small], axis=1).astype(BF)
    if len(dw_refs) == 1:
        dw_refs[0][...] = dw_buf[...]
        return
    rows = dw_refs[0].shape[1]
    column = jnp.concatenate([columns[:, h : h + 1] for h in range(heads)], axis=0)
    column = jnp.broadcast_to(column, (rows, spare)).astype(BF)
    last = lax.broadcasted_iota(jnp.int32, (rows, spare), 1) == spare - 1
    for n in range(8):
        at = pl.multiple_of(jnp.bitwise_xor(gx_ref[0], n) * rows, 32)
        piece = dw_buf[pl.ds(at, rows), :]
        tail = jnp.where(last, column, piece[:, 3 * width :])
        dw_refs[n % 2][n // 2] = jnp.concatenate([piece[:, : 3 * width], tail], axis=1)


def unsort_kernel(gy_ref, pos_ref, x_ref, d0_ref, d1_ref, d2_ref, d3_ref, out_ref):
    own = d0_ref.shape[0]
    gy = gy_ref[0]
    every = jnp.concatenate([ref[...] for ref in (d0_ref, d1_ref, d2_ref, d3_ref)], axis=0)
    for i in range(x_ref.shape[0] // BLOCK):
        rows = pl.ds(i * BLOCK, BLOCK)
        pos = pos_ref[rows, :]
        near = pos
        for j in range(4):
            start = jnp.bitwise_xor(gy, j) * own
            near = jnp.where((pos >= start) & (pos < start + own), pos - start + j * own, near)
        hot = one_hot_cols(near, 0, 4 * own)
        out_ref[rows, :] = x_ref[rows, :].astype(F32) + mm(hot, every)


def finish_kernel(gy_ref, own_ref, other_ref, g_ref, out_ref):
    gy = gy_ref[0]
    for j in range(4):
        rows = pl.ds(pl.multiple_of(jnp.bitwise_xor(gy, j) * BLOCK, BLOCK), BLOCK)
        source = other_ref if j % 2 else own_ref
        out_ref[rows, :] = g_ref[rows, :].astype(F32) + source[j // 2].astype(F32)


def close_kernel(experts, small_ref, line_ref, project_ref, *outs):
    first_ref, second_ref, route_ref, out_ref = outs
    rows, spare = small_ref.shape
    width = out_ref.shape[1]
    line = line_ref[...]
    out_ref[...] = project_ref[...][:, :width] + line[:, spare:]
    small = small_ref[...] + line[:, :spare]
    small = jnp.concatenate([small, jnp.zeros((rows, LANES - spare), F32)], axis=1)
    small = jnp.concatenate([small, jnp.zeros((LANES - rows, LANES), F32)], axis=0)
    small = jnp.transpose(small)[:, :rows]
    first_ref[...] = small[0:1]
    second_ref[...] = small[1:2]
    route_ref[...] = small[2 : 2 + experts]


def swap(x, axis, bit):
    size = lax.axis_size(axis)
    return lax.ppermute(x, axis, [(i, i ^ bit) for i in range(size)])


def gather_rows(chains, *fills):
    size = lax.axis_size("gx")
    if size != len(RING):
        return [
            lax.all_to_all(
                jnp.broadcast_to(x[None], (size,) + x.shape).reshape(-1, x.shape[1]),
                "gx",
                split_axis=0,
                concat_axis=0,
                tiled=True,
            )
            for x in chains
        ]
    ahead = [(RING[n], RING[(n + 1) % size]) for n in range(size)]
    back = [(b, a) for a, b in ahead]
    out = [[x] for x in chains]
    up, down = list(chains), list(chains)
    for step in range(3):
        for n in range(len(chains)):
            up[n] = lax.ppermute(up[n], "gx", ahead)
            down[n] = lax.ppermute(down[n], "gx", back)
            out[n] += [up[n], down[n]]
        if step < len(fills):
            up[0] = after(up[0], *fills[step])
    return sum([out[n] + [lax.ppermute(up[n], "gx", ahead)] for n in range(len(chains))], [])


def spread(parts, experts):
    if len(parts) == experts:
        return [parts[0]] + [swap(parts[k], "gx", 2 * k) for k in range(1, experts)]
    rows = parts[0].shape[0] // experts
    cut = [parts[0][k * rows : (k + 1) * rows] for k in range(experts)]
    return [jnp.concatenate(spread(cut, experts), axis=0)]


def sum_begin(parts, *fill):
    if len(parts) == 1:
        size = lax.axis_size("gx")
        arrived = lax.all_to_all(parts[0], "gx", split_axis=0, concat_axis=0, tiled=True)
        arrived = arrived.reshape(size, parts[0].shape[0] // size, parts[0].shape[1])
        return [arrived.astype(F32).sum(axis=0)], fill[0]
    pair = add(parts[0], after(swap(parts[1], "gx", 1), *fill)).astype(BF)
    return [pair[0]] + [swap(pair[n], "gx", 2 * n) for n in range(1, pair.shape[0])], pair


def sum_all(x, axis):
    bit = 1
    while bit < lax.axis_size(axis):
        x = x + swap(x, axis, bit)
        bit *= 2
    return x


def after(x, *others):
    return lax.optimization_barrier((x, *others))[0]


def add(a, b):
    return a.astype(F32) + b.astype(F32)


def on_device(
    layer_input,
    w_query,
    w_key,
    w_value,
    w_output,
    attn_gain,
    moe_gain,
    router,
    rel_table,
    w_in,
    w_out,
    expert_ids,
    buckets,
    block_mask,
    grad_out,
):
    n_gx = lax.axis_size("gx")
    n_gy = lax.axis_size("gy")
    seq, model = layer_input.shape
    heads, bucket_count = rel_table.shape
    width = w_query.shape[1]
    shard = w_query.shape[0]
    experts = router.shape[1]
    hidden = w_in.shape[2]
    capacity = 5 * seq // (4 * experts)
    piece = capacity // (2 * n_gy)
    own = experts * 2 * piece
    blocks = seq // BLOCK
    pairs = blocks * (blocks + 1) // 2
    gy = lax.axis_index("gy").astype(jnp.int32).reshape(1)

    gx = lax.axis_index("gx").astype(jnp.int32).reshape(1)
    group = own // experts
    pieces = experts if group % 16 == 0 else 1

    qkv_w, extras = call(
        pack_kernel,
        "pack",
        [struct((shard, 3 * width), BF), struct((shard, LANES + width), BF)],
        [VM] * 7,
        (
            w_query,
            w_key,
            w_value,
            w_output,
            attn_gain.reshape(1, shard),
            moe_gain.reshape(1, shard),
            router.T,
        ),
        cost=1,
    )
    half_model = model // 2
    rear = after(w_out, qkv_w)[0]
    pack = jnp.concatenate([w_in[0], rear[:, :half_model], rear[:, half_model:]], axis=0)
    pack_x = swap(pack, "gy", 2)

    pos_row, pos_col, info = call(
        partial(place_kernel, experts, capacity, group),
        "place",
        [
            struct((1, seq), jnp.int32),
            struct((seq, 1), jnp.int32),
            struct((LANES, seq), BF),
        ],
        [SM, VM],
        (gx, after(expert_ids, qkv_w).reshape(1, seq)),
        cost=2,
    )
    backwards = jnp.concatenate([buckets[::-1], jnp.full((BLOCK,), -1, jnp.int32)])
    brev = jnp.stack(
        [
            backwards[seq - BLOCK * (k + 1) : seq - BLOCK * (k + 1) + 2 * BLOCK]
            for k in range(blocks)
        ]
    )
    table_pad = jnp.concatenate([rel_table, jnp.zeros((8 - heads, bucket_count), F32)], axis=0)
    weights = gather_rows((qkv_w, extras), (pos_row,), (brev, table_pad))
    parts = len(weights) // 2
    pack_y = swap(after(pack, weights[-1]), "gx", 1)
    extras, out_own = call(
        partial(unpack_kernel, parts),
        "unpack",
        [struct((model, LANES), BF), struct((model, width), BF)],
        [SM] + [ANY] * parts,
        (gx, *weights[parts:]),
        scratch=[
            pltpu.VMEM((model, LANES + width), BF),
            pltpu.SemaphoreType.DMA((parts,)),
        ],
        cost=2,
    )
    extras, pack_x = lax.optimization_barrier((extras, pack_x))
    out_core = swap(out_own, "gy", 1)
    out_x = swap(out_own, "gy", 2)
    pack_c = swap(pack, "gy", 1)
    pack_xc = swap(pack_x, "gy", 1)

    h1, qkv, prob, mixed, *sorted_parts, w_full = call(
        partial(attend_kernel, parts),
        "attend",
        [
            struct((seq, model), BF),
            struct((seq, 3 * width), BF),
            struct((heads * pairs, BLOCK, BLOCK), BF),
            struct((seq, width), BF),
        ]
        + [struct((own * 3 // 2, LANES), BF)] * 4
        + [struct((model, 3 * width), BF)],
        [SM, SM, SM] + [VM] * 5 + [ANY] * parts,
        (
            gy,
            gx,
            block_mask,
            layer_input,
            extras,
            table_pad,
            brev,
            pos_row,
            *weights[:parts],
        ),
        scratch=[
            pltpu.VMEM((blocks, BLOCK, BLOCK), F32),
            pltpu.VMEM((seq, model), BF),
            pltpu.VMEM((seq, 3 * width), BF),
            pltpu.VMEM((heads * pairs, BLOCK, BLOCK), BF),
            pltpu.VMEM((model, 3 * width), BF),
            pltpu.SemaphoreType.DMA((parts,)),
            pltpu.SemaphoreType.DMA((3 + heads,)),
        ],
        out_specs=[ANY] * 3 + [VM] * 5 + [ANY],
        cost=60,
    )
    mixed_pieces = [sorted_parts[0]] + [swap(sorted_parts[j], "gy", j) for j in (1, 2, 3)]
    xs, gs, infos = call(
        presort_kernel,
        "presort",
        [struct((own, model), BF), struct((own, model), BF), struct((own, LANES), F32)],
        [SM, VM, VM, VM, VM],
        (gy, after(pos_row, sorted_parts[0]), layer_input, grad_out, info),
        cost=5,
    )
    pack_d = swap(after(pack_x, sorted_parts[0]), "gx", 1)
    out_far = swap(after(out_x, sorted_parts[0]), "gy", 1)
    out_pieces = [out_own, out_core, out_x, out_far]
    mixed_pieces[0], pack_c, pack_xc = lax.optimization_barrier((mixed_pieces[0], pack_c, pack_xc))
    slot_shapes = [struct((own // pieces, model), BF)] * pieces
    routed = call(
        partial(route_kernel, experts, pieces),
        "route",
        slot_shapes
        + slot_shapes
        + [
            struct((own, model), F32),
            struct((own, LANES), F32),
            struct((own, LANES), F32),
        ],
        [VM] * 12,
        (*mixed_pieces, *out_pieces, xs, gs, infos, extras),
        cost=5,
    )
    h2, sg = routed[:pieces], routed[pieces : 2 * pieces]
    residual, router_prob, gate = routed[2 * pieces :]
    pack_yc = swap(after(pack_y, h2[0]), "gy", 1)
    rows_in = spread(h2, experts)
    near = [pack, pack_c, pack_x, pack_xc]
    sg = list(lax.optimization_barrier((*sg, *rows_in))[: len(sg)])
    grads_in = spread(sg, experts)

    def pack_scratch(shards):
        return [
            pltpu.VMEM((model, shards * hidden), BF),
            pltpu.VMEM((shards * hidden, model), BF),
            pltpu.SemaphoreType.DMA((3 * shards,)),
        ]

    kept_shapes = [struct((own, 4 * hidden), BF)] * 2
    begun, act_a, slope_a = call(
        partial(expert_kernel, pieces, False),
        "expert_near",
        [struct((own, model), F32)] + kept_shapes,
        [VM] * pieces + [ANY] * 4,
        (*rows_in, *near),
        scratch=pack_scratch(4),
        cost=7,
    )
    pack_d, begun = lax.optimization_barrier((pack_d, begun, *grads_in))[:2]
    far = [pack_y, pack_yc, pack_d, swap(pack_d, "gy", 1)]
    *result, act_b, slope_b = call(
        partial(expert_kernel, pieces, True),
        "expert_far",
        slot_shapes + kept_shapes,
        [VM] * (pieces + 1) + [ANY] * 4,
        (*rows_in, begun, *far),
        scratch=pack_scratch(4),
        cost=7.5,
    )
    result_back = spread(result, experts)
    ours = ((0, 0), (0, 2), (1, 2), (1, 0))
    theirs = ((0, 1), (0, 3), (1, 3), (1, 1))
    (out_sent,) = call(
        partial(outer_sent_kernel, pieces, theirs, True),
        "outer_out_sent",
        [struct((4, hidden, model), BF)],
        [VM] * (pieces + 2),
        (*grads_in, act_a, act_b),
        cost=4.7,
    )
    out_arrived = swap(out_sent, "gy", 1)
    slope_b = after(slope_b, out_sent)
    *grad_rows, grad_pre = call(
        partial(expert_back_kernel, pieces),
        "expert_back",
        slot_shapes + [struct((own, 8 * hidden), BF)],
        [VM] * (pieces + 2) + [ANY] * 8,
        (*grads_in, slope_a, slope_b, *near, *far),
        scratch=pack_scratch(8),
        cost=12,
    )
    rows_back = spread(grad_rows, experts)
    small_rows = -(-(2 + experts) // 8) * 8
    held_args = (*grads_in, act_a, act_b, out_arrived)
    sent_args = (*rows_in, grad_pre)
    deliver_args = (*result_back, residual, xs, gs, infos, router_prob, gate, extras, *h2)
    out_mine, out_by_x, out_far_y, out_by_y, in_sent, d1, grad_hidden, router_part = call(
        partial(
            joined_kernel,
            ((len(held_args), 4), (len(sent_args), 1), (len(deliver_args), 3)),
            (
                partial(outer_held_kernel, pieces, ours, True),
                partial(
                    outer_sent_kernel, pieces, tuple((0, 4 * a + b) for a, b in theirs), False
                ),
                partial(deliver_kernel, experts, pieces),
            ),
        ),
        "fill_rows",
        [
            struct((hidden, model), F32),
            struct((hidden, model), BF),
            struct((hidden, model), BF),
            struct((hidden, model), BF),
            struct((4, model, hidden), BF),
            struct((own, model), BF),
            struct((own, model), F32),
            struct((small_rows, model), F32),
        ],
        [VM] * (len(held_args) + len(sent_args) + len(deliver_args)),
        (*held_args, *sent_args, *deliver_args),
        cost=13,
    )
    out_far_y = swap(out_far_y, "gx", 1)
    in_arrived = swap(in_sent, "gy", 1)
    *mixed_grads, d2, small, project_keep, project_send = call(
        partial(combine_kernel, pieces),
        "combine",
        [struct((own * 3 // 2, LANES), BF)] * 4
        + [
            struct((own, model), BF),
            struct((small_rows, model), F32),
            struct((model, 2 * width), BF),
            struct((model, 2 * width), BF),
        ],
        [VM] * (pieces + 13),
        (
            *rows_back,
            grad_hidden,
            residual,
            gs,
            router_part,
            extras,
            *out_pieces,
            *mixed_pieces,
        ),
        cost=40,
    )
    grads_mixed = [mixed_grads[0]] + [swap(mixed_grads[j], "gy", j) for j in (1, 2, 3)]
    project_other = swap(project_send, "gy", 1)
    in_mine, in_by_x, in_far_y, in_by_y = call(
        partial(outer_held_kernel, pieces, tuple((0, 4 * a + b) for a, b in ours), False),
        "outer_in_held",
        [
            struct((model, hidden), F32),
            struct((model, hidden), BF),
            struct((model, hidden), BF),
            struct((model, hidden), BF),
        ],
        [VM] * (pieces + 2),
        (*rows_in, after(grad_pre, mixed_grads[0]), in_arrived),
        cost=1,
    )
    grads_mixed[1:] = lax.optimization_barrier((*grads_mixed[1:], in_mine))[:-1]
    in_far_y = swap(in_far_y, "gx", 1)
    out_sum_x = add(out_by_x, after(out_far_y, in_mine)).astype(BF)
    projected = add(after(project_keep, in_mine), project_other).astype(BF)
    grads_mixed[0], in_by_x, out_sum_x, projected = lax.optimization_barrier(
        (grads_mixed[0], in_by_x, out_sum_x, projected)
    )
    projected = lax.all_to_all(projected, "gx", split_axis=0, concat_axis=0, tiled=True)
    out_from_x = swap(out_sum_x, "gy", 2)
    out_from_y = swap(out_by_y, "gx", 1)
    d1_x = swap(after(d1, *grads_mixed[1:]), "gy", 2)
    spare = -(-3 * width // LANES) * LANES - 3 * width
    count = 2 if n_gx == len(RING) and heads * bucket_count == shard else 1
    dw_shape = (model, 3 * width + spare) if count == 1 else (4, shard, 3 * width + spare)
    *dw, keep, send, table = call(
        partial(attend_back_kernel, count),
        "attend_back",
        [struct(dw_shape, BF)] * count
        + [
            struct((2, BLOCK, model), BF),
            struct((2, BLOCK, model), BF),
            struct((bucket_count, 8), F32),
        ],
        [SM, SM] + [VM] * 5 + [ANY, VM, ANY, ANY, ANY] + [VM] * 4,
        (
            gy,
            gx,
            *grads_mixed,
            pos_col,
            prob,
            qkv,
            h1,
            layer_input,
            w_full,
            extras,
            brev,
            d2,
            small,
        ),
        scratch=[
            pltpu.VMEM((seq, width), BF),
            pltpu.VMEM((seq, 3 * width), BF),
            pltpu.VMEM((model, 3 * width + spare), BF),
            pltpu.VMEM((heads * pairs, BLOCK, BLOCK), BF),
            pltpu.VMEM((seq, model), BF),
            pltpu.VMEM((seq, model), BF),
            pltpu.VMEM((model, 3 * width), BF),
            pltpu.SemaphoreType.DMA((heads + 3,)),
        ],
        cost=60,
    )
    keep, send, in_far_y, out_from_x, out_from_y, d1_x, projected, *dw = lax.optimization_barrier(
        (keep, send, in_far_y, out_from_x, out_from_y, d1_x, projected, *dw)
    )
    half = add(keep, swap(send, "gy", 1)).astype(BF)
    half, d1, d1_x, in_by_x = lax.optimization_barrier((half, d1, d1_x, in_by_x))
    half_far = swap(half, "gy", 2)
    in_sum_x = add(in_by_x, in_far_y).astype(BF)
    in_from_x = swap(in_sum_x, "gy", 2)
    d1s = [after(d1, in_sum_x), swap(d1, "gy", 1), d1_x, swap(d1_x, "gy", 1)]
    (layer_output,) = call(
        unsort_kernel,
        "unsort",
        [struct((seq, model), F32)],
        [SM] + [VM] * 6,
        (gy, pos_col, layer_input, *d1s),
        cost=1,
    )
    projected = projected.reshape(n_gx, shard, 2 * width).astype(F32).sum(axis=0)
    sums, dw_done = sum_begin(dw, layer_output)
    in_from_y = swap(after(in_by_y, dw_done), "gx", 1)
    half_far, *sums = lax.optimization_barrier((half_far, layer_output, *sums))
    sums = sums[1:]
    total = add(half, half_far[::-1]).astype(BF)
    other = swap(total, "gy", 1)
    (grad_input,) = call(
        finish_kernel,
        "finish",
        [struct((seq, model), F32)],
        [SM] + [VM] * 3,
        (gy, total, other, grad_out),
        cost=1,
    )
    summed = sums[0].astype(F32)
    for part in sums[1:]:
        summed = summed + part.astype(F32)
    small = summed[:, 3 * width :]
    small = small + swap(small, "gy", 1)
    line = swap(jnp.concatenate([small, projected[:, width:]], axis=1), "gy", 2)
    line = after(line, grad_input)
    grad_first, grad_second, grad_route, grad_out_proj = call(
        partial(close_kernel, experts),
        "close",
        [
            struct((1, shard), F32),
            struct((1, shard), F32),
            struct((experts, shard), F32),
            struct((shard, width), F32),
        ],
        [VM] * 3,
        (small, line, projected),
        cost=1,
    )
    grad_w_out = add(add(out_mine, out_from_y), out_from_x)
    in_from_x, in_from_y = lax.optimization_barrier((in_from_x, in_from_y, grad_input))[:2]
    grad_w_in = add(add(in_mine, in_from_y), in_from_x)
    if count == 1:
        grad_table = sum_all(table, "gx")[:, :heads].T
    else:
        grad_table = summed[:, -1].reshape(heads, bucket_count)

    return (
        layer_output,
        grad_input,
        summed[:, :width],
        summed[:, width : 2 * width],
        summed[:, 2 * width : 3 * width],
        grad_out_proj,
        grad_first.reshape(shard),
        grad_second.reshape(shard),
        grad_route.T,
        grad_table,
        grad_w_in[None],
        grad_w_out[None],
    )


def solution(mesh):
    return jax.shard_map(
        on_device,
        mesh=mesh,
        in_specs=(
            P("gx", None),
            P("gx", "gy"),
            P("gx", "gy"),
            P("gx", "gy"),
            P("gx", "gy"),
            P("gx"),
            P("gx"),
            P("gx", None),
            P("gy", None),
            P("gx", None, "gy"),
            P("gx", "gy", None),
            P("gx", None),
            P(),
            P(),
            P("gx", None),
        ),
        out_specs=(
            P("gx", None),
            P("gx", None),
            P("gx", "gy"),
            P("gx", "gy"),
            P("gx", "gy"),
            P("gx", "gy"),
            P("gx"),
            P("gx"),
            P("gx", None),
            P("gy", None),
            P("gx", None, "gy"),
            P("gx", "gy", None),
        ),
        check_vma=False,
    )
```
